32 devices in a mesh: seq: 4 (over y, core), dp: 8 (over z, x).
Axes of the slice: x: 2, y: 2, z: 4, core: 2. Of those that a mesh axis runs over, the one named last changes fastest.
Arguments:
- tokens: bfloat16 [16, 1024, 1024], P('dp', 'seq'), may hold values from -6 to 6
- lengths: int32 [16], P('dp'), may hold values from 256 to 1024, as said below
- cotangent: bfloat16 [16, 1024, 1024], P('dp', 'seq'), may hold values from -6 to 6
- first_gain: bfloat16 [1024], P(('seq', 'dp')), may hold values from 0.5 to 1.5
- first_bias: bfloat16 [1024], P(('seq', 'dp')), may hold values from -1 to 1
- mix_key: bfloat16 [1024], P(('seq', 'dp')), may hold values from 0 to 1
- mix_value: bfloat16 [1024], P(('seq', 'dp')), may hold values from 0 to 1
- mix_recept: bfloat16 [1024], P(('seq', 'dp')), may hold values from 0 to 1
- time_decay: bfloat16 [1024], P(('seq', 'dp')), as said below
- time_first: bfloat16 [1024], P(('seq', 'dp')), may hold values from -1 to 1
- key_weight: bfloat16 [1024, 1024], P(('seq', 'dp')), may hold values from -0.1875 to 0.1875
- value_weight: bfloat16 [1024, 1024], P(('seq', 'dp')), may hold values from -0.1875 to 0.1875
- recept_weight: bfloat16 [1024, 1024], P(('seq', 'dp')), may hold values from -0.1875 to 0.1875
- output_weight: bfloat16 [1024, 1024], P(('seq', 'dp')), may hold values from -0.75 to 0.75
- second_gain: bfloat16 [1024], P(('seq', 'dp')), may hold values from 0.5 to 1.5
- second_bias: bfloat16 [1024], P(('seq', 'dp')), may hold values from -1 to 1
- shift_key: bfloat16 [1024], P(('seq', 'dp')), may hold values from 0 to 1
- shift_recept: bfloat16 [1024], P(('seq', 'dp')), may hold values from 0 to 1
- up_weight: bfloat16 [1024, 4096], P(('seq', 'dp')), may hold values from -0.1875 to 0.1875
- gate_weight: bfloat16 [1024, 1024], P(('seq', 'dp')), may hold values from -0.1875 to 0.1875
- down_weight: bfloat16 [4096, 1024], P(('seq', 'dp')), may hold values from -0.09375 to 0.09375
Outputs:
- output: bfloat16 [16, 1024, 1024], P('dp', 'seq')
- tokens_grad: float32 [16, 1024, 1024], P('dp', 'seq')
- grad_first_gain: float32 [1024], P(('seq', 'dp'))
- grad_first_bias: float32 [1024], P(('seq', 'dp'))
- grad_mix_key: float32 [1024], P(('seq', 'dp'))
- grad_mix_value: float32 [1024], P(('seq', 'dp'))
- grad_mix_recept: float32 [1024], P(('seq', 'dp'))
- grad_time_decay: float32 [1024], P(('seq', 'dp'))
- grad_time_first: float32 [1024], P(('seq', 'dp'))
- grad_key_weight: float32 [1024, 1024], P(('seq', 'dp'))
- grad_value_weight: float32 [1024, 1024], P(('seq', 'dp'))
- grad_recept_weight: float32 [1024, 1024], P(('seq', 'dp'))
- grad_output_weight: float32 [1024, 1024], P(('seq', 'dp'))
- grad_second_gain: float32 [1024], P(('seq', 'dp'))
- grad_second_bias: float32 [1024], P(('seq', 'dp'))
- grad_shift_key: float32 [1024], P(('seq', 'dp'))
- grad_shift_recept: float32 [1024], P(('seq', 'dp'))
- grad_up_weight: float32 [1024, 4096], P(('seq', 'dp'))
- grad_gate_weight: float32 [1024, 1024], P(('seq', 'dp'))
- grad_down_weight: float32 [4096, 1024], P(('seq', 'dp'))
The draws below stay inside these ranges and needn't reach their ends.
Inputs may be any that keep to these rules, and one draw needn't show every extreme that they name: `lengths`: each sequence has between 256 and 1024 live tokens at its start, the rest of its slots are padding; some sequence has each of the two. exp(time_decay) lies between 0.3 / 1024 and 0.08.
All inputs are finite; a program needn't handle non-finite values.
Results may differ from the reference program's by a relative error of at most 0.013.
Values may be sent and summed in bfloat16 or wider, within the bound.
No kernel may reach another device: no remote copies, remote signals or barrier semaphores. Data moves between devices by JAX's collectives and lax.ppermute only.
A program may use at most 256 MiB of HBM per device.

```python
import math
import jax
import jax.numpy as jnp
from jax import lax

D = 1024
FF = 4096
BLK = 64
LENGTH = 1024
SEQS = 16


def draw_lengths(key, part):
    pick_key, order_key = jax.random.split(jax.random.fold_in(key, 11))
    lengths_out = jax.random.randint(pick_key, (SEQS,), LENGTH // 4, LENGTH + 1, dtype=jnp.int32)
    shuffled = jax.random.permutation(order_key, SEQS)
    lengths_out = lengths_out.at[shuffled[0]].set(LENGTH)
    lengths_out = lengths_out.at[shuffled[1]].set(LENGTH // 4)
    return lengths_out.astype(jnp.int32)


def draw_time_decay(key, part):
    pick_key, slow_key, fast_key = jax.random.split(jax.random.fold_in(key, 23), 3)
    slow_share = 0.5
    chooser = jax.random.uniform(pick_key, (D,), dtype=jnp.float32)
    slow_log = jax.random.uniform(slow_key, (D,), dtype=jnp.float32, minval=math.log(0.3 / LENGTH), maxval=math.log(2.3 / LENGTH))
    fast_log = jax.random.uniform(fast_key, (D,), dtype=jnp.float32, minval=math.log(2.3 / LENGTH), maxval=math.log(0.08))
    return jnp.where(chooser < slow_share, slow_log, fast_log).astype(jnp.bfloat16)


def block_scale(stream_key, extent, cuts, smallest, top_value):
    factor_of = 1.0
    for axis_at, parts in cuts:
        heights = jax.random.uniform(jax.random.fold_in(jax.random.fold_in(stream_key, 6), axis_at), (parts,), jnp.float32, smallest / len(cuts), top_value / len(cuts))
        factor_of = factor_of * jnp.repeat(jnp.exp(heights), extent[axis_at] // parts).reshape((-1,) + (1,) * (len(extent) - 1 - axis_at))
    return factor_of


def scatter_about(own_key, dims, scale, most, shards=(), held_as=jnp.bfloat16):
    level = block_scale(own_key, dims, shards, -0.22, 0.18) if shards else 1.0
    result = jax.random.normal(own_key, dims, jnp.float32) * scale * level
    return jnp.minimum(jnp.maximum(result, -most), most).astype(held_as)


def setup_inputs(seed: int = 0) -> dict:
    streams_of = jax.random.split(jax.random.key(seed), 22)
    tokens = scatter_about(streams_of[0], (SEQS, LENGTH, D), 1.0, 6.0, ((0, 8), (1, 4)))
    lengths = draw_lengths(jax.random.fold_in(streams_of[21], 71), 0)
    cotangent = scatter_about(streams_of[2], (SEQS, LENGTH, D), 1.0, 6.0, ((0, 8), (1, 4)))
    first_gain = jnp.clip(1.0 + 0.1 * jax.random.normal(streams_of[3], (D,), jnp.float32), 0.5, 1.5).astype(jnp.bfloat16)
    first_bias = scatter_about(streams_of[4], (D,), 0.2, 1.0, ((0, 32),))
    mix_key = jnp.clip(1.0 * jax.random.uniform(streams_of[5], (D,), jnp.float32) ** block_scale(streams_of[5], (D,), ((0, 32),), -0.2, 0.2), 0.0, 1.0).astype(jnp.bfloat16)
    mix_value = jnp.clip(1.0 * jax.random.uniform(streams_of[6], (D,), jnp.float32) ** block_scale(streams_of[6], (D,), ((0, 32),), -0.2, 0.2), 0.0, 1.0).astype(jnp.bfloat16)
    mix_recept = jnp.clip(1.0 * jax.random.uniform(streams_of[7], (D,), jnp.float32) ** block_scale(streams_of[7], (D,), ((0, 32),), -0.2, 0.2), 0.0, 1.0).astype(jnp.bfloat16)
    time_decay = draw_time_decay(jax.random.fold_in(streams_of[21], 71), 0)
    time_first = jnp.clip(jax.random.uniform(streams_of[9], (D,), jnp.float32, -1.0, 1.0) * block_scale(streams_of[9], (D,), ((0, 32),), -0.4, 0.0), -1.0, 1.0).astype(jnp.bfloat16)
    key_weight = scatter_about(streams_of[10], (D, D), D ** -0.5, 0.1875, ((0, 32),))
    value_weight = scatter_about(streams_of[11], (D, D), D ** -0.5, 0.1875, ((0, 32),))
    recept_weight = scatter_about(streams_of[12], (D, D), D ** -0.5, 0.1875, ((0, 32),))
    output_weight = scatter_about(streams_of[13], (D, D), (D // 16) ** -0.5, 0.75, ((0, 32),))
    second_gain = jnp.clip(1.0 + 0.1 * jax.random.normal(streams_of[14], (D,), jnp.float32), 0.5, 1.5).astype(jnp.bfloat16)
    second_bias = scatter_about(streams_of[15], (D,), 0.2, 1.0, ((0, 32),))
    shift_key = jnp.clip(1.0 * jax.random.uniform(streams_of[16], (D,), jnp.float32) ** block_scale(streams_of[16], (D,), ((0, 32),), -0.2, 0.2), 0.0, 1.0).astype(jnp.bfloat16)
    shift_recept = jnp.clip(1.0 * jax.random.uniform(streams_of[17], (D,), jnp.float32) ** block_scale(streams_of[17], (D,), ((0, 32),), -0.2, 0.2), 0.0, 1.0).astype(jnp.bfloat16)
    up_weight = scatter_about(streams_of[18], (D, FF), D ** -0.5, 0.1875, ((0, 32),))
    gate_weight = scatter_about(streams_of[19], (D, D), D ** -0.5, 0.1875, ((0, 32),))
    down_weight = scatter_about(streams_of[20], (FF, D), FF ** -0.5, 0.09375, ((0, 32),))
    return dict(tokens=tokens, lengths=lengths, cotangent=cotangent, first_gain=first_gain, first_bias=first_bias, mix_key=mix_key, mix_value=mix_value, mix_recept=mix_recept, time_decay=time_decay, time_first=time_first, key_weight=key_weight, value_weight=value_weight, recept_weight=recept_weight, output_weight=output_weight, second_gain=second_gain, second_bias=second_bias, shift_key=shift_key, shift_recept=shift_recept, up_weight=up_weight, gate_weight=gate_weight, down_weight=down_weight)


@jax.custom_vjp
def low(v):
    return lax.optimization_barrier(v.astype(jnp.bfloat16)).astype(jnp.float32)

@jax.custom_vjp
def low_back(v):
    return v

def low_keep(v):
    return (low(v), None)

def low_pass(kept, grad):
    return (grad,)

def back_keep(v):
    return (v, None)

def back_low(kept, grad):
    return (low(grad),)
low.defvjp(low_keep, low_pass)
low_back.defvjp(back_keep, back_low)
EPS = 1e-05

def norm_rows(field, gain_vec, bias_vec):
    center = field - lax.optimization_barrier(jnp.mean(field, axis=-1, keepdims=True))
    spread = lax.optimization_barrier(jnp.mean(center * center, axis=-1, keepdims=True))
    return center * lax.rsqrt(spread + EPS) * gain_vec + bias_vec

def shifted(field):
    return jnp.concatenate([jnp.zeros_like(field[:, :1]), field[:, :-1]], axis=1)

def project(left, right):
    return jnp.einsum('nlc,cd->nld', left, right, precision=lax.Precision.HIGHEST)

def compute_attention_recurrence(lookup_matrix_output, content_matrix_output, fading_rate_vector, boost_log_scale, starting_accumulator, starting_normalizer):
    seq_count, span_len, channels = lookup_matrix_output.shape
    blocks = span_len // BLK
    offset = jnp.arange(BLK, dtype=jnp.float32)[:, None]
    strict_lower = (jnp.arange(BLK)[:, None] > jnp.arange(BLK)[None, :]).astype(jnp.float32)
    rising = jnp.exp(offset * fading_rate_vector)
    falling = jnp.exp(-offset * fading_rate_vector)
    carry_fall = jnp.exp((1.0 - offset) * fading_rate_vector)
    end_fall = jnp.exp(-BLK * fading_rate_vector)
    end_carry = jnp.exp((1.0 - BLK) * fading_rate_vector)

    def one_block(state, inputs):
        state_a, state_b = state
        lookup_piece_entries, content_piece_entries = inputs
        weight = jnp.exp(lookup_piece_entries) * rising
        weighted = weight * content_piece_entries
        sum_a = jnp.einsum('ts,nsc->ntc', strict_lower, weighted, precision=lax.Precision.HIGHEST)
        sum_b = jnp.einsum('ts,nsc->ntc', strict_lower, weight, precision=lax.Precision.HIGHEST)
        earlier_accumulator = falling * state_a[:, None, :] + carry_fall * sum_a
        earlier_normalizer = falling * state_b[:, None, :] + carry_fall * sum_b
        current_token_boost = jnp.exp(boost_log_scale + lookup_piece_entries)
        module_output_tensor = (earlier_accumulator + current_token_boost * content_piece_entries) / (earlier_normalizer + current_token_boost)
        next_a = end_fall * state_a + end_carry * lax.optimization_barrier(jnp.sum(weighted, axis=1))
        next_b = end_fall * state_b + end_carry * lax.optimization_barrier(jnp.sum(weight, axis=1))
        return ((next_a, next_b), module_output_tensor)
    key_seq = jnp.moveaxis(lookup_matrix_output.reshape(seq_count, blocks, BLK, channels), 1, 0)
    value_seq = jnp.moveaxis(content_matrix_output.reshape(seq_count, blocks, BLK, channels), 1, 0)
    final_state, results = lax.scan(jax.checkpoint(one_block), (starting_accumulator, starting_normalizer), (key_seq, value_seq))
    return jnp.moveaxis(results, 0, 1).reshape(seq_count, span_len, channels)

def block_forward(tokens, live_mask, params):
    first_gain, first_bias, mix_key, mix_value, mix_recept, time_decay, time_first, key_weight, value_weight, recept_weight, output_weight, second_gain, second_bias, shift_key, shift_recept, up_weight, gate_weight, down_weight = params
    normed = norm_rows(tokens, first_gain, first_bias)
    before = shifted(normed)
    key_in = low(normed * mix_key + before * (1.0 - mix_key))
    value_in = low(normed * mix_value + before * (1.0 - mix_value))
    recept_in = low(normed * mix_recept + before * (1.0 - mix_recept))
    lookup_matrix_output = low_back(project(key_in, key_weight))
    content_matrix_output = low_back(project(value_in, value_weight))
    recept_proj = low_back(project(recept_in, recept_weight))
    fading_rate_vector = jnp.exp(time_decay)
    zero_state = jnp.zeros((tokens.shape[0], tokens.shape[2]), jnp.float32)
    blended = compute_attention_recurrence(lookup_matrix_output, content_matrix_output, fading_rate_vector, time_first, zero_state, zero_state)
    mixed_out = low(jax.nn.sigmoid(recept_proj) * blended)
    branch = low_back(project(mixed_out, output_weight))
    residual = tokens + branch
    normed_two = norm_rows(residual, second_gain, second_bias)
    before_two = shifted(normed_two)
    ffn_key = low(normed_two * shift_key + before_two * (1.0 - shift_key))
    ffn_recept = low(normed_two * shift_recept + before_two * (1.0 - shift_recept))
    up_proj = low_back(project(ffn_key, up_weight))
    squared = low(jnp.square(jax.nn.relu(up_proj)))
    down_proj = low_back(project(squared, down_weight))
    gate_value = jax.nn.sigmoid(low_back(project(ffn_recept, gate_weight)))
    return (residual + gate_value * down_proj) * live_mask[:, :, None]

def reference(tokens, lengths, cotangent, first_gain, first_bias, mix_key, mix_value, mix_recept, time_decay, time_first, key_weight, value_weight, recept_weight, output_weight, second_gain, second_bias, shift_key, shift_recept, up_weight, gate_weight, down_weight):
    params = jax.tree.map(lambda value: value.astype(jnp.float32), (first_gain, first_bias, mix_key, mix_value, mix_recept, time_decay, time_first, key_weight, value_weight, recept_weight, output_weight, second_gain, second_bias, shift_key, shift_recept, up_weight, gate_weight, down_weight))
    per_group = math.gcd(SEQS, max(1, 4096 // LENGTH))
    groups = SEQS // per_group
    tok_groups = tokens.reshape(groups, per_group, LENGTH, D)
    cot_groups = cotangent.reshape(groups, per_group, LENGTH, D)
    len_groups = lengths.reshape(groups, per_group)

    def group_step(totals, batch_in):
        tok_block, cot_block, len_block = batch_in
        live_mask = (jnp.arange(LENGTH, dtype=jnp.int32)[None, :] < len_block[:, None]).astype(jnp.float32)
        forward_out, pullback = jax.vjp(lambda field, weights: block_forward(field, live_mask, weights), tok_block.astype(jnp.float32), params)
        field_grad, weight_grads = pullback(cot_block.astype(jnp.float32))
        totals = jax.tree.map(jnp.add, totals, weight_grads)
        return (totals, (forward_out.astype(jnp.bfloat16), field_grad))
    zero_grads = jax.tree.map(jnp.zeros_like, params)
    totals, (outputs, field_grads) = lax.scan(group_step, zero_grads, (tok_groups, cot_groups, len_groups))
    g_first_gain, g_first_bias, g_mix_key, g_mix_value, g_mix_recept, g_time_decay, g_time_first, g_key_weight, g_value_weight, g_recept_weight, g_output_weight, g_second_gain, g_second_bias, g_shift_key, g_shift_recept, g_up_weight, g_gate_weight, g_down_weight = totals
    return (outputs.reshape(SEQS, LENGTH, D), field_grads.reshape(SEQS, LENGTH, D), g_first_gain, g_first_bias, g_mix_key, g_mix_value, g_mix_recept, g_time_decay, g_time_first, g_key_weight, g_value_weight, g_recept_weight, g_output_weight, g_second_gain, g_second_bias, g_shift_key, g_shift_recept, g_up_weight, g_gate_weight, g_down_weight)
```

```python
import jax
import jax.numpy as jnp
from jax import lax
from jax.sharding import PartitionSpec as P

BLK = 64


EPS = 1e-05

def norm_stats(field):
    center = field - jnp.mean(field, axis=-1, keepdims=True)
    inverse = lax.rsqrt(jnp.mean(center * center, axis=-1, keepdims=True) + EPS)
    return (center * inverse, inverse)


def norm_back(grad_normed, normalized, inverse):
    mean_grad = jnp.mean(grad_normed, axis=-1, keepdims=True)
    mean_proj = jnp.mean(grad_normed * normalized, axis=-1, keepdims=True)
    return inverse * (grad_normed - mean_grad - normalized * mean_proj)


def summary(lookup_matrix_output, content_matrix_output, fading_rate_vector):
    span_len = lookup_matrix_output.shape[1]
    distance = (span_len - 1 - jnp.arange(span_len, dtype=jnp.float32))[:, None]
    weight = jnp.exp(lookup_matrix_output - distance * fading_rate_vector)
    return (jnp.sum(weight * content_matrix_output, axis=1), jnp.sum(weight, axis=1))


def combine_state(earlier, later):
    return (
        earlier[0] * later[0],
        later[0] * earlier[1] + later[1],
        later[0] * earlier[2] + later[2],
    )


def compute_attention_recurrence(
    lookup_matrix_output,
    content_matrix_output,
    fading_rate_vector,
    boost_log_scale,
    starting_accumulator,
    starting_normalizer,
):
    seq_count, span_len, channels = lookup_matrix_output.shape
    blocks = span_len // BLK
    offset = jnp.arange(BLK, dtype=jnp.float32)[:, None]
    strict_lower = (jnp.arange(BLK)[:, None] > jnp.arange(BLK)[None, :]).astype(jnp.float32)
    rising = jnp.exp(offset * fading_rate_vector)
    falling = jnp.exp(-offset * fading_rate_vector)
    carry_fall = jnp.exp((1.0 - offset) * fading_rate_vector)
    end_fall = jnp.exp(-BLK * fading_rate_vector)
    end_carry = jnp.exp((1.0 - BLK) * fading_rate_vector)

    def one_block(state, inputs):
        state_a, state_b = state
        lookup_piece_entries, content_piece_entries = inputs
        weight = jnp.exp(lookup_piece_entries) * rising
        weighted = weight * content_piece_entries
        sum_a = jnp.einsum("ts,nsc->ntc", strict_lower, weighted, precision=lax.Precision.HIGHEST)
        sum_b = jnp.einsum("ts,nsc->ntc", strict_lower, weight, precision=lax.Precision.HIGHEST)
        earlier_accumulator = falling * state_a[:, None, :] + carry_fall * sum_a
        earlier_normalizer = falling * state_b[:, None, :] + carry_fall * sum_b
        current_token_boost = jnp.exp(boost_log_scale + lookup_piece_entries)
        module_output_tensor = (
            earlier_accumulator + current_token_boost * content_piece_entries
        ) / (earlier_normalizer + current_token_boost)
        next_a = end_fall * state_a + end_carry * jnp.sum(weighted, axis=1)
        next_b = end_fall * state_b + end_carry * jnp.sum(weight, axis=1)
        return ((next_a, next_b), module_output_tensor)

    key_seq = jnp.moveaxis(lookup_matrix_output.reshape(seq_count, blocks, BLK, channels), 1, 0)
    value_seq = jnp.moveaxis(content_matrix_output.reshape(seq_count, blocks, BLK, channels), 1, 0)
    final_state, results = lax.scan(
        jax.checkpoint(one_block), (starting_accumulator, starting_normalizer), (key_seq, value_seq)
    )
    return jnp.moveaxis(results, 0, 1).reshape(seq_count, span_len, channels)


SEQ = ("y", "core")
DP = ("z", "x")
ALL = ("y", "core", "z", "x")


def matmul(form, left, right):
    return jnp.einsum(form, left, right, preferred_element_type=jnp.float32)


def shifted(block, axis, distance):
    count = lax.axis_size(axis)
    route = [(i - distance, i) for i in range(count) if 0 <= i - distance < count]
    return lax.ppermute(block, axis, route)


def previous_rows(field):
    came = shifted(field[:, -1, :], SEQ, 1)
    return jnp.concatenate([came[:, None, :], field[:, :-1, :]], axis=1)


def next_rows(field):
    came = shifted(field[:, 0, :], SEQ, -1)
    return jnp.concatenate([field[:, 1:, :], came[:, None, :]], axis=1)


def prefix(x, reverse):
    count, mine = (lax.axis_size(SEQ), lax.axis_index(SEQ))
    factor, a, b = x
    every = lax.all_gather(jnp.stack([a, b]), SEQ)
    total = jnp.zeros_like(every[0])
    for k in range(count):
        at = count - 1 - k if reverse else k
        reached = at > mine if reverse else at < mine
        total = jnp.where(reached, factor * total + every[at], total)
    return (total[0], total[1])


def rs_axis(parts, dim, axis, kind):
    count, mine = (lax.axis_size(axis), lax.axis_index(axis))

    def take(j):
        taken = [lax.dynamic_index_in_dim(p, j, dim, keepdims=False) for p in parts]
        return taken[0] if len(taken) == 1 else jnp.concatenate(taken, axis=-2)

    came = []
    for k in range(1, count):
        route = [(i, (i + k) % count) for i in range(count)]
        block = take(lax.rem(mine + k, count)).astype(jnp.bfloat16)
        came.append(lax.ppermute(block, axis, route))
    total = take(mine).astype(jnp.float32)
    for block in came:
        total = total + block.astype(jnp.float32)
    return total.astype(kind)


def reduce_scatter(parts):
    low = jnp.bfloat16
    g = rs_axis(parts, 1, "core", low)
    half = g.shape[-1] // 2
    a, b = (g[..., :half], g[..., half:])
    a = rs_axis([a], 2, "x", low)
    b = rs_axis([b], 0, "y", low)
    a = rs_axis([a], 0, "y", low)
    b = rs_axis([b], 1, "x", low)
    return rs_axis([jnp.concatenate([a, b], axis=-1)], 0, "z", jnp.float32)


def per_device(
    tokens,
    lengths,
    cotangent,
    first_gain,
    first_bias,
    mix_key,
    mix_value,
    mix_recept,
    time_decay,
    time_first,
    key_weight,
    value_weight,
    recept_weight,
    output_weight,
    second_gain,
    second_bias,
    shift_key,
    shift_recept,
    up_weight,
    gate_weight,
    down_weight,
):
    grid = tuple(lax.axis_size(axis) for axis in ALL)
    count = grid[0] * grid[1] * grid[2] * grid[3]
    seq_count, piece_len, channels = tokens.shape
    hidden = up_weight.shape[1]
    mine = channels // count
    blocks = hidden // channels

    vectors = (
        first_gain,
        first_bias,
        mix_key,
        mix_value,
        mix_recept,
        time_decay,
        time_first,
        second_gain,
        second_bias,
        shift_key,
        shift_recept,
    )
    n_vec = len(vectors)
    flat = jnp.concatenate(vectors)
    packed = jnp.pad(flat, (0, 8 * channels - n_vec * mine)).reshape(8, channels)
    early = lax.all_gather(
        jnp.concatenate([key_weight, value_weight, recept_weight, packed]), ALL, axis=0
    )
    late = lax.all_gather(
        jnp.concatenate(
            [output_weight]
            + [up_weight[:, j * channels : (j + 1) * channels] for j in range(blocks)]
            + [gate_weight, down_weight]
        ),
        ALL,
        axis=0,
    )

    def square(gathered, at, rows=mine):
        return gathered[:, at : at + rows].reshape(count * rows, channels)

    key_mat, value_mat, recept_mat = (square(early, j * mine) for j in range(3))
    vecs = early[:, 3 * mine].reshape(count, -1)[:, : n_vec * mine].reshape(count, n_vec, mine)
    vecs = jnp.moveaxis(vecs, 1, 0).reshape(n_vec, channels).astype(jnp.float32)
    (
        norm_gain,
        norm_bias,
        key_mix,
        value_mix,
        recept_mix,
        decay_log,
        boost_log_scale,
        gain_two,
        bias_two,
        chan_key_mix,
        chan_recept_mix,
    ) = (vecs[j] for j in range(n_vec))
    output_mat = square(late, 0)
    up_mat = jnp.concatenate([square(late, (1 + j) * mine) for j in range(blocks)], axis=1)
    gate_mat = square(late, (1 + blocks) * mine)
    down_mat = square(late, (2 + blocks) * mine, hidden // count)

    seq_index = lax.axis_index(SEQ)
    positions = seq_index * piece_len + jnp.arange(piece_len, dtype=jnp.int32)
    live_mask = (positions[None, :] < lengths[:, None]).astype(jnp.float32)[:, :, None]
    field = tokens.astype(jnp.float32)
    normed_one, inverse_one = norm_stats(field)
    normed = normed_one * norm_gain + norm_bias
    before = previous_rows(normed)
    key_in = (normed * key_mix + before * (1.0 - key_mix)).astype(jnp.bfloat16)
    value_in = (normed * value_mix + before * (1.0 - value_mix)).astype(jnp.bfloat16)
    recept_in = (normed * recept_mix + before * (1.0 - recept_mix)).astype(jnp.bfloat16)
    lookup_matrix_output = matmul("nlc,cd->nld", key_in, key_mat)
    content_matrix_output = matmul("nlc,cd->nld", value_in, value_mat)
    recept_proj = matmul("nlc,cd->nld", recept_in, recept_mat)
    fading_rate_vector = jnp.exp(decay_log)
    (local_a, local_b), summary_pull = jax.vjp(
        summary, lookup_matrix_output, content_matrix_output, fading_rate_vector
    )
    piece_fall = jnp.exp(-piece_len * fading_rate_vector)
    starting_accumulator, starting_normalizer = prefix((piece_fall, local_a, local_b), False)
    blended, weighted_kv_pullback = jax.vjp(
        compute_attention_recurrence,
        lookup_matrix_output,
        content_matrix_output,
        fading_rate_vector,
        boost_log_scale,
        starting_accumulator,
        starting_normalizer,
    )
    recept_sig = jax.nn.sigmoid(recept_proj)
    mixed_out = (recept_sig * blended).astype(jnp.bfloat16)
    branch = matmul("nlc,cd->nld", mixed_out, output_mat)
    residual = field + branch
    normed_two_raw, inverse_two = norm_stats(residual)
    normed_two = normed_two_raw * gain_two + bias_two
    before_two = previous_rows(normed_two)
    ffn_key = (normed_two * chan_key_mix + before_two * (1.0 - chan_key_mix)).astype(jnp.bfloat16)
    ffn_recept = (normed_two * chan_recept_mix + before_two * (1.0 - chan_recept_mix)).astype(
        jnp.bfloat16
    )
    up_proj = matmul("nlc,cf->nlf", ffn_key, up_mat)
    squared = jnp.square(jax.nn.relu(up_proj)).astype(jnp.bfloat16)
    down_proj = matmul("nlf,fd->nld", squared, down_mat)
    gate_value = jax.nn.sigmoid(matmul("nlc,cd->nld", ffn_recept, gate_mat))
    output = ((residual + gate_value * down_proj) * live_mask).astype(jnp.bfloat16)

    def outer(left, right):
        whole = jnp.einsum("nlc,nld->cd", left, right, preferred_element_type=jnp.float32)
        return whole.astype(jnp.bfloat16).reshape(*grid, -1, right.shape[-1])

    def by_columns(g):
        return [g[..., j * channels : (j + 1) * channels] for j in range(g.shape[-1] // channels)]

    seed = cotangent.astype(jnp.float32) * live_mask
    down_grad = (seed * gate_value).astype(jnp.bfloat16)
    gate_grad = (seed * down_proj * gate_value * (1.0 - gate_value)).astype(jnp.bfloat16)
    first = reduce_scatter([outer(squared, down_grad), outer(ffn_recept, gate_grad)])
    squared_grad = matmul("nld,fd->nlf", down_grad, down_mat)
    up_grad = (squared_grad * 2.0 * jax.nn.relu(up_proj)).astype(jnp.bfloat16)
    grad_up_part = by_columns(outer(ffn_key, up_grad))
    ffn_key_grad = matmul("nlf,cf->nlc", up_grad, up_mat)
    ffn_recept_grad = matmul("nld,cd->nlc", gate_grad, gate_mat)
    normed_two_grad = (
        ffn_key_grad * chan_key_mix
        + ffn_recept_grad * chan_recept_mix
        + next_rows(ffn_key_grad * (1.0 - chan_key_mix) + ffn_recept_grad * (1.0 - chan_recept_mix))
    )
    gap_two = normed_two - before_two
    grad_chan_key = jnp.sum(ffn_key_grad * gap_two, axis=(0, 1))
    grad_chan_recept = jnp.sum(ffn_recept_grad * gap_two, axis=(0, 1))
    grad_gain_two = jnp.sum(normed_two_grad * normed_two_raw, axis=(0, 1))
    grad_bias_two = jnp.sum(normed_two_grad, axis=(0, 1))
    residual_grad = seed + norm_back(normed_two_grad * gain_two, normed_two_raw, inverse_two)
    branch_grad = residual_grad.astype(jnp.bfloat16)
    second = reduce_scatter(grad_up_part + [outer(mixed_out, branch_grad)])
    mixed_grad = matmul("nld,cd->nlc", branch_grad, output_mat)
    recept_grad = (mixed_grad * blended * recept_sig * (1.0 - recept_sig)).astype(jnp.bfloat16)
    blended_grad = mixed_grad * recept_sig
    (
        key_gradient_first,
        value_gradient_first,
        decay_gradient_first,
        boost_adjoint_term,
        initial_numerator_gradient,
        initial_denominator_gradient,
    ) = weighted_kv_pullback(blended_grad)
    carry_a, carry_b = prefix(
        (piece_fall, initial_numerator_gradient, initial_denominator_gradient), True
    )
    key_grad_b, value_grad_b, rate_grad_b = summary_pull((carry_a, carry_b))
    factor_grad = jnp.sum(carry_a * starting_accumulator + carry_b * starting_normalizer, axis=0)
    rate_grad = decay_gradient_first + rate_grad_b - piece_len * piece_fall * factor_grad
    grad_decay = rate_grad * fading_rate_vector
    key_grad = (key_gradient_first + key_grad_b).astype(jnp.bfloat16)
    value_grad = (value_gradient_first + value_grad_b).astype(jnp.bfloat16)
    key_in_grad = matmul("nld,cd->nlc", key_grad, key_mat)
    value_in_grad = matmul("nld,cd->nlc", value_grad, value_mat)
    recept_in_grad = matmul("nld,cd->nlc", recept_grad, recept_mat)
    normed_grad = (
        key_in_grad * key_mix
        + value_in_grad * value_mix
        + recept_in_grad * recept_mix
        + next_rows(
            key_in_grad * (1.0 - key_mix)
            + value_in_grad * (1.0 - value_mix)
            + recept_in_grad * (1.0 - recept_mix)
        )
    )
    gap_one = normed - before
    grad_key_mix = jnp.sum(key_in_grad * gap_one, axis=(0, 1))
    grad_value_mix = jnp.sum(value_in_grad * gap_one, axis=(0, 1))
    grad_recept_mix = jnp.sum(recept_in_grad * gap_one, axis=(0, 1))
    grad_gain_one = jnp.sum(normed_grad * normed_one, axis=(0, 1))
    grad_bias_one = jnp.sum(normed_grad, axis=(0, 1))
    tokens_grad = residual_grad + norm_back(normed_grad * norm_gain, normed_one, inverse_one)
    sums = jnp.stack(
        [
            grad_gain_one,
            grad_bias_one,
            grad_key_mix,
            grad_value_mix,
            grad_recept_mix,
            grad_decay,
            boost_adjoint_term,
            grad_gain_two,
            grad_bias_two,
            grad_chan_key,
            grad_chan_recept,
        ]
    )
    sums = jnp.moveaxis(sums.reshape(n_vec, *grid, mine), 0, -2).reshape(*grid, n_vec * mine)
    padding = [(0, 0)] * 4 + [(0, 8 * channels - n_vec * mine)]
    sums = jnp.pad(sums, padding).reshape(*grid, 8, channels).astype(jnp.bfloat16)
    third = reduce_scatter(
        [outer(key_in, key_grad), outer(value_in, value_grad), outer(recept_in, recept_grad), sums]
    )
    vec_out = third[3 * mine :].reshape(-1)[: n_vec * mine].reshape(n_vec, mine)
    rows_down = hidden // count
    return (
        output,
        tokens_grad,
        *(vec_out[j] for j in range(7)),
        *(third[j * mine : (j + 1) * mine] for j in range(3)),
        second[blocks * mine :],
        *(vec_out[j] for j in range(7, n_vec)),
        jnp.concatenate([second[j * mine : (j + 1) * mine] for j in range(blocks)], axis=1),
        first[rows_down:],
        first[:rows_down],
    )


def solution(mesh):
    seq, dp = (mesh.shape["seq"], mesh.shape["dp"])
    wide = len({device.coords[0] for device in mesh.devices.reshape(-1)})
    fine = jax.sharding.Mesh(mesh.devices.reshape(seq // 2, 2, dp // wide, wide), ALL)
    field, vector, matrix = (P(DP, SEQ, None), P(ALL), P(ALL, None))
    return jax.shard_map(
        per_device,
        mesh=fine,
        in_specs=(field, P(DP), field) + (vector,) * 7 + (matrix,) * 4 + (vector,) * 4 + (matrix,) * 3,
        out_specs=(field, field) + (vector,) * 7 + (matrix,) * 4 + (vector,) * 4 + (matrix,) * 3,
        check_vma=False,
    )
```

```python
import functools

import jax
import jax.numpy as jnp
from jax import lax
from jax.experimental import pallas as pl
from jax.experimental.pallas import tpu as pltpu
from jax.sharding import PartitionSpec as P

EPS = 1e-05

def norm_stats(field):
    center = field - jnp.mean(field, axis=-1, keepdims=True)
    inverse = lax.rsqrt(jnp.mean(center * center, axis=-1, keepdims=True) + EPS)
    return (center * inverse, inverse)


def norm_back(grad_normed, normalized, inverse):
    mean_grad = jnp.mean(grad_normed, axis=-1, keepdims=True)
    mean_proj = jnp.mean(grad_normed * normalized, axis=-1, keepdims=True)
    return inverse * (grad_normed - mean_grad - normalized * mean_proj)


SEQ = ("y", "core")
DP = ("z", "x")
ALL = ("y", "core", "z", "x")


def scan_tiles(rate, reverse):
    row = lax.broadcasted_iota(jnp.int32, (8, rate.shape[-1]), 0)
    steps = []
    for distance in (1, 2, 4):
        inside = row < 8 - distance if reverse else row >= distance
        steps.append((distance, jnp.where(inside, jnp.exp(-float(distance) * rate), 0.0)))
    return row, steps


def turn(x, distance, reverse):
    return pltpu.roll(x, 8 - distance if reverse else distance, 0)


def scan_rows(x, steps, reverse):
    for distance, factor in steps:
        x = x + factor * turn(x, distance, reverse)
    return x


def wkv_kernel(k_ref, v_ref, r_ref, a0_ref, b0_ref, u_ref, rate_ref, a_ref, b_ref, mixed_ref):
    seqs, span, lanes = k_ref.shape
    rate = rate_ref[...]
    boost = jnp.exp(u_ref[...])
    row, steps = scan_tiles(rate, False)
    falling = jnp.exp(-row.astype(jnp.float32) * rate)
    fall_all = jnp.exp(-8.0 * rate)
    first = row < 1
    pair = 16

    def body(i, carry):
        at = pl.ds(pl.multiple_of(i * pair, pair), pair)
        new = []
        for n in range(seqs):
            k16, v16, r16 = (ref[n, at, :] for ref in (k_ref, v_ref, r_ref))
            state = carry[2 * n : 2 * n + 2]
            tiles = []
            for g in range(2):
                k, v, r = (t[g * 8 : g * 8 + 8] for t in (k16, v16, r16))
                weight = jnp.exp(k)
                bonus = boost * weight
                sums = [scan_rows(t, steps, False) for t in (weight * v, weight)]
                a, b = (
                    falling * c + jnp.where(first, 0.0, turn(t, 1, False))
                    for c, t in zip(state, sums)
                )
                state = tuple(fall_all * c + t[7:8] for c, t in zip(state, sums))
                mixed = jax.nn.sigmoid(r) * ((a + bonus * v) / (b + bonus))
                tiles.append((a, b, mixed))
            a, b, mixed = (jnp.concatenate(t, axis=0) for t in zip(*tiles))
            a_ref[n, at, :] = a
            b_ref[n, at, :] = b
            mixed_ref[n, at, :] = mixed.astype(mixed_ref.dtype)
            new += state
        return tuple(new)

    start = []
    for n in range(seqs):
        start += [a0_ref[n : n + 1, :], b0_ref[n : n + 1, :]]
    lax.fori_loop(0, span // pair, body, tuple(start), unroll=2)


def wkv_back_kernel(
    k_ref, v_ref, r_ref, a_ref, b_ref, g_ref, p0_ref, q0_ref, u_ref, rate_ref,
    k_out, v_out, rate_out, first_out,
):
    seqs, span, lanes = k_ref.shape
    rate = rate_ref[...]
    boost = jnp.exp(u_ref[...])
    row, steps = scan_tiles(rate, True)
    falling = jnp.exp((row.astype(jnp.float32) - 7.0) * rate)
    fall_all = jnp.exp(-8.0 * rate)
    last = row > 6
    pair = 16
    count = span // pair

    def body(i, carry):
        at = pl.ds(pl.multiple_of((count - 1 - i) * pair, pair), pair)
        new = []
        rate_sum, first_sum = carry[-2:]
        for n in range(seqs):
            loaded = [ref[n, at, :] for ref in (k_ref, v_ref, r_ref, a_ref, b_ref, g_ref)]
            state = carry[2 * n : 2 * n + 2]
            tiles = []
            for g in (1, 0):
                k, v, r, a, b, grad = (t[g * 8 : g * 8 + 8] for t in loaded)
                weight = jnp.exp(k)
                bonus = boost * weight
                over = 1.0 / (b + bonus)
                wkv = (a + bonus * v) * over
                alpha = grad * jax.nn.sigmoid(r) * over
                sums = [scan_rows(t, steps, True) for t in (alpha, -alpha * wkv)]
                p, q = (
                    falling * c + jnp.where(last, 0.0, turn(t, 1, True))
                    for c, t in zip(state, sums)
                )
                state = tuple(fall_all * c + t[0:1] for c, t in zip(state, sums))
                share = alpha * bonus
                own = share * (v - wkv)
                tiles.append((own + weight * (p * v + q), share + weight * p))
                rate_sum = rate_sum + (a * p + b * q)
                first_sum = first_sum + own
            k_grad, v_grad = (jnp.concatenate(t, axis=0) for t in zip(*tiles[::-1]))
            k_out[n, at, :] = k_grad.astype(k_out.dtype)
            v_out[n, at, :] = v_grad.astype(v_out.dtype)
            new += state
        return tuple(new) + (rate_sum, first_sum)

    start = []
    for n in range(seqs):
        start += [p0_ref[n : n + 1, :], q0_ref[n : n + 1, :]]
    zero = jnp.zeros((8, lanes), jnp.float32)
    done = lax.fori_loop(0, count, body, tuple(start) + (zero, zero), unroll=2)
    rate_out[...] = -rate * jnp.exp(-rate) * jnp.sum(done[-2], axis=0, keepdims=True)
    first_out[...] = jnp.sum(done[-1], axis=0, keepdims=True)


LANES = 256


def wkv_specs(seqs, span):
    field = pl.BlockSpec((seqs, span, LANES), lambda j: (0, 0, j))
    state = pl.BlockSpec((seqs, LANES), lambda j: (0, j))
    vector = pl.BlockSpec((1, LANES), lambda j: (0, j))
    return field, state, vector


def wkv_forward(k, v, r, a0, b0, u, rate):
    seqs, span, channels = k.shape
    field, state, vector = wkv_specs(seqs, span)
    return pl.pallas_call(
        wkv_kernel,
        grid=(channels // LANES,),
        out_shape=[jax.ShapeDtypeStruct(k.shape, t) for t in (jnp.float32, jnp.float32, jnp.bfloat16)],
        in_specs=[field] * 3 + [state] * 2 + [vector] * 2,
        out_specs=[field] * 3,
        compiler_params=pltpu.CompilerParams(vmem_limit_bytes=32 << 20),
        cost_estimate=pl.CostEstimate(flops=30 * k.size, bytes_accessed=22 * k.size, transcendentals=3 * k.size),
    )(k, v, r, a0, b0, u[None], rate[None])


def wkv_backward(k, v, r, a, b, grad, p0, q0, u, rate):
    seqs, span, channels = k.shape
    field, state, vector = wkv_specs(seqs, span)
    k_grad, v_grad, decay_grad, first_grad = pl.pallas_call(
        wkv_back_kernel,
        grid=(channels // LANES,),
        out_shape=[jax.ShapeDtypeStruct(k.shape, jnp.bfloat16)] * 2
        + [jax.ShapeDtypeStruct((1, channels), jnp.float32)] * 2,
        in_specs=[field] * 6 + [state] * 2 + [vector] * 2,
        out_specs=[field] * 2 + [vector] * 2,
        compiler_params=pltpu.CompilerParams(vmem_limit_bytes=32 << 20),
        cost_estimate=pl.CostEstimate(flops=50 * k.size, bytes_accessed=28 * k.size, transcendentals=3 * k.size),
    )(k, v, r, a, b, grad, p0, q0, u[None], rate[None])
    return k_grad, v_grad, decay_grad[0], first_grad[0]


def matmul(form, left, right):
    return jnp.einsum(form, left, right, preferred_element_type=jnp.float32)


def shifted(block, axis, distance):
    count = lax.axis_size(axis)
    route = [(i - distance, i) for i in range(count) if 0 <= i - distance < count]
    return lax.ppermute(block, axis, route)


def previous_rows(field):
    came = shifted(field[:, -1, :], SEQ, 1)
    return jnp.concatenate([came[:, None, :], field[:, :-1, :]], axis=1)


def next_rows(field):
    came = shifted(field[:, 0, :], SEQ, -1)
    return jnp.concatenate([field[:, 1:, :], came[:, None, :]], axis=1)


def entering(factor, states, reverse):
    block = jnp.stack(states)
    total, power = (jnp.zeros_like(block), jnp.ones_like(factor))
    for k in range(1, lax.axis_size(SEQ)):
        total = total + power * shifted(block, SEQ, -k if reverse else k)
        power = power * factor
    return (total[0], total[1])


def after(x, deps):
    return lax.optimization_barrier((x, tuple(deps)))[0] if deps else x


def spread(block, axis):
    count = lax.axis_size(axis)
    return [
        lax.ppermute(block, axis, [(i, (i + k) % count) for i in range(count)])
        for k in range(1, count)
    ]


def beside_z(own):
    half = own.shape[1] // 2
    rows = lax.all_gather(own, "z", axis=0)
    return (rows[:, :, :half], rows[:, :, half:])


def beside_xy(pair, axes):
    return [[block] + spread(block, axis) for block, axis in zip(pair, axes)]


def other_core(parts):
    return [[spread(block, "core")[0] for block in part] for part in parts]


def assemble_kernel(entries, grid, at_ref, *refs):
    n_out = 1 + max(entry[2] for entry in entries)
    sources, outs, sems = (refs[: -n_out - 1], refs[-n_out - 1 : -1], refs[-1])
    ys, cs, zs, xs = grid
    y, c, x = (at_ref[j] for j in range(3))

    def back(at, k, count):
        return lax.rem(at - k + count, count)

    index = 0
    for dc in range(cs):
        for half, lead in enumerate((xs, ys)):
            for far in range(ys if half == 0 else xs):
                source = sources[index]
                index += 1

                def copy(k, _, source=source, dc=dc, half=half, far=far):
                    near, dz = (k // zs, lax.rem(k, zs))
                    dy, dx = (far, near) if half == 0 else (near, far)
                    block = back(y, dy, ys) * cs + back(c, dc, cs)
                    block = (block * zs + dz) * xs + back(x, dx, xs)
                    for first, rows, out, column in entries:
                        width = source.shape[-1]
                        pltpu.make_async_copy(
                            source.at[near, dz, pl.ds(first, rows), :],
                            outs[out].at[block, :, pl.ds(column + half * width, width)],
                            sems.at[out],
                        ).start()
                    return 0

                lax.fori_loop(0, lead * zs, copy, 0)
    for out in range(n_out):
        pltpu.make_async_copy(outs[out], outs[out], sems.at[out]).wait()


def assemble(mine, other, entries, shapes, grid):
    sources = [b for part in mine for b in part] + [b for part in other for b in part]
    at = jnp.stack([lax.axis_index(axis) for axis in ("y", "core", "x")]).astype(jnp.int32)
    count = grid[0] * grid[1] * grid[2] * grid[3]
    outs = pl.pallas_call(
        functools.partial(assemble_kernel, entries, grid),
        out_shape=[jax.ShapeDtypeStruct((count, *shape), jnp.bfloat16) for shape in shapes],
        in_specs=[pl.BlockSpec(memory_space=pltpu.SMEM)]
        + [pl.BlockSpec(memory_space=pl.ANY)] * len(sources),
        out_specs=[pl.BlockSpec(memory_space=pltpu.VMEM)] * len(shapes),
        scratch_shapes=[pltpu.SemaphoreType.DMA((len(shapes),))],
        compiler_params=pltpu.CompilerParams(vmem_limit_bytes=40 << 20),
    )(at, *sources)
    return [out.reshape(-1, out.shape[-1]) for out in outs]


class Partial:
    def __init__(self, parts, dim, axis, deps=(), kind=jnp.bfloat16):
        self.parts, self.dim = (parts, dim)
        self.count, self.mine = (lax.axis_size(axis), lax.axis_index(axis))
        self.sent, self.came = ([], [])
        for k in range(1, self.count):
            route = [(i, (i + k) % self.count) for i in range(self.count)]
            block = self.take(lax.rem(self.mine + k, self.count)).astype(kind)
            block = after(block, deps)
            self.sent.append(block)
            self.came.append(lax.ppermute(block, axis, route))

    def take(self, j):
        taken = [lax.dynamic_index_in_dim(p, j, self.dim, keepdims=False) for p in self.parts]
        return taken[0] if len(taken) == 1 else jnp.concatenate(taken, axis=-2)

    def finish(self, kind=jnp.bfloat16, deps=()):
        total = self.take(self.mine).astype(jnp.float32)
        for block in after(tuple(self.came), deps):
            total = total + block.astype(jnp.float32)
        return total.astype(kind)


def first_xy(parts, deps=()):
    half = parts[0].shape[-1] // 2
    a, b = ([p[..., :half] for p in parts], [p[..., half:] for p in parts])
    return (Partial(a, 2, "x", deps), Partial(b, 0, "y", deps))


def second_xy(pair, deps=(), also=()):
    a, b = (part.finish(deps=also) for part in pair)
    return (Partial([a], 0, "y", deps), Partial([b], 1, "x", deps))


def last_z(pair, also=()):
    a, b = (part.finish(deps=also) for part in pair)
    whole = jnp.concatenate([a, b], axis=-1)
    return lax.psum_scatter(whole, "z", scatter_dimension=0, tiled=False).astype(jnp.float32)


def sent(*steps):
    return [block for step in steps for block in step.sent]


def came(*steps):
    return [block for step in steps for block in step.came]


def per_device(
    tokens,
    lengths,
    cotangent,
    first_gain,
    first_bias,
    mix_key,
    mix_value,
    mix_recept,
    time_decay,
    time_first,
    key_weight,
    value_weight,
    recept_weight,
    output_weight,
    second_gain,
    second_bias,
    shift_key,
    shift_recept,
    up_weight,
    gate_weight,
    down_weight,
):
    grid = tuple(lax.axis_size(axis) for axis in ALL)
    count = grid[0] * grid[1] * grid[2] * grid[3]
    seq_count, piece_len, channels = tokens.shape
    hidden = up_weight.shape[1]
    mine = channels // count
    blocks = hidden // channels

    vectors = (
        first_gain,
        first_bias,
        mix_key,
        mix_value,
        mix_recept,
        time_decay,
        time_first,
        second_gain,
        second_bias,
        shift_key,
        shift_recept,
    )
    n_vec = len(vectors)
    packed = jnp.pad(jnp.stack(vectors), ((0, 16 - n_vec), (0, channels - mine)))
    pieces = (
        [key_weight, value_weight, recept_weight, packed],
        [output_weight] + [up_weight[:, j * channels : (j + 1) * channels] for j in range(blocks)],
        [gate_weight, down_weight],
    )
    places = (
        [(0, 0), (1, 0), (2, 0), (3, 0)],
        [(0, 0)] + [(1, j * channels) for j in range(blocks)],
        [(0, 0), (1, 0)],
    )
    chunks = [jnp.concatenate(piece) for piece in pieces]
    plans = []
    for piece, place in zip(pieces, places):
        first, entries, shapes = (0, [], {})
        for part, (out, column) in zip(piece, place):
            entries.append((first, part.shape[0], out, column))
            shapes[out] = (part.shape[0], column + channels)
            first += part.shape[0]
        plans.append((entries, [shapes[o] for o in sorted(shapes)]))
    stepwise = mine % 16 == 0

    def whole(at):
        gathered = lax.all_gather(chunks[at], ALL, axis=0)
        entries, shapes = plans[at]
        outs = []
        for out, shape in enumerate(shapes):
            cols = [gathered[:, f : f + r] for f, r, o, _ in entries if o == out]
            outs.append(jnp.concatenate(cols, axis=-1).reshape(-1, shape[1]))
        return outs

    if stepwise:
        z0 = beside_z(chunks[0])
        z1 = beside_z(after(chunks[1], z0))
        z2 = beside_z(after(chunks[2], z1))
        xy0 = beside_xy(z0, ("x", "y"))
        a0, b0 = (jnp.stack(part) for part in xy0)
        yx0 = beside_xy((a0, b0), ("y", "x"))
        xy1 = beside_xy(after(z1, yx0), ("x", "y"))
        key_mat, value_mat, recept_mat, vecs = assemble(yx0, other_core(yx0), *plans[0], grid)
    else:
        key_mat, value_mat, recept_mat, vecs = whole(0)
    vecs = vecs.reshape(count, 16, channels)[:, :n_vec, :mine]
    vecs = jnp.moveaxis(vecs, 1, 0).reshape(n_vec, channels).astype(jnp.float32)
    (
        norm_gain,
        norm_bias,
        key_mix,
        value_mix,
        recept_mix,
        decay_log,
        boost_log_scale,
        gain_two,
        bias_two,
        chan_key_mix,
        chan_recept_mix,
    ) = (vecs[j] for j in range(n_vec))
    seq_index = lax.axis_index(SEQ)
    positions = seq_index * piece_len + jnp.arange(piece_len, dtype=jnp.int32)
    live_mask = (positions[None, :] < lengths[:, None]).astype(jnp.float32)[:, :, None]
    field = tokens.astype(jnp.float32)
    normed_one, inverse_one = norm_stats(field)
    normed = normed_one * norm_gain + norm_bias
    before = previous_rows(normed)
    key_in = (normed * key_mix + before * (1.0 - key_mix)).astype(jnp.bfloat16)
    value_in = (normed * value_mix + before * (1.0 - value_mix)).astype(jnp.bfloat16)
    recept_in = (normed * recept_mix + before * (1.0 - recept_mix)).astype(jnp.bfloat16)
    lookup_matrix_output = matmul("nlc,cd->nld", key_in, key_mat)
    content_matrix_output = matmul("nlc,cd->nld", value_in, value_mat)
    recept_proj = matmul("nlc,cd->nld", recept_in, recept_mat)
    if stepwise:
        pair = after(tuple(jnp.stack(part) for part in xy1), (recept_proj, content_matrix_output))
        yx1 = beside_xy(pair, ("y", "x"))
    fading_rate_vector = jnp.exp(decay_log)
    place = jnp.arange(piece_len, dtype=jnp.float32)[:, None]
    weight = jnp.exp(lookup_matrix_output - (piece_len - 1 - place) * fading_rate_vector)
    local = (jnp.sum(weight * content_matrix_output, axis=1), jnp.sum(weight, axis=1))
    piece_fall = jnp.exp(-piece_len * fading_rate_vector)
    starting_accumulator, starting_normalizer = entering(piece_fall, local, False)
    state_a, state_b, mixed_out = wkv_forward(
        lookup_matrix_output,
        content_matrix_output,
        recept_proj,
        starting_accumulator,
        starting_normalizer,
        boost_log_scale,
        fading_rate_vector,
    )
    if stepwise:
        xy2 = beside_xy(after(z2, (yx1, mixed_out)), ("x", "y"))
        output_mat, up_mat = assemble(yx1, other_core(yx1), *plans[1], grid)
    else:
        output_mat, up_mat = whole(1)
    branch = matmul("nlc,cd->nld", mixed_out, output_mat)
    residual = field + branch
    normed_two_raw, inverse_two = norm_stats(residual)
    normed_two = normed_two_raw * gain_two + bias_two
    before_two = previous_rows(normed_two)
    ffn_key = (normed_two * chan_key_mix + before_two * (1.0 - chan_key_mix)).astype(jnp.bfloat16)
    ffn_recept = (normed_two * chan_recept_mix + before_two * (1.0 - chan_recept_mix)).astype(
        jnp.bfloat16
    )
    if stepwise:
        pair = after(tuple(jnp.stack(part) for part in xy2), (ffn_key, ffn_recept))
        yx2 = beside_xy(pair, ("y", "x"))
    up_proj = matmul("nlc,cf->nlf", ffn_key, up_mat)
    relu_up = jax.nn.relu(up_proj)
    squared = jnp.square(relu_up).astype(jnp.bfloat16)
    relu_up = relu_up.astype(jnp.bfloat16)
    if stepwise:
        gate_mat, down_mat = assemble(yx2, other_core(yx2), *plans[2], grid)
    else:
        gate_mat, down_mat = whole(2)
    down_proj = matmul("nlf,fd->nld", squared, down_mat)
    gate_value = jax.nn.sigmoid(matmul("nlc,cd->nld", ffn_recept, gate_mat))
    output = ((residual + gate_value * down_proj) * live_mask).astype(jnp.bfloat16)

    core = lax.axis_index("core")

    def outer(left, right, at):
        width = left.shape[-1] // (2 * grid[0])
        cut = [left[..., k * width : (k + 1) * width] for k in range(2 * grid[0])]
        cut = [jnp.where(at == 0, a, b) for a, b in zip(cut[::2], cut[1::2])]
        left = jnp.concatenate(cut, axis=-1)
        rows = jnp.einsum("nlc,nld->cd", left, right, preferred_element_type=jnp.float32)
        return rows.reshape(grid[0], grid[2], grid[3], -1, right.shape[-1])

    def to_core(left, right):
        send = outer(left, right, 1 - core).astype(jnp.bfloat16)
        return send, spread(send, "core")[0]

    def both_cores(left, right, came):
        return (outer(left, right, core) + came.astype(jnp.float32)).astype(jnp.bfloat16)

    def by_columns(g):
        return [g[..., j * channels : (j + 1) * channels] for j in range(g.shape[-1] // channels)]

    seed = cotangent.astype(jnp.float32) * live_mask
    down_grad = (seed * gate_value).astype(jnp.bfloat16)
    gate_grad = (seed * down_proj * gate_value * (1.0 - gate_value)).astype(jnp.bfloat16)
    down_send, down_came = to_core(squared, down_grad)
    gate_send, gate_came = to_core(ffn_recept, gate_grad)
    squared_grad = matmul("nld,fd->nlf", after(down_grad, (down_send, gate_send)), down_mat)
    up_grad = (squared_grad * 2.0 * relu_up.astype(jnp.float32)).astype(jnp.bfloat16)
    up_send, up_came = to_core(ffn_key, up_grad)
    late = (down_grad, gate_grad, down_came, gate_came)
    d_grad, g_grad, down_came, gate_came = after(late, (up_send,))
    xy1 = first_xy([both_cores(squared, d_grad, down_came), both_cores(ffn_recept, g_grad, gate_came)])
    u_grad, gate_grad, up_came = after((up_grad, gate_grad, up_came), sent(*xy1))
    ffn_key_grad = matmul("nlf,cf->nlc", u_grad, up_mat)
    ffn_recept_grad = matmul("nld,cd->nlc", gate_grad, gate_mat)
    u_grad, up_came = after((u_grad, up_came), (ffn_key_grad, ffn_recept_grad))
    grad_up_part = by_columns(both_cores(ffn_key, u_grad, up_came))
    normed_two_grad = (
        ffn_key_grad * chan_key_mix
        + ffn_recept_grad * chan_recept_mix
        + next_rows(ffn_key_grad * (1.0 - chan_key_mix) + ffn_recept_grad * (1.0 - chan_recept_mix))
    )
    gap_two = normed_two - before_two
    grad_chan_key = jnp.sum(ffn_key_grad * gap_two, axis=(0, 1))
    grad_chan_recept = jnp.sum(ffn_recept_grad * gap_two, axis=(0, 1))
    grad_gain_two = jnp.sum(normed_two_grad * normed_two_raw, axis=(0, 1))
    grad_bias_two = jnp.sum(normed_two_grad, axis=(0, 1))
    residual_grad = seed + norm_back(normed_two_grad * gain_two, normed_two_raw, inverse_two)
    branch_grad = residual_grad.astype(jnp.bfloat16)
    yx1 = second_xy(xy1, also=(branch_grad,))
    branch_grad = after(branch_grad, sent(*yx1))
    mixed_grad = matmul("nld,cd->nlc", branch_grad, output_mat)
    out_send, out_came = to_core(mixed_out, branch_grad)
    bonus = jnp.exp(boost_log_scale) * jnp.exp(lookup_matrix_output)
    over = 1.0 / (state_b + bonus)
    blended = (state_a + bonus * content_matrix_output) * over
    recept_sig = jax.nn.sigmoid(recept_proj)
    recept_grad = (mixed_grad * blended * recept_sig * (1.0 - recept_sig)).astype(jnp.bfloat16)
    alpha = mixed_grad * recept_sig * over * jnp.exp(-place * fading_rate_vector)
    local = (jnp.sum(alpha, axis=1), -jnp.sum(alpha * blended, axis=1))
    carry_p, carry_q = entering(piece_fall, local, True)
    xy2 = first_xy(grad_up_part, deps=came(*yx1))
    z1 = last_z(yx1, also=sent(*xy2))
    recept_send, recept_came = to_core(recept_in, recept_grad)
    carry_p, carry_q = after((carry_p, carry_q), sent(*xy2) + [recept_send])
    key_grad, value_grad, grad_decay, boost_adjoint_term = wkv_backward(
        lookup_matrix_output,
        content_matrix_output,
        recept_proj,
        state_a,
        state_b,
        mixed_grad,
        carry_p,
        carry_q,
        boost_log_scale,
        fading_rate_vector,
    )
    key_send, key_came = to_core(key_in, key_grad)
    value_send, value_came = to_core(value_in, value_grad)
    part_out = both_cores(mixed_out, after(branch_grad, (key_send, value_send)), out_came)
    part_recept = both_cores(recept_in, after(recept_grad, (key_send, value_send)), recept_came)
    yx2 = second_xy(xy2, also=(part_out, part_recept))
    late = (key_grad, value_grad, key_came, value_came)
    k_grad, v_grad, key_came, value_came = after(late, sent(*yx2))
    part_key = both_cores(key_in, k_grad, key_came)
    part_value = both_cores(value_in, v_grad, value_came)
    k_grad, v_grad, r_grad = after((k_grad, v_grad, recept_grad), (part_key, part_value))
    xy3 = first_xy([part_out, part_recept, part_key, part_value], deps=came(*yx2))
    z2 = last_z(yx2, also=sent(*xy3))
    k_grad, v_grad, r_grad = after((k_grad, v_grad, r_grad), sent(*xy3))
    key_in_grad = matmul("nld,cd->nlc", k_grad, key_mat)
    value_in_grad = matmul("nld,cd->nlc", v_grad, value_mat)
    recept_in_grad = matmul("nld,cd->nlc", r_grad, recept_mat)
    normed_grad = (
        key_in_grad * key_mix
        + value_in_grad * value_mix
        + recept_in_grad * recept_mix
        + next_rows(
            key_in_grad * (1.0 - key_mix)
            + value_in_grad * (1.0 - value_mix)
            + recept_in_grad * (1.0 - recept_mix)
        )
    )
    gap_one = normed - before
    grad_key_mix = jnp.sum(key_in_grad * gap_one, axis=(0, 1))
    grad_value_mix = jnp.sum(value_in_grad * gap_one, axis=(0, 1))
    grad_recept_mix = jnp.sum(recept_in_grad * gap_one, axis=(0, 1))
    grad_gain_one = jnp.sum(normed_grad * normed_one, axis=(0, 1))
    grad_bias_one = jnp.sum(normed_grad, axis=(0, 1))
    tokens_grad = residual_grad + norm_back(normed_grad * norm_gain, normed_one, inverse_one)
    sums = jnp.stack(
        [
            grad_gain_one,
            grad_bias_one,
            grad_key_mix,
            grad_value_mix,
            grad_recept_mix,
            grad_decay,
            boost_adjoint_term,
            grad_gain_two,
            grad_bias_two,
            grad_chan_key,
            grad_chan_recept,
        ]
    )
    sums = jnp.moveaxis(sums.reshape(n_vec, *grid, mine), 0, -2)
    yx3 = second_xy(xy3, also=(tokens_grad,))
    for dim, axis in ((1, "core"), (2, "x"), (0, "y"), (0, "z")):
        sums = Partial([sums], dim, axis, kind=jnp.float32).finish(jnp.float32)
    third = last_z(yx3)
    first, second = (z1, z2)
    rows_down = hidden // count
    return (
        output,
        tokens_grad,
        *(sums[j] for j in range(7)),
        third[2 * mine : 3 * mine],
        third[3 * mine :],
        third[mine : 2 * mine],
        third[:mine],
        *(sums[j] for j in range(7, n_vec)),
        jnp.concatenate([second[j * mine : (j + 1) * mine] for j in range(blocks)], axis=1),
        first[rows_down:],
        first[:rows_down],
    )


def solution(mesh):
    seq, dp = (mesh.shape["seq"], mesh.shape["dp"])
    wide = len({device.coords[0] for device in mesh.devices.reshape(-1)})
    fine = jax.sharding.Mesh(mesh.devices.reshape(seq // 2, 2, dp // wide, wide), ALL)
    field, vector, matrix = (P(DP, SEQ, None), P(ALL), P(ALL, None))
    return jax.shard_map(
        per_device,
        mesh=fine,
        in_specs=(field, P(DP), field) + (vector,) * 7 + (matrix,) * 4 + (vector,) * 4 + (matrix,) * 3,
        out_specs=(field, field) + (vector,) * 7 + (matrix,) * 4 + (vector,) * 4 + (matrix,) * 3,
        check_vma=False,
    )
```

```python
import functools

import jax
import jax.numpy as jnp
from jax import lax
from jax.experimental import pallas as pl
from jax.experimental.pallas import tpu as pltpu
from jax.sharding import PartitionSpec as P

EPS = 1e-05

def norm_stats(field):
    center = field - jnp.mean(field, axis=-1, keepdims=True)
    inverse = lax.rsqrt(jnp.mean(center * center, axis=-1, keepdims=True) + EPS)
    return (center * inverse, inverse)


def norm_back(grad_normed, normalized, inverse):
    mean_grad = jnp.mean(grad_normed, axis=-1, keepdims=True)
    mean_proj = jnp.mean(grad_normed * normalized, axis=-1, keepdims=True)
    return inverse * (grad_normed - mean_grad - normalized * mean_proj)


SEQ = ("y", "core")
DP = ("z", "x")
ALL = ("y", "core", "z", "x")


def scan_tiles(rate, reverse):
    row = lax.broadcasted_iota(jnp.int32, (8, rate.shape[-1]), 0)
    steps = []
    for distance in (1, 2, 4):
        inside = row < 8 - distance if reverse else row >= distance
        steps.append((distance, jnp.where(inside, jnp.exp(-float(distance) * rate), 0.0)))
    return row, steps


def turn(x, distance, reverse):
    return pltpu.roll(x, 8 - distance if reverse else distance, 0)


def scan_rows(x, steps, reverse):
    for distance, factor in steps:
        x = x + factor * turn(x, distance, reverse)
    return x


def wkv_kernel(k_ref, v_ref, r_ref, a0_ref, b0_ref, u_ref, rate_ref, a_ref, b_ref, mixed_ref):
    seqs, span, lanes = k_ref.shape
    rate = rate_ref[...]
    boost = jnp.exp(u_ref[...])
    row, steps = scan_tiles(rate, False)
    falling = jnp.exp(-row.astype(jnp.float32) * rate)
    fall_all = jnp.exp(-8.0 * rate)
    first = row < 1
    pair = 16

    def body(i, carry):
        at = pl.ds(pl.multiple_of(i * pair, pair), pair)
        new = []
        for n in range(seqs):
            k16, v16, r16 = (ref[n, at, :] for ref in (k_ref, v_ref, r_ref))
            state = carry[2 * n : 2 * n + 2]
            tiles = []
            for g in range(2):
                k, v, r = (t[g * 8 : g * 8 + 8] for t in (k16, v16, r16))
                weight = jnp.exp(k)
                bonus = boost * weight
                sums = [scan_rows(t, steps, False) for t in (weight * v, weight)]
                a, b = (
                    falling * c + jnp.where(first, 0.0, turn(t, 1, False))
                    for c, t in zip(state, sums)
                )
                state = tuple(fall_all * c + t[7:8] for c, t in zip(state, sums))
                mixed = jax.nn.sigmoid(r) * ((a + bonus * v) / (b + bonus))
                tiles.append((a, b, mixed))
            a, b, mixed = (jnp.concatenate(t, axis=0) for t in zip(*tiles))
            a_ref[n, at, :] = a
            b_ref[n, at, :] = b
            mixed_ref[n, at, :] = mixed.astype(mixed_ref.dtype)
            new += state
        return tuple(new)

    start = []
    for n in range(seqs):
        start += [a0_ref[n : n + 1, :], b0_ref[n : n + 1, :]]
    lax.fori_loop(0, span // pair, body, tuple(start), unroll=2)


def wkv_back_kernel(
    k_ref, v_ref, r_ref, a_ref, b_ref, g_ref, p0_ref, q0_ref, u_ref, rate_ref,
    k_out, v_out, rate_out, first_out,
):
    seqs, span, lanes = k_ref.shape
    rate = rate_ref[...]
    boost = jnp.exp(u_ref[...])
    row, steps = scan_tiles(rate, True)
    falling = jnp.exp((row.astype(jnp.float32) - 7.0) * rate)
    fall_all = jnp.exp(-8.0 * rate)
    last = row > 6
    pair = 16
    count = span // pair

    def body(i, carry):
        at = pl.ds(pl.multiple_of((count - 1 - i) * pair, pair), pair)
        new = []
        rate_sum, first_sum = carry[-2:]
        for n in range(seqs):
            loaded = [ref[n, at, :] for ref in (k_ref, v_ref, r_ref, a_ref, b_ref, g_ref)]
            state = carry[2 * n : 2 * n + 2]
            tiles = []
            for g in (1, 0):
                k, v, r, a, b, grad = (t[g * 8 : g * 8 + 8] for t in loaded)
                weight = jnp.exp(k)
                bonus = boost * weight
                over = 1.0 / (b + bonus)
                wkv = (a + bonus * v) * over
                alpha = grad * jax.nn.sigmoid(r) * over
                sums = [scan_rows(t, steps, True) for t in (alpha, -alpha * wkv)]
                p, q = (
                    falling * c + jnp.where(last, 0.0, turn(t, 1, True))
                    for c, t in zip(state, sums)
                )
                state = tuple(fall_all * c + t[0:1] for c, t in zip(state, sums))
                share = alpha * bonus
                own = share * (v - wkv)
                tiles.append((own + weight * (p * v + q), share + weight * p))
                rate_sum = rate_sum + (a * p + b * q)
                first_sum = first_sum + own
            k_grad, v_grad = (jnp.concatenate(t, axis=0) for t in zip(*tiles[::-1]))
            k_out[n, at, :] = k_grad.astype(k_out.dtype)
            v_out[n, at, :] = v_grad.astype(v_out.dtype)
            new += state
        return tuple(new) + (rate_sum, first_sum)

    start = []
    for n in range(seqs):
        start += [p0_ref[n : n + 1, :], q0_ref[n : n + 1, :]]
    zero = jnp.zeros((8, lanes), jnp.float32)
    done = lax.fori_loop(0, count, body, tuple(start) + (zero, zero), unroll=2)
    rate_out[...] = -rate * jnp.exp(-rate) * jnp.sum(done[-2], axis=0, keepdims=True)
    first_out[...] = jnp.sum(done[-1], axis=0, keepdims=True)


def first_kernel(flag_ref, tok_ref, prev_ref, vec_ref, w_ref, x0_ref, x1_ref, x2_ref, y_ref, local_ref, normed, before, key):
    seqs, span, channels = tok_ref.shape
    j = pl.program_id(0)

    @pl.when(j == 0)
    def _():
        gain, bias = (vec_ref[0:1, :], vec_ref[1:2, :])
        for n in range(seqs):
            rows = pl.ds(n * span, span)
            field = norm_stats(tok_ref[n].astype(jnp.float32))[0] * gain + bias
            edge = norm_stats(prev_ref[n : n + 1, :].astype(jnp.float32))[0] * gain + bias
            edge = jnp.where(flag_ref[0] > 0, edge, 0.0)
            row = lax.broadcasted_iota(jnp.int32, field.shape, 0)
            normed[rows, :] = field
            before[rows, :] = jnp.where(row < 1, edge, pltpu.roll(field, 1, 0))

    mix = vec_ref[pl.ds(2 + j, 1), :]
    x = (normed[...] * mix + before[...] * (1.0 - mix)).astype(jnp.bfloat16)
    y = jnp.dot(x, w_ref[0], preferred_element_type=jnp.float32)
    y_ref[0] = y.reshape(seqs, span, channels)
    for k, ref in enumerate((x0_ref, x1_ref, x2_ref)):

        @pl.when(j == k)
        def _(ref=ref):
            ref[...] = x.reshape(seqs, span, channels)

    @pl.when(j == 0)
    def _():
        key[...] = y

    @pl.when(j == 1)
    def _():
        rate = vec_ref[5:6, :]
        place = lax.broadcasted_iota(jnp.int32, (span, channels), 0).astype(jnp.float32)
        fall = (place - (span - 1.0)) * rate
        for n in range(seqs):
            rows = slice(n * span, (n + 1) * span)
            weight = jnp.exp(key[rows, :] + fall)
            local_ref[0, n : n + 1, :] = jnp.sum(weight * y[rows], axis=0, keepdims=True)
            local_ref[1, n : n + 1, :] = jnp.sum(weight, axis=0, keepdims=True)


def first_projections(flag, tokens, prev, vectors, mats):
    seqs, span, channels = tokens.shape
    fixed = lambda *shape: pl.BlockSpec(shape, lambda j: (0,) * len(shape))
    rows = (seqs * span, channels)
    outs = pl.pallas_call(
        first_kernel,
        grid=(3,),
        out_shape=[jax.ShapeDtypeStruct(tokens.shape, jnp.bfloat16)] * 3
        + [jax.ShapeDtypeStruct((3, *tokens.shape), jnp.float32)]
        + [jax.ShapeDtypeStruct((2, seqs, channels), jnp.float32)],
        in_specs=[
            pl.BlockSpec(memory_space=pltpu.SMEM),
            fixed(*tokens.shape),
            fixed(*prev.shape),
            fixed(*vectors.shape),
            pl.BlockSpec((1, channels, channels), lambda j: (j, 0, 0)),
        ],
        out_specs=[fixed(*tokens.shape)] * 3
        + [pl.BlockSpec((1, *tokens.shape), lambda j: (j, 0, 0, 0)), fixed(2, seqs, channels)],
        scratch_shapes=[pltpu.VMEM(rows, jnp.float32)] * 3,
        compiler_params=pltpu.CompilerParams(vmem_limit_bytes=48 << 20),
        cost_estimate=pl.CostEstimate(flops=1 << 20, bytes_accessed=1 << 16, transcendentals=0),
    )(flag, tokens, prev, vectors, mats)
    return outs[:3], outs[3], outs[4]


def ffn_back_kernel(grad_ref, relu_ref, down_ref, up_ref, up_grad_ref, out_ref):
    wide = (((1,), (1,)), ((), ()))
    squared = lax.dot_general(grad_ref[...], down_ref[...], wide, preferred_element_type=jnp.float32)
    up_grad = (squared * (2.0 * relu_ref[...].astype(jnp.float32))).astype(jnp.bfloat16)
    up_grad_ref[...] = up_grad
    part = lax.dot_general(up_grad, up_ref[...], wide, preferred_element_type=jnp.float32)

    @pl.when(pl.program_id(0) == 0)
    def _():
        out_ref[...] = part

    @pl.when(pl.program_id(0) > 0)
    def _():
        out_ref[...] += part


def ffn_backward(grad, relu_up, down, up):
    rows, channels = grad.shape
    hidden = up.shape[1]
    block = 512
    column = pl.BlockSpec((rows, block), lambda j: (0, j))
    return pl.pallas_call(
        ffn_back_kernel,
        grid=(hidden // block,),
        out_shape=[
            jax.ShapeDtypeStruct((rows, hidden), jnp.bfloat16),
            jax.ShapeDtypeStruct((rows, channels), jnp.float32),
        ],
        in_specs=[
            pl.BlockSpec((rows, channels), lambda j: (0, 0)),
            column,
            pl.BlockSpec((block, channels), lambda j: (j, 0)),
            pl.BlockSpec((channels, block), lambda j: (0, j)),
        ],
        out_specs=[column, pl.BlockSpec((rows, channels), lambda j: (0, 0))],
        compiler_params=pltpu.CompilerParams(vmem_limit_bytes=40 << 20),
        cost_estimate=pl.CostEstimate(
            flops=1 << 20, bytes_accessed=24 << 20, transcendentals=0
        ),
    )(grad, relu_up, down, up)


def in_grads_kernel(k_ref, v_ref, r_ref, gap_ref, mix_ref, w_ref, now_ref, next_ref, sum_ref):
    j = pl.program_id(0)
    grad = jnp.where(j == 0, k_ref[...], jnp.where(j == 1, v_ref[...], r_ref[...]))
    wide = (((1,), (1,)), ((), ()))
    part = lax.dot_general(grad, w_ref[0], wide, preferred_element_type=jnp.float32)
    mix = mix_ref[pl.ds(j, 1), :]
    now = part * mix
    sum_ref[pl.ds(j, 1), :] = jnp.sum(part * gap_ref[...], axis=0, keepdims=True)

    @pl.when(j == 0)
    def _():
        now_ref[...] = now
        next_ref[...] = part - now

    @pl.when(j > 0)
    def _():
        now_ref[...] += now
        next_ref[...] += part - now


def input_gradients(grads, gap, mixes, mats):
    rows, channels = gap.shape
    fixed = lambda *shape: pl.BlockSpec(shape, lambda j: (0,) * len(shape))
    return pl.pallas_call(
        in_grads_kernel,
        grid=(3,),
        out_shape=[jax.ShapeDtypeStruct(gap.shape, jnp.float32)] * 2
        + [jax.ShapeDtypeStruct((3, channels), jnp.float32)],
        in_specs=[fixed(rows, channels)] * 4
        + [fixed(3, channels), pl.BlockSpec((1, channels, channels), lambda j: (j, 0, 0))],
        out_specs=[fixed(rows, channels)] * 2 + [fixed(3, channels)],
        compiler_params=pltpu.CompilerParams(vmem_limit_bytes=40 << 20),
        cost_estimate=pl.CostEstimate(flops=1 << 20, bytes_accessed=8 << 20, transcendentals=0),
    )(*grads, gap, mixes, mats)


LANES = 256


def wkv_specs(seqs, span):
    field = pl.BlockSpec((seqs, span, LANES), lambda j: (0, 0, j))
    state = pl.BlockSpec((seqs, LANES), lambda j: (0, j))
    vector = pl.BlockSpec((1, LANES), lambda j: (0, j))
    return field, state, vector


def stacked_specs(seqs, span):
    shape = (None, seqs, span, LANES)
    return [pl.BlockSpec(shape, lambda j, n=n: (n, 0, 0, j)) for n in range(3)]


def wkv_forward(kvr, a0, b0, u, rate):
    shape = kvr.shape[1:]
    _, span, channels = shape
    seqs = shape[0]
    field, state, vector = wkv_specs(seqs, span)
    return pl.pallas_call(
        wkv_kernel,
        grid=(channels // LANES,),
        out_shape=[jax.ShapeDtypeStruct(shape, t) for t in (jnp.float32, jnp.float32, jnp.bfloat16)],
        in_specs=stacked_specs(seqs, span) + [state] * 2 + [vector] * 2,
        out_specs=[field] * 3,
        compiler_params=pltpu.CompilerParams(vmem_limit_bytes=32 << 20),
        cost_estimate=pl.CostEstimate(flops=1 << 20, bytes_accessed=1 << 16, transcendentals=0),
    )(kvr, kvr, kvr, a0, b0, u[None], rate[None])


def wkv_backward(kvr, a, b, grad, p0, q0, u, rate):
    seqs, span, channels = a.shape
    field, state, vector = wkv_specs(seqs, span)
    k_grad, v_grad, decay_grad, first_grad = pl.pallas_call(
        wkv_back_kernel,
        grid=(channels // LANES,),
        out_shape=[jax.ShapeDtypeStruct(a.shape, jnp.bfloat16)] * 2
        + [jax.ShapeDtypeStruct((1, channels), jnp.float32)] * 2,
        in_specs=stacked_specs(seqs, span) + [field] * 3 + [state] * 2 + [vector] * 2,
        out_specs=[field] * 2 + [vector] * 2,
        compiler_params=pltpu.CompilerParams(vmem_limit_bytes=32 << 20),
        cost_estimate=pl.CostEstimate(flops=1 << 20, bytes_accessed=1 << 16, transcendentals=0),
    )(kvr, kvr, kvr, a, b, grad, p0, q0, u[None], rate[None])
    return k_grad, v_grad, decay_grad[0], first_grad[0]


def matmul(form, left, right):
    return jnp.einsum(form, left, right, preferred_element_type=jnp.float32)


def shifted(block, axis, distance):
    count = lax.axis_size(axis)
    route = [(i - distance, i) for i in range(count) if 0 <= i - distance < count]
    return lax.ppermute(block, axis, route)


def previous_rows(field):
    came = shifted(field[:, -1, :], SEQ, 1)
    return jnp.concatenate([came[:, None, :], field[:, :-1, :]], axis=1)


def next_rows(field):
    came = shifted(field[:, 0, :], SEQ, -1)
    return jnp.concatenate([field[:, 1:, :], came[:, None, :]], axis=1)


def entering(factor, states, reverse):
    block = jnp.stack(states)
    low, high = in_order(block, spread(block, "core")[0])
    near, far = (high, low) if reverse else (low, high)
    chip = factor * near + far
    total, power = (jnp.zeros_like(block), jnp.ones_like(factor))
    for k in range(1, lax.axis_size("y")):
        total = total + power * shifted(chip, "y", -k if reverse else k)
        power = power * factor * factor
    core = lax.axis_index("core")
    total = jnp.where(core == (1 if reverse else 0), total, factor * total + near)
    return (total[0], total[1])


def in_order(own, other):
    core = lax.axis_index("core")
    return (jnp.where(core == 0, own, other), jnp.where(core == 0, other, own))


def own_half(x, own=True):
    half = x.shape[-1] // 2
    core = lax.axis_index("core")
    return jnp.where((core == 0) == own, x[..., :half], x[..., half:])


def after(x, deps):
    return lax.optimization_barrier((x, deps))[0] if jax.tree.leaves(deps) else x


def spread(block, axis):
    count = lax.axis_size(axis)
    return [
        lax.ppermute(block, axis, [(i, (i + k) % count) for i in range(count)])
        for k in range(1, count)
    ]


def cross(block, first, k):
    ys, cs, zs, xs = (lax.axis_size(axis) for axis in ALL)
    route = []
    for i in range(ys * cs * zs * xs):
        y, c, z, x = (i // (cs * zs * xs), i // (zs * xs) % cs, i // xs % zs, i % xs)
        if (c == 0) == first:
            x = (x + k) % xs
        else:
            y = (y + k) % ys
        route.append((i, ((y * cs + c) * zs + z) * xs + x))
    return lax.ppermute(block, ALL, route)


def beside_z(own):
    half = own.shape[1] // 2
    rows = lax.all_gather(own, "z", axis=0)
    return (rows[:, :, :half], rows[:, :, half:])


def beside_xy(pair, axes):
    return [[block] + spread(block, axis) for block, axis in zip(pair, axes)]


def other_core(parts):
    return [[spread(block, "core")[0] for block in part] for part in parts]


def assemble_kernel(entries, grid, at_ref, *refs):
    n_out = 1 + max(entry[2] for entry in entries)
    sources, outs, sems = (refs[: -n_out - 1], refs[-n_out - 1 : -1], refs[-1])
    ys, cs, zs, xs = grid
    y, c, x = (at_ref[j] for j in range(3))

    def back(at, k, count):
        return lax.rem(at - k + count, count)

    index = 0
    for dc in range(cs):
        for half, lead in enumerate((xs, ys)):
            for far in range(ys if half == 0 else xs):
                source = sources[index]
                index += 1

                def copy(k, _, source=source, dc=dc, half=half, far=far):
                    near, dz = (k // zs, lax.rem(k, zs))
                    dy, dx = (far, near) if half == 0 else (near, far)
                    block = back(y, dy, ys) * cs + back(c, dc, cs)
                    block = (block * zs + dz) * xs + back(x, dx, xs)
                    for first, rows, out, column, lead_at in entries:
                        width = source.shape[-1]
                        pltpu.make_async_copy(
                            source.at[near, dz, pl.ds(first, rows), :],
                            outs[out].at[lead_at, block, :, pl.ds(column + half * width, width)],
                            sems.at[out],
                        ).start()
                    return 0

                lax.fori_loop(0, lead * zs, copy, 0)
    for out in range(n_out):
        pltpu.make_async_copy(outs[out], outs[out], sems.at[out]).wait()


def assemble(mine, other, entries, shapes, grid):
    sources = [b for part in mine for b in part] + [b for part in other for b in part]
    at = jnp.stack([lax.axis_index(axis) for axis in ("y", "core", "x")]).astype(jnp.int32)
    count = grid[0] * grid[1] * grid[2] * grid[3]
    outs = pl.pallas_call(
        functools.partial(assemble_kernel, entries, grid),
        out_shape=[jax.ShapeDtypeStruct((n, count, *shape), jnp.bfloat16) for n, *shape in shapes],
        in_specs=[pl.BlockSpec(memory_space=pltpu.SMEM)]
        + [pl.BlockSpec(memory_space=pl.ANY)] * len(sources),
        out_specs=[pl.BlockSpec(memory_space=pltpu.VMEM)] * len(shapes),
        scratch_shapes=[pltpu.SemaphoreType.DMA((len(shapes),))],
        compiler_params=pltpu.CompilerParams(vmem_limit_bytes=40 << 20),
    )(at, *sources)
    return [out.reshape(out.shape[0], -1, out.shape[-1]) for out in outs]


class Partial:
    def __init__(self, parts, first, deps=()):
        self.parts, self.first = (parts, first)
        self.sent, self.came = ([], [])
        for k in range(1, lax.axis_size("x")):
            blocks = [after(self.take(p, k), deps) for p in parts]
            self.sent += blocks
            self.came.append([cross(block, first, k) for block in blocks])

    def take(self, p, k):
        count = lax.axis_size("x")
        x, y = (lax.rem(lax.axis_index(axis) + k, count) for axis in ("x", "y"))
        core = lax.axis_index("core")
        if self.first:
            by_x = lax.dynamic_index_in_dim(p, x, 3, keepdims=False).transpose(2, 1, 0, 3, 4)
            by_y = lax.dynamic_index_in_dim(p, y, 0, keepdims=False).transpose(1, 0, 2, 3, 4)
            return jnp.where(core == 0, by_x, by_y)
        return lax.dynamic_index_in_dim(p, jnp.where(core == 0, y, x), 2, keepdims=False)

    def finish(self, deps=()):
        totals = [self.take(p, 0).astype(jnp.float32) for p in self.parts]
        for blocks in after(self.came, deps):
            totals = [total + block.astype(jnp.float32) for total, block in zip(totals, blocks)]
        return [total.astype(jnp.bfloat16) for total in totals]


def stacked(parts, width):
    cut = [p[..., j : j + width] for p in parts for j in range(0, p.shape[-1], width)]
    return jnp.concatenate(cut, axis=2)


def over_z_direct(total):
    count, at = (lax.axis_size("z"), lax.axis_index("z"))
    block = lambda k: lax.dynamic_index_in_dim(total, lax.rem(at + k, count), 0, keepdims=False)
    out = block(0).astype(jnp.float32)
    for k in range(1, count):
        route = [(i, (i + k) % count) for i in range(count)]
        out = out + lax.ppermute(block(k), "z", route).astype(jnp.float32)
    return out.astype(jnp.bfloat16)


def over_z(total):
    zs, cores, rows, columns = total.shape
    flat = total.reshape(zs * cores * rows, columns)
    return lax.psum_scatter(flat, "z", scatter_dimension=0, tiled=True).reshape(cores, rows, columns)


def to_owner(total):
    core = lax.axis_index("core")
    came = spread(lax.dynamic_index_in_dim(total, 1 - core, 0, keepdims=False), "core")[0]
    return in_order(lax.dynamic_index_in_dim(total, core, 0, keepdims=False), came)


def per_device(
    tokens,
    lengths,
    cotangent,
    first_gain,
    first_bias,
    mix_key,
    mix_value,
    mix_recept,
    time_decay,
    time_first,
    key_weight,
    value_weight,
    recept_weight,
    output_weight,
    second_gain,
    second_bias,
    shift_key,
    shift_recept,
    up_weight,
    gate_weight,
    down_weight,
):
    grid = tuple(lax.axis_size(axis) for axis in ALL)
    count = grid[0] * grid[1] * grid[2] * grid[3]
    seq_count, piece_len, channels = tokens.shape
    hidden = up_weight.shape[1]
    mine = channels // count
    blocks = hidden // channels

    vectors = (
        first_gain,
        first_bias,
        mix_key,
        mix_value,
        mix_recept,
        time_decay,
        time_first,
        second_gain,
        second_bias,
        shift_key,
        shift_recept,
    )
    n_vec = len(vectors)
    packed = jnp.pad(jnp.stack(vectors), ((0, 16 - n_vec), (0, channels - mine)))
    pieces = (
        [key_weight, value_weight, recept_weight, packed],
        [output_weight] + [up_weight[:, j * channels : (j + 1) * channels] for j in range(blocks)],
        [gate_weight, down_weight],
    )
    places = (
        [(0, 0, 0), (0, 0, 1), (0, 0, 2), (1, 0, 0)],
        [(0, 0, 0)] + [(1, j * channels, 0) for j in range(blocks)],
        [(0, 0, 0), (1, 0, 0)],
    )
    chunks = [jnp.concatenate(piece) for piece in pieces]
    plans = []
    for piece, place in zip(pieces, places):
        first, entries, shapes = (0, [], {})
        for part, (out, column, lead) in zip(piece, place):
            entries.append((first, part.shape[0], out, column, lead))
            shapes[out] = (lead + 1, part.shape[0], column + channels)
            first += part.shape[0]
        plans.append((entries, [shapes[o] for o in sorted(shapes)]))
    stepwise = mine % 16 == 0

    def whole(at):
        gathered = lax.all_gather(chunks[at], ALL, axis=0)
        entries, shapes = plans[at]
        outs = []
        for out, (leads, _, columns) in enumerate(shapes):
            parts = [gathered[:, f : f + r] for f, r, o, _, _ in entries if o == out]
            if leads == 1:
                parts = [jnp.concatenate(parts, axis=-1)]
            outs.append(jnp.stack([p.reshape(-1, columns) for p in parts]))
        return outs

    if stepwise:
        half = channels // 2
        xy2 = beside_xy((chunks[2][:, :half], chunks[2][:, half:]), ("x", "y"))
        z0 = beside_z(chunks[0])
        z1 = beside_z(after(chunks[1], z0))
        z2 = [lax.all_gather(jnp.stack(part), "z", axis=1) for part in after(xy2, z0)]
        xy0 = beside_xy(after(z0, xy2), ("x", "y"))
        yx0 = beside_xy([jnp.stack(part) for part in xy0], ("y", "x"))
        xy1 = beside_xy(after(z1, yx0), ("x", "y"))
        first_mats, vecs = assemble(yx0, other_core(yx0), *plans[0], grid)
    else:
        first_mats, vecs = whole(0)
    vecs = vecs.reshape(count, 16, channels)[:, :n_vec, :mine]
    vecs = jnp.moveaxis(vecs, 1, 0).reshape(n_vec, channels).astype(jnp.float32)
    (
        norm_gain,
        norm_bias,
        key_mix,
        value_mix,
        recept_mix,
        decay_log,
        boost_log_scale,
        gain_two,
        bias_two,
        chan_key_mix,
        chan_recept_mix,
    ) = (vecs[j] for j in range(n_vec))
    seq_index = lax.axis_index(SEQ)
    positions = seq_index * piece_len + jnp.arange(piece_len, dtype=jnp.int32)
    live_mask = (positions[None, :] < lengths[:, None]).astype(jnp.float32)[:, :, None]
    field = tokens.astype(jnp.float32)
    normed_one, inverse_one = norm_stats(field)
    normed = normed_one * norm_gain + norm_bias
    before = previous_rows(normed)
    fading_rate_vector = jnp.exp(decay_log)
    place = jnp.arange(piece_len, dtype=jnp.float32)[:, None]
    piece_fall = jnp.exp(-piece_len * fading_rate_vector)
    rows = jnp.stack([norm_gain, norm_bias, key_mix, value_mix, recept_mix, fading_rate_vector])
    ins, kvr, local = first_projections(
        (seq_index > 0).astype(jnp.int32)[None], tokens, shifted(tokens[:, -1, :], SEQ, 1), rows, first_mats
    )
    if stepwise:
        pair = [jnp.stack(part) for part in after(xy1, (ins, local))]
        local = after(local, pair)
        yx1 = beside_xy(pair, ("y", "x"))
        core1 = other_core([[part[0]] for part in yx1])
    key_in, value_in, recept_in = ins
    lookup_matrix_output, content_matrix_output, recept_proj = kvr
    local = (local[0], local[1])
    starting_accumulator, starting_normalizer = entering(piece_fall, local, False)
    if stepwise:
        starting_accumulator, starting_normalizer = after(
            (starting_accumulator, starting_normalizer), (yx1, core1, z2)
        )
    state_a, state_b, mixed_out = wkv_forward(
        kvr,
        starting_accumulator,
        starting_normalizer,
        boost_log_scale,
        fading_rate_vector,
    )
    if stepwise:
        yx2 = beside_xy(after(tuple(z2), yx1), ("y", "x"))
        rest1 = other_core([part[1:] for part in yx1])
        core1 = [one + rest for one, rest in zip(core1, rest1)]
        yx1 = after(yx1, (state_a, state_b))
        (output_mat,), (up_mat,) = assemble(yx1, core1, *plans[1], grid)
    else:
        (output_mat,), (up_mat,) = whole(1)
    branch = matmul("nlc,cd->nld", mixed_out, output_mat)
    residual = field + branch
    normed_two_raw, inverse_two = norm_stats(residual)
    normed_two = normed_two_raw * gain_two + bias_two
    before_two = previous_rows(normed_two)
    ffn_key = (normed_two * chan_key_mix + before_two * (1.0 - chan_key_mix)).astype(jnp.bfloat16)
    ffn_recept = (normed_two * chan_recept_mix + before_two * (1.0 - chan_recept_mix)).astype(
        jnp.bfloat16
    )
    up_proj = matmul("nlc,cf->nlf", ffn_key, up_mat)
    relu_up = jax.nn.relu(up_proj)
    squared = jnp.square(relu_up).astype(jnp.bfloat16)
    relu_up = relu_up.astype(jnp.bfloat16)
    if stepwise:
        core2 = other_core([[part] for part in after(tuple(z2), (ffn_key, ffn_recept))])
        yx2 = after(yx2, (squared, relu_up, core2))
        rest2 = other_core([part[1:] for part in yx2])
        core2 = [one + rest for one, rest in zip(core2, rest2)]
        (gate_mat,), (down_mat,) = assemble(yx2, core2, *plans[2], grid)
    else:
        (gate_mat,), (down_mat,) = whole(2)
    down_proj = matmul("nlf,fd->nld", squared, down_mat)
    gate_value = jax.nn.sigmoid(matmul("nlc,cd->nld", ffn_recept, gate_mat))
    output = ((residual + gate_value * down_proj) * live_mask).astype(jnp.bfloat16)

    def outer(left, right):
        return jnp.einsum("nlc,nld->cd", left, right, preferred_element_type=jnp.float32)

    def to_core(left, right):
        send = outer(left, own_half(right, False)).astype(jnp.bfloat16)
        return send, spread(send, "core")[0]

    def both_cores(left, right, came):
        rows = outer(left, own_half(right)) + came.astype(jnp.float32)
        return rows.astype(jnp.bfloat16).reshape(*grid, -1, rows.shape[-1])

    seed = cotangent.astype(jnp.float32) * live_mask
    down_grad = (seed * gate_value).astype(jnp.bfloat16)
    gate_grad = (seed * down_proj * gate_value * (1.0 - gate_value)).astype(jnp.bfloat16)
    width = channels // 2
    down_send, down_came = to_core(squared, down_grad)
    gate_send, gate_came = to_core(ffn_recept, gate_grad)
    ffn_recept_grad = matmul("nld,cd->nlc", after(gate_grad, (down_send, gate_send)), gate_mat)
    late = (down_grad, gate_grad, down_came, gate_came)
    d_grad, g_grad, down_came, gate_came = after(late, ffn_recept_grad)
    way1 = Partial([both_cores(squared, d_grad, down_came), both_cores(ffn_recept, g_grad, gate_came)], True)
    flat = (seq_count * piece_len, -1)
    up_grad, ffn_key_grad = ffn_backward(
        after(down_grad, way1.sent).reshape(flat), relu_up.reshape(flat), down_mat, up_mat
    )
    up_grad = up_grad.reshape(seq_count, piece_len, hidden)
    ffn_key_grad = ffn_key_grad.reshape(tokens.shape)
    up_send, up_came = to_core(ffn_key, up_grad)
    u_grad, up_came = after((up_grad, up_came), up_send)
    grad_up_part = both_cores(ffn_key, u_grad, up_came)
    normed_two_grad = (
        ffn_key_grad * chan_key_mix
        + ffn_recept_grad * chan_recept_mix
        + next_rows(ffn_key_grad * (1.0 - chan_key_mix) + ffn_recept_grad * (1.0 - chan_recept_mix))
    )
    gap_two = normed_two - before_two
    grad_chan_key = jnp.sum(ffn_key_grad * gap_two, axis=(0, 1))
    grad_chan_recept = jnp.sum(ffn_recept_grad * gap_two, axis=(0, 1))
    grad_gain_two = jnp.sum(normed_two_grad * normed_two_raw, axis=(0, 1))
    grad_bias_two = jnp.sum(normed_two_grad, axis=(0, 1))
    residual_grad = seed + norm_back(normed_two_grad * gain_two, normed_two_raw, inverse_two)
    branch_grad = residual_grad.astype(jnp.bfloat16)
    back1 = Partial(way1.finish(deps=(branch_grad,)), False)
    branch_grad = after(branch_grad, back1.sent)
    mixed_grad = matmul("nld,cd->nlc", branch_grad, output_mat)
    out_send, out_came = to_core(mixed_out, branch_grad)
    bonus = jnp.exp(boost_log_scale) * jnp.exp(lookup_matrix_output)
    over = 1.0 / (state_b + bonus)
    blended = (state_a + bonus * content_matrix_output) * over
    recept_sig = jax.nn.sigmoid(recept_proj)
    recept_grad = (mixed_grad * blended * recept_sig * (1.0 - recept_sig)).astype(jnp.bfloat16)
    alpha = mixed_grad * recept_sig * over * jnp.exp(-place * fading_rate_vector)
    local = (jnp.sum(alpha, axis=1), -jnp.sum(alpha * blended, axis=1))
    carry_p, carry_q = entering(piece_fall, local, True)
    z1 = over_z(stacked(back1.finish(), width))
    recept_send, recept_came = to_core(recept_in, recept_grad)
    g_out, g_recept, out_came, recept_came = after((branch_grad, recept_grad, out_came, recept_came), recept_send)
    part_out = both_cores(mixed_out, g_out, out_came)
    part_recept = both_cores(recept_in, g_recept, recept_came)
    way2 = Partial([grad_up_part, part_out, part_recept], True, deps=back1.came)
    carry_p, carry_q = after((carry_p, carry_q), way2.sent)
    key_grad, value_grad, grad_decay, boost_adjoint_term = wkv_backward(
        kvr,
        state_a,
        state_b,
        mixed_grad,
        carry_p,
        carry_q,
        boost_log_scale,
        fading_rate_vector,
    )
    key_send, key_came = to_core(key_in, key_grad)
    value_send, value_came = to_core(value_in, value_grad)
    late = (key_grad, value_grad, key_came, value_came)
    back2 = Partial(way2.finish(deps=(key_send, value_send)), False)
    k_grad, v_grad, key_came, value_came = after(late, back2.sent)
    part_key = both_cores(key_in, k_grad, key_came)
    part_value = both_cores(value_in, v_grad, value_came)
    way3 = Partial([part_key, part_value], True)
    z2 = over_z(stacked(back2.finish(deps=way3.sent), width))
    flat = (seq_count * piece_len, channels)
    grads = [g.reshape(flat) for g in after((k_grad, v_grad, recept_grad), (back2.came, way3.sent))]
    gap_one = (normed - before).reshape(flat)
    mixes = jnp.stack([key_mix, value_mix, recept_mix])
    now_part, next_part, grad_mixes = input_gradients(grads, gap_one, mixes, first_mats)
    back3 = Partial(way3.finish(), False)
    now_part, next_part = after((now_part, next_part), back3.sent)
    normed_grad = now_part.reshape(tokens.shape) + next_rows(next_part.reshape(tokens.shape))
    grad_key_mix, grad_value_mix, grad_recept_mix = grad_mixes
    grad_gain_one = jnp.sum(normed_grad * normed_one, axis=(0, 1))
    grad_bias_one = jnp.sum(normed_grad, axis=(0, 1))
    tokens_grad = residual_grad + norm_back(normed_grad * norm_gain, normed_one, inverse_one)
    sums = jnp.concatenate(
        [
            grad_gain_one,
            grad_bias_one,
            grad_key_mix,
            grad_value_mix,
            grad_recept_mix,
            grad_decay,
            boost_adjoint_term,
            grad_gain_two,
            grad_bias_two,
            grad_chan_key,
            grad_chan_recept,
        ]
    )
    for axis in ("core", "x", "y", "z"):
        sums = sums + sum(spread(sums, axis))
    sums = lax.dynamic_slice_in_dim(sums.reshape(n_vec, channels), lax.axis_index(ALL) * mine, mine, 1)
    z3 = over_z_direct(stacked(back3.finish(), width))
    first, second, third = (to_owner(z) for z in (z1, z2, z3))

    def rows_of(pair, at, rows=mine, columns=1):
        cut = [h[at + j * rows : at + (j + 1) * rows] for h in pair for j in range(columns)]
        return jnp.concatenate(cut, axis=1).astype(jnp.float32)

    return (
        output,
        tokens_grad,
        *(sums[j] for j in range(7)),
        rows_of(third, 0),
        rows_of(third, mine),
        rows_of(second, (blocks + 1) * mine),
        rows_of(second, blocks * mine),
        *(sums[j] for j in range(7, n_vec)),
        rows_of(second, 0, columns=blocks),
        rows_of(first, hidden // count),
        rows_of(first, 0, hidden // count),
    )


def solution(mesh):
    seq, dp = (mesh.shape["seq"], mesh.shape["dp"])
    wide = len({device.coords[0] for device in mesh.devices.reshape(-1)})
    fine = jax.sharding.Mesh(mesh.devices.reshape(seq // 2, 2, dp // wide, wide), ALL)
    field, vector, matrix = (P(DP, SEQ, None), P(ALL), P(ALL, None))
    return jax.shard_map(
        per_device,
        mesh=fine,
        in_specs=(field, P(DP), field) + (vector,) * 7 + (matrix,) * 4 + (vector,) * 4 + (matrix,) * 3,
        out_specs=(field, field) + (vector,) * 7 + (matrix,) * 4 + (vector,) * 4 + (matrix,) * 3,
        check_vma=False,
    )
```

```python
import functools

import jax
import jax.numpy as jnp
from jax import lax
from jax.experimental import pallas as pl
from jax.experimental.pallas import tpu as pltpu
from jax.sharding import PartitionSpec as P

EPS = 1e-05

def norm_stats(field):
    center = field - jnp.mean(field, axis=-1, keepdims=True)
    inverse = lax.rsqrt(jnp.mean(center * center, axis=-1, keepdims=True) + EPS)
    return (center * inverse, inverse)


def norm_back(grad_normed, normalized, inverse):
    mean_grad = jnp.mean(grad_normed, axis=-1, keepdims=True)
    mean_proj = jnp.mean(grad_normed * normalized, axis=-1, keepdims=True)
    return inverse * (grad_normed - mean_grad - normalized * mean_proj)


SEQ = ("y", "core")
DP = ("z", "x")
ALL = ("y", "core", "z", "x")


def scan_tiles(rate, reverse):
    row = lax.broadcasted_iota(jnp.int32, (8, rate.shape[-1]), 0)
    steps = []
    for distance in (1, 2, 4):
        inside = row < 8 - distance if reverse else row >= distance
        steps.append((distance, jnp.where(inside, jnp.exp(-float(distance) * rate), 0.0)))
    return row, steps


def turn(x, distance, reverse):
    return pltpu.roll(x, 8 - distance if reverse else distance, 0)


def scan_rows(x, steps, reverse):
    for distance, factor in steps:
        x = x + factor * turn(x, distance, reverse)
    return x


def wkv_kernel(k_ref, v_ref, r_ref, a0_ref, b0_ref, u_ref, rate_ref, a_ref, b_ref, mixed_ref):
    seqs, span, lanes = k_ref.shape
    rate = rate_ref[...]
    boost = jnp.exp(u_ref[...])
    row, steps = scan_tiles(rate, False)
    falling = jnp.exp(-row.astype(jnp.float32) * rate)
    fall_all = jnp.exp(-8.0 * rate)
    first = row < 1
    pair = 16

    def body(i, carry):
        at = pl.ds(pl.multiple_of(i * pair, pair), pair)
        new = []
        for n in range(seqs):
            k16, v16, r16 = (ref[n, at, :] for ref in (k_ref, v_ref, r_ref))
            state = carry[2 * n : 2 * n + 2]
            tiles = []
            for g in range(2):
                k, v, r = (t[g * 8 : g * 8 + 8] for t in (k16, v16, r16))
                weight = jnp.exp(k)
                bonus = boost * weight
                sums = [scan_rows(t, steps, False) for t in (weight * v, weight)]
                a, b = (
                    falling * c + jnp.where(first, 0.0, turn(t, 1, False))
                    for c, t in zip(state, sums)
                )
                state = tuple(fall_all * c + t[7:8] for c, t in zip(state, sums))
                mixed = jax.nn.sigmoid(r) * ((a + bonus * v) / (b + bonus))
                tiles.append((a, b, mixed))
            a, b, mixed = (jnp.concatenate(t, axis=0) for t in zip(*tiles))
            a_ref[n, at, :] = a
            b_ref[n, at, :] = b
            mixed_ref[n, at, :] = mixed.astype(mixed_ref.dtype)
            new += state
        return tuple(new)

    start = []
    for n in range(seqs):
        start += [a0_ref[n : n + 1, :], b0_ref[n : n + 1, :]]
    lax.fori_loop(0, span // pair, body, tuple(start), unroll=2)


def wkv_back_kernel(
    k_ref, v_ref, r_ref, a_ref, b_ref, g_ref, p0_ref, q0_ref, u_ref, rate_ref,
    k_out, v_out, rate_out, first_out,
):
    seqs, span, lanes = k_ref.shape
    rate = rate_ref[...]
    boost = jnp.exp(u_ref[...])
    row, steps = scan_tiles(rate, True)
    falling = jnp.exp((row.astype(jnp.float32) - 7.0) * rate)
    fall_all = jnp.exp(-8.0 * rate)
    last = row > 6
    pair = 16
    count = span // pair

    def body(i, carry):
        at = pl.ds(pl.multiple_of((count - 1 - i) * pair, pair), pair)
        new = []
        rate_sum, first_sum = carry[-2:]
        for n in range(seqs):
            loaded = [ref[n, at, :] for ref in (k_ref, v_ref, r_ref, a_ref, b_ref, g_ref)]
            state = carry[2 * n : 2 * n + 2]
            tiles = []
            for g in (1, 0):
                k, v, r, a, b, grad = (t[g * 8 : g * 8 + 8] for t in loaded)
                weight = jnp.exp(k)
                bonus = boost * weight
                over = 1.0 / (b + bonus)
                wkv = (a + bonus * v) * over
                alpha = grad * jax.nn.sigmoid(r) * over
                sums = [scan_rows(t, steps, True) for t in (alpha, -alpha * wkv)]
                p, q = (
                    falling * c + jnp.where(last, 0.0, turn(t, 1, True))
                    for c, t in zip(state, sums)
                )
                state = tuple(fall_all * c + t[0:1] for c, t in zip(state, sums))
                share = alpha * bonus
                own = share * (v - wkv)
                tiles.append((own + weight * (p * v + q), share + weight * p))
                rate_sum = rate_sum + (a * p + b * q)
                first_sum = first_sum + own
            k_grad, v_grad = (jnp.concatenate(t, axis=0) for t in zip(*tiles[::-1]))
            k_out[n, at, :] = k_grad.astype(k_out.dtype)
            v_out[n, at, :] = v_grad.astype(v_out.dtype)
            new += state
        return tuple(new) + (rate_sum, first_sum)

    start = []
    for n in range(seqs):
        start += [p0_ref[n : n + 1, :], q0_ref[n : n + 1, :]]
    zero = jnp.zeros((8, lanes), jnp.float32)
    done = lax.fori_loop(0, count, body, tuple(start) + (zero, zero), unroll=2)
    rate_out[...] = -rate * jnp.exp(-rate) * jnp.sum(done[-2], axis=0, keepdims=True)
    first_out[...] = jnp.sum(done[-1], axis=0, keepdims=True)


def first_kernel(flag_ref, tok_ref, prev_ref, vec_ref, w_ref, x0_ref, x1_ref, x2_ref, y_ref, local_ref, normed, before, key):
    seqs, span, channels = tok_ref.shape
    j = pl.program_id(0)

    @pl.when(j == 0)
    def _():
        gain, bias = (vec_ref[0:1, :], vec_ref[1:2, :])
        for n in range(seqs):
            rows = pl.ds(n * span, span)
            field = norm_stats(tok_ref[n].astype(jnp.float32))[0] * gain + bias
            edge = norm_stats(prev_ref[n : n + 1, :].astype(jnp.float32))[0] * gain + bias
            edge = jnp.where(flag_ref[0] > 0, edge, 0.0)
            row = lax.broadcasted_iota(jnp.int32, field.shape, 0)
            normed[rows, :] = field
            before[rows, :] = jnp.where(row < 1, edge, pltpu.roll(field, 1, 0))

    mix = vec_ref[pl.ds(2 + j, 1), :]
    x = (normed[...] * mix + before[...] * (1.0 - mix)).astype(jnp.bfloat16)
    y = jnp.dot(x, w_ref[0], preferred_element_type=jnp.float32)
    y_ref[0] = y.reshape(seqs, span, channels)
    for k, ref in enumerate((x0_ref, x1_ref, x2_ref)):

        @pl.when(j == k)
        def _(ref=ref):
            ref[...] = x.reshape(seqs, span, channels)

    @pl.when(j == 0)
    def _():
        key[...] = y

    @pl.when(j == 1)
    def _():
        rate = vec_ref[5:6, :]
        place = lax.broadcasted_iota(jnp.int32, (span, channels), 0).astype(jnp.float32)
        fall = (place - (span - 1.0)) * rate
        for n in range(seqs):
            rows = slice(n * span, (n + 1) * span)
            weight = jnp.exp(key[rows, :] + fall)
            local_ref[0, n : n + 1, :] = jnp.sum(weight * y[rows], axis=0, keepdims=True)
            local_ref[1, n : n + 1, :] = jnp.sum(weight, axis=0, keepdims=True)


def first_projections(flag, tokens, prev, vectors, mats):
    seqs, span, channels = tokens.shape
    fixed = lambda *shape: pl.BlockSpec(shape, lambda j: (0,) * len(shape))
    rows = (seqs * span, channels)
    outs = pl.pallas_call(
        first_kernel,
        grid=(3,),
        out_shape=[jax.ShapeDtypeStruct(tokens.shape, jnp.bfloat16)] * 3
        + [jax.ShapeDtypeStruct((3, *tokens.shape), jnp.float32)]
        + [jax.ShapeDtypeStruct((2, seqs, channels), jnp.float32)],
        in_specs=[
            pl.BlockSpec(memory_space=pltpu.SMEM),
            fixed(*tokens.shape),
            fixed(*prev.shape),
            fixed(*vectors.shape),
            pl.BlockSpec((1, channels, channels), lambda j: (j, 0, 0)),
        ],
        out_specs=[fixed(*tokens.shape)] * 3
        + [pl.BlockSpec((1, *tokens.shape), lambda j: (j, 0, 0, 0)), fixed(2, seqs, channels)],
        scratch_shapes=[pltpu.VMEM(rows, jnp.float32)] * 3,
        compiler_params=pltpu.CompilerParams(vmem_limit_bytes=48 << 20),
        cost_estimate=pl.CostEstimate(flops=1 << 20, bytes_accessed=1 << 16, transcendentals=0),
    )(flag, tokens, prev, vectors, mats)
    return outs[:3], outs[3], outs[4]


def ffn_back_kernel(grad_ref, relu_ref, down_ref, up_ref, up_grad_ref, out_ref):
    wide = (((1,), (1,)), ((), ()))
    squared = lax.dot_general(grad_ref[...], down_ref[...], wide, preferred_element_type=jnp.float32)
    up_grad = (squared * (2.0 * relu_ref[...].astype(jnp.float32))).astype(jnp.bfloat16)
    up_grad_ref[...] = up_grad
    part = lax.dot_general(up_grad, up_ref[...], wide, preferred_element_type=jnp.float32)

    @pl.when(pl.program_id(0) == 0)
    def _():
        out_ref[...] = part

    @pl.when(pl.program_id(0) > 0)
    def _():
        out_ref[...] += part


def ffn_backward(grad, relu_up, down, up):
    rows, channels = grad.shape
    hidden = up.shape[1]
    block = 512
    column = pl.BlockSpec((rows, block), lambda j: (0, j))
    return pl.pallas_call(
        ffn_back_kernel,
        grid=(hidden // block,),
        out_shape=[
            jax.ShapeDtypeStruct((rows, hidden), jnp.bfloat16),
            jax.ShapeDtypeStruct((rows, channels), jnp.float32),
        ],
        in_specs=[
            pl.BlockSpec((rows, channels), lambda j: (0, 0)),
            column,
            pl.BlockSpec((block, channels), lambda j: (j, 0)),
            pl.BlockSpec((channels, block), lambda j: (0, j)),
        ],
        out_specs=[column, pl.BlockSpec((rows, channels), lambda j: (0, 0))],
        compiler_params=pltpu.CompilerParams(vmem_limit_bytes=40 << 20),
        cost_estimate=pl.CostEstimate(
            flops=1 << 20, bytes_accessed=24 << 20, transcendentals=0
        ),
    )(grad, relu_up, down, up)


def in_grads_kernel(k_ref, v_ref, r_ref, gap_ref, mix_ref, w_ref, now_ref, next_ref, sum_ref):
    j = pl.program_id(0)
    grad = jnp.where(j == 0, k_ref[...], jnp.where(j == 1, v_ref[...], r_ref[...]))
    wide = (((1,), (1,)), ((), ()))
    part = lax.dot_general(grad, w_ref[0], wide, preferred_element_type=jnp.float32)
    mix = mix_ref[pl.ds(j, 1), :]
    now = part * mix
    sum_ref[pl.ds(j, 1), :] = jnp.sum(part * gap_ref[...], axis=0, keepdims=True)

    @pl.when(j == 0)
    def _():
        now_ref[...] = now
        next_ref[...] = part - now

    @pl.when(j > 0)
    def _():
        now_ref[...] += now
        next_ref[...] += part - now


def input_gradients(grads, gap, mixes, mats):
    rows, channels = gap.shape
    fixed = lambda *shape: pl.BlockSpec(shape, lambda j: (0,) * len(shape))
    return pl.pallas_call(
        in_grads_kernel,
        grid=(3,),
        out_shape=[jax.ShapeDtypeStruct(gap.shape, jnp.float32)] * 2
        + [jax.ShapeDtypeStruct((3, channels), jnp.float32)],
        in_specs=[fixed(rows, channels)] * 4
        + [fixed(3, channels), pl.BlockSpec((1, channels, channels), lambda j: (j, 0, 0))],
        out_specs=[fixed(rows, channels)] * 2 + [fixed(3, channels)],
        compiler_params=pltpu.CompilerParams(vmem_limit_bytes=40 << 20),
        cost_estimate=pl.CostEstimate(flops=1 << 20, bytes_accessed=8 << 20, transcendentals=0),
    )(*grads, gap, mixes, mats)


LANES = 256


def wkv_specs(seqs, span):
    field = pl.BlockSpec((seqs, span, LANES), lambda j: (0, 0, j))
    state = pl.BlockSpec((seqs, LANES), lambda j: (0, j))
    vector = pl.BlockSpec((1, LANES), lambda j: (0, j))
    return field, state, vector


def stacked_specs(seqs, span):
    shape = (None, seqs, span, LANES)
    return [pl.BlockSpec(shape, lambda j, n=n: (n, 0, 0, j)) for n in range(3)]


def wkv_forward(kvr, a0, b0, u, rate):
    shape = kvr.shape[1:]
    _, span, channels = shape
    seqs = shape[0]
    field, state, vector = wkv_specs(seqs, span)
    return pl.pallas_call(
        wkv_kernel,
        grid=(channels // LANES,),
        out_shape=[jax.ShapeDtypeStruct(shape, t) for t in (jnp.float32, jnp.float32, jnp.bfloat16)],
        in_specs=stacked_specs(seqs, span) + [state] * 2 + [vector] * 2,
        out_specs=[field] * 3,
        compiler_params=pltpu.CompilerParams(vmem_limit_bytes=32 << 20),
        cost_estimate=pl.CostEstimate(flops=1 << 20, bytes_accessed=1 << 16, transcendentals=0),
    )(kvr, kvr, kvr, a0, b0, u[None], rate[None])


def wkv_backward(kvr, a, b, grad, p0, q0, u, rate):
    seqs, span, channels = a.shape
    field, state, vector = wkv_specs(seqs, span)
    k_grad, v_grad, decay_grad, first_grad = pl.pallas_call(
        wkv_back_kernel,
        grid=(channels // LANES,),
        out_shape=[jax.ShapeDtypeStruct(a.shape, jnp.bfloat16)] * 2
        + [jax.ShapeDtypeStruct((1, channels), jnp.float32)] * 2,
        in_specs=stacked_specs(seqs, span) + [field] * 3 + [state] * 2 + [vector] * 2,
        out_specs=[field] * 2 + [vector] * 2,
        compiler_params=pltpu.CompilerParams(vmem_limit_bytes=32 << 20),
        cost_estimate=pl.CostEstimate(flops=1 << 20, bytes_accessed=1 << 16, transcendentals=0),
    )(kvr, kvr, kvr, a, b, grad, p0, q0, u[None], rate[None])
    return k_grad, v_grad, decay_grad[0], first_grad[0]


def matmul(form, left, right):
    return jnp.einsum(form, left, right, preferred_element_type=jnp.float32)


def shifted(block, axis, distance):
    count = lax.axis_size(axis)
    route = [(i - distance, i) for i in range(count) if 0 <= i - distance < count]
    return lax.ppermute(block, axis, route)


def previous_rows(field):
    came = shifted(field[:, -1, :], SEQ, 1)
    return jnp.concatenate([came[:, None, :], field[:, :-1, :]], axis=1)


def next_rows(field):
    came = shifted(field[:, 0, :], SEQ, -1)
    return jnp.concatenate([field[:, 1:, :], came[:, None, :]], axis=1)


def entering(factor, states, reverse):
    block = jnp.stack(states)
    low, high = in_order(block, spread(block, "core")[0])
    near, far = (high, low) if reverse else (low, high)
    chip = factor * near + far
    total, power = (jnp.zeros_like(block), jnp.ones_like(factor))
    for k in range(1, lax.axis_size("y")):
        total = total + power * shifted(chip, "y", -k if reverse else k)
        power = power * factor * factor
    core = lax.axis_index("core")
    total = jnp.where(core == (1 if reverse else 0), total, factor * total + near)
    return (total[0], total[1])


def in_order(own, other):
    core = lax.axis_index("core")
    return (jnp.where(core == 0, own, other), jnp.where(core == 0, other, own))


def own_half(x, own=True):
    half = x.shape[-1] // 2
    core = lax.axis_index("core")
    return jnp.where((core == 0) == own, x[..., :half], x[..., half:])


def after(x, deps):
    return lax.optimization_barrier((x, deps))[0] if jax.tree.leaves(deps) else x


def spread(block, axis):
    count = lax.axis_size(axis)
    return [
        lax.ppermute(block, axis, [(i, (i + k) % count) for i in range(count)])
        for k in range(1, count)
    ]


def cross(block, first, k):
    ys, cs, zs, xs = (lax.axis_size(axis) for axis in ALL)
    route = []
    for i in range(ys * cs * zs * xs):
        y, c, z, x = (i // (cs * zs * xs), i // (zs * xs) % cs, i // xs % zs, i % xs)
        if (c == 0) == first:
            x = (x + k) % xs
        else:
            y = (y + k) % ys
        route.append((i, ((y * cs + c) * zs + z) * xs + x))
    return lax.ppermute(block, ALL, route)


def beside_z(own):
    half = own.shape[1] // 2
    rows = lax.all_gather(own, "z", axis=0)
    return (rows[:, :, :half], rows[:, :, half:])


def beside_xy(pair, axes):
    return [[block] + spread(block, axis) for block, axis in zip(pair, axes)]


def other_core(parts):
    return [[spread(block, "core")[0] for block in part] for part in parts]


def assemble_kernel(entries, grid, at_ref, *refs):
    n_out = 1 + max(entry[2] for entry in entries)
    sources, outs, sems = (refs[: -n_out - 1], refs[-n_out - 1 : -1], refs[-1])
    ys, cs, zs, xs = grid
    y, c, x = (at_ref[j] for j in range(3))

    def back(at, k, count):
        return lax.rem(at - k + count, count)

    index = 0
    for dc in range(cs):
        for half, lead in enumerate((xs, ys)):
            for far in range(ys if half == 0 else xs):
                source = sources[index]
                index += 1

                def copy(k, _, source=source, dc=dc, half=half, far=far):
                    near, dz = (k // zs, lax.rem(k, zs))
                    dy, dx = (far, near) if half == 0 else (near, far)
                    block = back(y, dy, ys) * cs + back(c, dc, cs)
                    block = (block * zs + dz) * xs + back(x, dx, xs)
                    for first, rows, out, column, lead_at in entries:
                        width = source.shape[-1]
                        pltpu.make_async_copy(
                            source.at[near, dz, pl.ds(first, rows), :],
                            outs[out].at[lead_at, block, :, pl.ds(column + half * width, width)],
                            sems.at[out],
                        ).start()
                    return 0

                lax.fori_loop(0, lead * zs, copy, 0)
    for out in range(n_out):
        pltpu.make_async_copy(outs[out], outs[out], sems.at[out]).wait()


def assemble(mine, other, entries, shapes, grid):
    sources = [b for part in mine for b in part] + [b for part in other for b in part]
    at = jnp.stack([lax.axis_index(axis) for axis in ("y", "core", "x")]).astype(jnp.int32)
    count = grid[0] * grid[1] * grid[2] * grid[3]
    outs = pl.pallas_call(
        functools.partial(assemble_kernel, entries, grid),
        out_shape=[jax.ShapeDtypeStruct((n, count, *shape), jnp.bfloat16) for n, *shape in shapes],
        in_specs=[pl.BlockSpec(memory_space=pltpu.SMEM)]
        + [pl.BlockSpec(memory_space=pl.ANY)] * len(sources),
        out_specs=[pl.BlockSpec(memory_space=pltpu.VMEM)] * len(shapes),
        scratch_shapes=[pltpu.SemaphoreType.DMA((len(shapes),))],
        compiler_params=pltpu.CompilerParams(vmem_limit_bytes=40 << 20),
    )(at, *sources)
    return [out.reshape(out.shape[0], -1, out.shape[-1]) for out in outs]


class Partial:
    def __init__(self, parts, first, deps=()):
        self.parts, self.first = (parts, first)
        self.sent, self.came = ([], [])
        for k in range(1, lax.axis_size("x")):
            blocks = [after(self.take(p, k), deps) for p in parts]
            self.sent += blocks
            self.came.append([cross(block, first, k) for block in blocks])

    def take(self, p, k):
        count = lax.axis_size("x")
        x, y = (lax.rem(lax.axis_index(axis) + k, count) for axis in ("x", "y"))
        core = lax.axis_index("core")
        if self.first:
            by_x = lax.dynamic_index_in_dim(p, x, 3, keepdims=False).transpose(2, 1, 0, 3, 4)
            by_y = lax.dynamic_index_in_dim(p, y, 0, keepdims=False).transpose(1, 0, 2, 3, 4)
            return jnp.where(core == 0, by_x, by_y)
        return lax.dynamic_index_in_dim(p, jnp.where(core == 0, y, x), 2, keepdims=False)

    def finish(self, deps=()):
        totals = [self.take(p, 0).astype(jnp.float32) for p in self.parts]
        for blocks in after(self.came, deps):
            totals = [total + block.astype(jnp.float32) for total, block in zip(totals, blocks)]
        return [total.astype(jnp.bfloat16) for total in totals]


def stacked(parts, width):
    cut = [p[..., j : j + width] for p in parts for j in range(0, p.shape[-1], width)]
    return jnp.concatenate(cut, axis=2)


def over_z_direct(total):
    count, at = (lax.axis_size("z"), lax.axis_index("z"))
    block = lambda k: lax.dynamic_index_in_dim(total, lax.rem(at + k, count), 0, keepdims=False)
    out = block(0).astype(jnp.float32)
    for k in range(1, count):
        route = [(i, (i + k) % count) for i in range(count)]
        out = out + lax.ppermute(block(k), "z", route).astype(jnp.float32)
    return out.astype(jnp.bfloat16)


def over_z(total):
    zs, cores, rows, columns = total.shape
    flat = total.reshape(zs * cores * rows, columns)
    return lax.psum_scatter(flat, "z", scatter_dimension=0, tiled=True).reshape(cores, rows, columns)


def to_owner(total):
    core = lax.axis_index("core")
    came = spread(lax.dynamic_index_in_dim(total, 1 - core, 0, keepdims=False), "core")[0]
    return in_order(lax.dynamic_index_in_dim(total, core, 0, keepdims=False), came)


def per_device(
    tokens,
    lengths,
    cotangent,
    first_gain,
    first_bias,
    mix_key,
    mix_value,
    mix_recept,
    time_decay,
    time_first,
    key_weight,
    value_weight,
    recept_weight,
    output_weight,
    second_gain,
    second_bias,
    shift_key,
    shift_recept,
    up_weight,
    gate_weight,
    down_weight,
):
    grid = tuple(lax.axis_size(axis) for axis in ALL)
    count = grid[0] * grid[1] * grid[2] * grid[3]
    seq_count, piece_len, channels = tokens.shape
    hidden = up_weight.shape[1]
    mine = channels // count
    blocks = hidden // channels

    vectors = (
        first_gain,
        first_bias,
        mix_key,
        mix_value,
        mix_recept,
        time_decay,
        time_first,
        second_gain,
        second_bias,
        shift_key,
        shift_recept,
    )
    n_vec = len(vectors)
    packed = jnp.pad(jnp.stack(vectors), ((0, 16 - n_vec), (0, channels - mine)))
    pieces = (
        [key_weight, value_weight, recept_weight, packed],
        [output_weight] + [up_weight[:, j * channels : (j + 1) * channels] for j in range(blocks)],
        [gate_weight, down_weight],
    )
    places = (
        [(0, 0, 0), (0, 0, 1), (0, 0, 2), (1, 0, 0)],
        [(0, 0, 0)] + [(1, j * channels, 0) for j in range(blocks)],
        [(0, 0, 0), (1, 0, 0)],
    )
    chunks = [jnp.concatenate(piece) for piece in pieces]
    plans = []
    for piece, place in zip(pieces, places):
        first, entries, shapes = (0, [], {})
        for part, (out, column, lead) in zip(piece, place):
            entries.append((first, part.shape[0], out, column, lead))
            shapes[out] = (lead + 1, part.shape[0], column + channels)
            first += part.shape[0]
        plans.append((entries, [shapes[o] for o in sorted(shapes)]))
    stepwise = mine % 16 == 0

    def whole(at):
        gathered = lax.all_gather(chunks[at], ALL, axis=0)
        entries, shapes = plans[at]
        outs = []
        for out, (leads, _, columns) in enumerate(shapes):
            parts = [gathered[:, f : f + r] for f, r, o, _, _ in entries if o == out]
            if leads == 1:
                parts = [jnp.concatenate(parts, axis=-1)]
            outs.append(jnp.stack([p.reshape(-1, columns) for p in parts]))
        return outs

    if stepwise:
        half = channels // 2
        xy2 = beside_xy((chunks[2][:, :half], chunks[2][:, half:]), ("x", "y"))
        z0 = beside_z(chunks[0])
        z1 = beside_z(after(chunks[1], z0))
        z2 = [lax.all_gather(jnp.stack(part), "z", axis=1) for part in after(xy2, z0)]
        xy0 = beside_xy(after(z0, xy2), ("x", "y"))
        yx0 = beside_xy([jnp.stack(part) for part in xy0], ("y", "x"))
        xy1 = beside_xy(after(z1, yx0), ("x", "y"))
        first_mats, vecs = assemble(yx0, other_core(yx0), *plans[0], grid)
    else:
        first_mats, vecs = whole(0)
    vecs = vecs.reshape(count, 16, channels)[:, :n_vec, :mine]
    vecs = jnp.moveaxis(vecs, 1, 0).reshape(n_vec, channels).astype(jnp.float32)
    (
        norm_gain,
        norm_bias,
        key_mix,
        value_mix,
        recept_mix,
        decay_log,
        boost_log_scale,
        gain_two,
        bias_two,
        chan_key_mix,
        chan_recept_mix,
    ) = (vecs[j] for j in range(n_vec))
    seq_index = lax.axis_index(SEQ)
    positions = seq_index * piece_len + jnp.arange(piece_len, dtype=jnp.int32)
    live_mask = (positions[None, :] < lengths[:, None]).astype(jnp.float32)[:, :, None]
    field = tokens.astype(jnp.float32)
    normed_one, inverse_one = norm_stats(field)
    normed = normed_one * norm_gain + norm_bias
    before = previous_rows(normed)
    fading_rate_vector = jnp.exp(decay_log)
    place = jnp.arange(piece_len, dtype=jnp.float32)[:, None]
    piece_fall = jnp.exp(-piece_len * fading_rate_vector)
    rows = jnp.stack([norm_gain, norm_bias, key_mix, value_mix, recept_mix, fading_rate_vector])
    ins, kvr, local = first_projections(
        (seq_index > 0).astype(jnp.int32)[None], tokens, shifted(tokens[:, -1, :], SEQ, 1), rows, first_mats
    )
    if stepwise:
        pair = [jnp.stack(part) for part in after(xy1, (ins, local))]
        local = after(local, pair)
        yx1 = beside_xy(pair, ("y", "x"))
        core1 = other_core([[part[0]] for part in yx1])
    key_in, value_in, recept_in = ins
    lookup_matrix_output, content_matrix_output, recept_proj = kvr
    local = (local[0], local[1])
    starting_accumulator, starting_normalizer = entering(piece_fall, local, False)
    if stepwise:
        starting_accumulator, starting_normalizer = after(
            (starting_accumulator, starting_normalizer), (yx1, core1, z2)
        )
    state_a, state_b, mixed_out = wkv_forward(
        kvr,
        starting_accumulator,
        starting_normalizer,
        boost_log_scale,
        fading_rate_vector,
    )
    if stepwise:
        yx2 = beside_xy(after(tuple(z2), yx1), ("y", "x"))
        rest1 = other_core([part[1:] for part in yx1])
        core1 = [one + rest for one, rest in zip(core1, rest1)]
        yx1 = after(yx1, (state_a, state_b))
        (output_mat,), (up_mat,) = assemble(yx1, core1, *plans[1], grid)
    else:
        (output_mat,), (up_mat,) = whole(1)
    branch = matmul("nlc,cd->nld", mixed_out, output_mat)
    residual = field + branch
    normed_two_raw, inverse_two = norm_stats(residual)
    normed_two = normed_two_raw * gain_two + bias_two
    before_two = previous_rows(normed_two)
    ffn_key = (normed_two * chan_key_mix + before_two * (1.0 - chan_key_mix)).astype(jnp.bfloat16)
    ffn_recept = (normed_two * chan_recept_mix + before_two * (1.0 - chan_recept_mix)).astype(
        jnp.bfloat16
    )
    up_proj = matmul("nlc,cf->nlf", ffn_key, up_mat)
    relu_up = jax.nn.relu(up_proj)
    squared = jnp.square(relu_up).astype(jnp.bfloat16)
    relu_up = relu_up.astype(jnp.bfloat16)
    if stepwise:
        core2 = other_core([[part] for part in after(tuple(z2), (ffn_key, ffn_recept))])
        yx2 = after(yx2, (squared, relu_up, core2))
        rest2 = other_core([part[1:] for part in yx2])
        core2 = [one + rest for one, rest in zip(core2, rest2)]
        (gate_mat,), (down_mat,) = assemble(yx2, core2, *plans[2], grid)
    else:
        (gate_mat,), (down_mat,) = whole(2)
    down_proj = matmul("nlf,fd->nld", squared, down_mat)
    gate_value = jax.nn.sigmoid(matmul("nlc,cd->nld", ffn_recept, gate_mat))
    output = ((residual + gate_value * down_proj) * live_mask).astype(jnp.bfloat16)

    def outer(left, right):
        return jnp.einsum("nlc,nld->cd", left, right, preferred_element_type=jnp.float32)

    def to_core(left, right):
        send = outer(left, own_half(right, False)).astype(jnp.bfloat16)
        return send, spread(send, "core")[0]

    def both_cores(left, right, came):
        rows = outer(left, own_half(right)) + came.astype(jnp.float32)
        return rows.astype(jnp.bfloat16).reshape(*grid, -1, rows.shape[-1])

    seed = cotangent.astype(jnp.float32) * live_mask
    down_grad = (seed * gate_value).astype(jnp.bfloat16)
    gate_grad = (seed * down_proj * gate_value * (1.0 - gate_value)).astype(jnp.bfloat16)
    width = channels // 2
    down_send, down_came = to_core(squared, down_grad)
    gate_send, gate_came = to_core(ffn_recept, gate_grad)
    ffn_recept_grad = matmul("nld,cd->nlc", after(gate_grad, (down_send, gate_send)), gate_mat)
    late = (down_grad, gate_grad, down_came, gate_came)
    d_grad, g_grad, down_came, gate_came = after(late, ffn_recept_grad)
    way1 = Partial([both_cores(squared, d_grad, down_came), both_cores(ffn_recept, g_grad, gate_came)], True)
    flat = (seq_count * piece_len, -1)
    up_grad, ffn_key_grad = ffn_backward(
        after(down_grad, way1.sent).reshape(flat), relu_up.reshape(flat), down_mat, up_mat
    )
    up_grad = up_grad.reshape(seq_count, piece_len, hidden)
    ffn_key_grad = ffn_key_grad.reshape(tokens.shape)
    up_send, up_came = to_core(ffn_key, up_grad)
    u_grad, up_came = after((up_grad, up_came), up_send)
    grad_up_part = both_cores(ffn_key, u_grad, up_came)
    normed_two_grad = (
        ffn_key_grad * chan_key_mix
        + ffn_recept_grad * chan_recept_mix
        + next_rows(ffn_key_grad * (1.0 - chan_key_mix) + ffn_recept_grad * (1.0 - chan_recept_mix))
    )
    gap_two = normed_two - before_two
    grad_chan_key = jnp.sum(ffn_key_grad * gap_two, axis=(0, 1))
    grad_chan_recept = jnp.sum(ffn_recept_grad * gap_two, axis=(0, 1))
    grad_gain_two = jnp.sum(normed_two_grad * normed_two_raw, axis=(0, 1))
    grad_bias_two = jnp.sum(normed_two_grad, axis=(0, 1))
    residual_grad = seed + norm_back(normed_two_grad * gain_two, normed_two_raw, inverse_two)
    branch_grad = residual_grad.astype(jnp.bfloat16)
    back1 = Partial(way1.finish(deps=(branch_grad,)), False)
    branch_grad = after(branch_grad, back1.sent)
    mixed_grad = matmul("nld,cd->nlc", branch_grad, output_mat)
    out_send, out_came = to_core(mixed_out, branch_grad)
    bonus = jnp.exp(boost_log_scale) * jnp.exp(lookup_matrix_output)
    over = 1.0 / (state_b + bonus)
    blended = (state_a + bonus * content_matrix_output) * over
    recept_sig = jax.nn.sigmoid(recept_proj)
    recept_grad = (mixed_grad * blended * recept_sig * (1.0 - recept_sig)).astype(jnp.bfloat16)
    alpha = mixed_grad * recept_sig * over * jnp.exp(-place * fading_rate_vector)
    local = (jnp.sum(alpha, axis=1), -jnp.sum(alpha * blended, axis=1))
    carry_p, carry_q = entering(piece_fall, local, True)
    z1 = over_z(stacked(back1.finish(), width))
    recept_send, recept_came = to_core(recept_in, recept_grad)
    g_out, g_recept, out_came, recept_came = after((branch_grad, recept_grad, out_came, recept_came), recept_send)
    part_out = both_cores(mixed_out, g_out, out_came)
    part_recept = both_cores(recept_in, g_recept, recept_came)
    way2 = Partial([grad_up_part, part_out, part_recept], True, deps=back1.came)
    carry_p, carry_q = after((carry_p, carry_q), way2.sent)
    key_grad, value_grad, grad_decay, boost_adjoint_term = wkv_backward(
        kvr,
        state_a,
        state_b,
        mixed_grad,
        carry_p,
        carry_q,
        boost_log_scale,
        fading_rate_vector,
    )
    key_send, key_came = to_core(key_in, key_grad)
    value_send, value_came = to_core(value_in, value_grad)
    late = (key_grad, value_grad, key_came, value_came)
    back2 = Partial(way2.finish(deps=(key_send, value_send)), False)
    k_grad, v_grad, key_came, value_came = after(late, back2.sent)
    part_key = both_cores(key_in, k_grad, key_came)
    part_value = both_cores(value_in, v_grad, value_came)
    way3 = Partial([part_key, part_value], True, deps=back2.came)
    z2 = over_z(stacked(back2.finish(deps=way3.sent), width))
    flat = (seq_count * piece_len, channels)
    grads = [g.reshape(flat) for g in after((k_grad, v_grad, recept_grad), (part_key, part_value))]
    gap_one = (normed - before).reshape(flat)
    mixes = jnp.stack([key_mix, value_mix, recept_mix])
    now_part, next_part, grad_mixes = input_gradients(grads, gap_one, mixes, first_mats)
    back3 = Partial(way3.finish(), False)
    now_part, next_part = after((now_part, next_part), way3.sent)
    normed_grad = now_part.reshape(tokens.shape) + next_rows(next_part.reshape(tokens.shape))
    grad_key_mix, grad_value_mix, grad_recept_mix = grad_mixes
    grad_gain_one = jnp.sum(normed_grad * normed_one, axis=(0, 1))
    grad_bias_one = jnp.sum(normed_grad, axis=(0, 1))
    tokens_grad = residual_grad + norm_back(normed_grad * norm_gain, normed_one, inverse_one)
    sums = jnp.concatenate(
        [
            grad_gain_one,
            grad_bias_one,
            grad_key_mix,
            grad_value_mix,
            grad_recept_mix,
            grad_decay,
            boost_adjoint_term,
            grad_gain_two,
            grad_bias_two,
            grad_chan_key,
            grad_chan_recept,
        ]
    )
    for axis in ("core", "x", "y", "z"):
        sums = sums + sum(spread(sums, axis))
    sums = lax.dynamic_slice_in_dim(sums.reshape(n_vec, channels), lax.axis_index(ALL) * mine, mine, 1)
    z3 = over_z_direct(stacked(back3.finish(), width))
    first, second, third = (to_owner(z) for z in (z1, z2, z3))

    def rows_of(pair, at, rows=mine, columns=1):
        cut = [h[at + j * rows : at + (j + 1) * rows] for h in pair for j in range(columns)]
        return jnp.concatenate(cut, axis=1).astype(jnp.float32)

    return (
        output,
        tokens_grad,
        *(sums[j] for j in range(7)),
        rows_of(third, 0),
        rows_of(third, mine),
        rows_of(second, (blocks + 1) * mine),
        rows_of(second, blocks * mine),
        *(sums[j] for j in range(7, n_vec)),
        rows_of(second, 0, columns=blocks),
        rows_of(first, hidden // count),
        rows_of(first, 0, hidden // count),
    )


def solution(mesh):
    seq, dp = (mesh.shape["seq"], mesh.shape["dp"])
    wide = len({device.coords[0] for device in mesh.devices.reshape(-1)})
    fine = jax.sharding.Mesh(mesh.devices.reshape(seq // 2, 2, dp // wide, wide), ALL)
    field, vector, matrix = (P(DP, SEQ, None), P(ALL), P(ALL, None))
    return jax.shard_map(
        per_device,
        mesh=fine,
        in_specs=(field, P(DP), field) + (vector,) * 7 + (matrix,) * 4 + (vector,) * 4 + (matrix,) * 3,
        out_specs=(field, field) + (vector,) * 7 + (matrix,) * 4 + (vector,) * 4 + (matrix,) * 3,
        check_vma=False,
    )
```

```python
import functools

import jax
import jax.numpy as jnp
from jax import lax
from jax.experimental import pallas as pl
from jax.experimental.pallas import tpu as pltpu
from jax.sharding import PartitionSpec as P

EPS = 1e-05

def norm_stats(field):
    center = field - jnp.mean(field, axis=-1, keepdims=True)
    inverse = lax.rsqrt(jnp.mean(center * center, axis=-1, keepdims=True) + EPS)
    return (center * inverse, inverse)


def norm_back(grad_normed, normalized, inverse):
    mean_grad = jnp.mean(grad_normed, axis=-1, keepdims=True)
    mean_proj = jnp.mean(grad_normed * normalized, axis=-1, keepdims=True)
    return inverse * (grad_normed - mean_grad - normalized * mean_proj)


SEQ = ("y", "core")
DP = ("z", "x")
ALL = ("y", "core", "z", "x")


def scan_tiles(rate, reverse):
    row = lax.broadcasted_iota(jnp.int32, (8, rate.shape[-1]), 0)
    steps = []
    for distance in (1, 2, 4):
        inside = row < 8 - distance if reverse else row >= distance
        steps.append((distance, jnp.where(inside, jnp.exp(-float(distance) * rate), 0.0)))
    return row, steps


def turn(x, distance, reverse):
    return pltpu.roll(x, 8 - distance if reverse else distance, 0)


def scan_rows(x, steps, reverse):
    for distance, factor in steps:
        x = x + factor * turn(x, distance, reverse)
    return x


def wkv_kernel(k_ref, v_ref, r_ref, a0_ref, b0_ref, u_ref, rate_ref, a_ref, b_ref, mixed_ref):
    seqs, span, lanes = k_ref.shape
    rate = rate_ref[...]
    boost = jnp.exp(u_ref[...])
    row, steps = scan_tiles(rate, False)
    falling = jnp.exp(-row.astype(jnp.float32) * rate)
    fall_all = jnp.exp(-8.0 * rate)
    first = row < 1
    pair = 16

    def body(i, carry):
        at = pl.ds(pl.multiple_of(i * pair, pair), pair)
        new = []
        for n in range(seqs):
            k16, v16, r16 = (ref[n, at, :] for ref in (k_ref, v_ref, r_ref))
            state = carry[2 * n : 2 * n + 2]
            tiles = []
            for g in range(2):
                k, v, r = (t[g * 8 : g * 8 + 8] for t in (k16, v16, r16))
                weight = jnp.exp(k)
                bonus = boost * weight
                sums = [scan_rows(t, steps, False) for t in (weight * v, weight)]
                a, b = (
                    falling * c + jnp.where(first, 0.0, turn(t, 1, False))
                    for c, t in zip(state, sums)
                )
                state = tuple(fall_all * c + t[7:8] for c, t in zip(state, sums))
                mixed = jax.nn.sigmoid(r) * ((a + bonus * v) / (b + bonus))
                tiles.append((a, b, mixed))
            a, b, mixed = (jnp.concatenate(t, axis=0) for t in zip(*tiles))
            a_ref[n, at, :] = a
            b_ref[n, at, :] = b
            mixed_ref[n, at, :] = mixed.astype(mixed_ref.dtype)
            new += state
        return tuple(new)

    start = []
    for n in range(seqs):
        start += [a0_ref[n : n + 1, :], b0_ref[n : n + 1, :]]
    lax.fori_loop(0, span // pair, body, tuple(start), unroll=2)


def wkv_back_kernel(
    k_ref, v_ref, r_ref, a_ref, b_ref, g_ref, p0_ref, q0_ref, u_ref, rate_ref,
    k_out, v_out, rate_out, first_out,
):
    seqs, span, lanes = k_ref.shape
    rate = rate_ref[...]
    boost = jnp.exp(u_ref[...])
    row, steps = scan_tiles(rate, True)
    falling = jnp.exp((row.astype(jnp.float32) - 7.0) * rate)
    fall_all = jnp.exp(-8.0 * rate)
    last = row > 6
    pair = 16
    count = span // pair

    def body(i, carry):
        at = pl.ds(pl.multiple_of((count - 1 - i) * pair, pair), pair)
        new = []
        rate_sum, first_sum = carry[-2:]
        for n in range(seqs):
            loaded = [ref[n, at, :] for ref in (k_ref, v_ref, r_ref, a_ref, b_ref, g_ref)]
            state = carry[2 * n : 2 * n + 2]
            tiles = []
            for g in (1, 0):
                k, v, r, a, b, grad = (t[g * 8 : g * 8 + 8] for t in loaded)
                weight = jnp.exp(k)
                bonus = boost * weight
                over = 1.0 / (b + bonus)
                wkv = (a + bonus * v) * over
                alpha = grad * jax.nn.sigmoid(r) * over
                sums = [scan_rows(t, steps, True) for t in (alpha, -alpha * wkv)]
                p, q = (
                    falling * c + jnp.where(last, 0.0, turn(t, 1, True))
                    for c, t in zip(state, sums)
                )
                state = tuple(fall_all * c + t[0:1] for c, t in zip(state, sums))
                share = alpha * bonus
                own = share * (v - wkv)
                tiles.append((own + weight * (p * v + q), share + weight * p))
                rate_sum = rate_sum + (a * p + b * q)
                first_sum = first_sum + own
            k_grad, v_grad = (jnp.concatenate(t, axis=0) for t in zip(*tiles[::-1]))
            k_out[n, at, :] = k_grad.astype(k_out.dtype)
            v_out[n, at, :] = v_grad.astype(v_out.dtype)
            new += state
        return tuple(new) + (rate_sum, first_sum)

    start = []
    for n in range(seqs):
        start += [p0_ref[n : n + 1, :], q0_ref[n : n + 1, :]]
    zero = jnp.zeros((8, lanes), jnp.float32)
    done = lax.fori_loop(0, count, body, tuple(start) + (zero, zero), unroll=2)
    rate_out[...] = -rate * jnp.exp(-rate) * jnp.sum(done[-2], axis=0, keepdims=True)
    first_out[...] = jnp.sum(done[-1], axis=0, keepdims=True)


def first_kernel(flag_ref, tok_ref, prev_ref, vec_ref, w_ref, x0_ref, x1_ref, x2_ref, y_ref, local_ref, gap_ref, normed, before, key):
    seqs, span, channels = tok_ref.shape
    j = pl.program_id(0)

    @pl.when(j == 0)
    def _():
        gain, bias = (vec_ref[0:1, :], vec_ref[1:2, :])
        for n in range(seqs):
            rows = pl.ds(n * span, span)
            field = norm_stats(tok_ref[n].astype(jnp.float32))[0] * gain + bias
            edge = norm_stats(prev_ref[n : n + 1, :].astype(jnp.float32))[0] * gain + bias
            edge = jnp.where(flag_ref[0] > 0, edge, 0.0)
            row = lax.broadcasted_iota(jnp.int32, field.shape, 0)
            normed[rows, :] = field
            earlier = jnp.where(row < 1, edge, pltpu.roll(field, 1, 0))
            before[rows, :] = earlier
            gap_ref[rows, :] = field - earlier

    mix = vec_ref[pl.ds(2 + j, 1), :]
    x = (normed[...] * mix + before[...] * (1.0 - mix)).astype(jnp.bfloat16)
    y = jnp.dot(x, w_ref[0], preferred_element_type=jnp.float32)
    y_ref[0] = y.reshape(seqs, span, channels)
    for k, ref in enumerate((x0_ref, x1_ref, x2_ref)):

        @pl.when(j == k)
        def _(ref=ref):
            ref[...] = x.reshape(seqs, span, channels)

    @pl.when(j == 0)
    def _():
        key[...] = y

    @pl.when(j == 1)
    def _():
        rate = vec_ref[5:6, :]
        place = lax.broadcasted_iota(jnp.int32, (span, channels), 0).astype(jnp.float32)
        fall = (place - (span - 1.0)) * rate
        for n in range(seqs):
            rows = slice(n * span, (n + 1) * span)
            weight = jnp.exp(key[rows, :] + fall)
            local_ref[0, n : n + 1, :] = jnp.sum(weight * y[rows], axis=0, keepdims=True)
            local_ref[1, n : n + 1, :] = jnp.sum(weight, axis=0, keepdims=True)


def first_projections(flag, tokens, prev, vectors, mats):
    seqs, span, channels = tokens.shape
    fixed = lambda *shape: pl.BlockSpec(shape, lambda j: (0,) * len(shape))
    rows = (seqs * span, channels)
    outs = pl.pallas_call(
        first_kernel,
        grid=(3,),
        out_shape=[jax.ShapeDtypeStruct(tokens.shape, jnp.bfloat16)] * 3
        + [jax.ShapeDtypeStruct((3, *tokens.shape), jnp.float32)]
        + [jax.ShapeDtypeStruct((2, seqs, channels), jnp.float32), jax.ShapeDtypeStruct(rows, jnp.float32)],
        in_specs=[
            pl.BlockSpec(memory_space=pltpu.SMEM),
            fixed(*tokens.shape),
            fixed(*prev.shape),
            fixed(*vectors.shape),
            pl.BlockSpec((1, channels, channels), lambda j: (j, 0, 0)),
        ],
        out_specs=[fixed(*tokens.shape)] * 3
        + [pl.BlockSpec((1, *tokens.shape), lambda j: (j, 0, 0, 0)), fixed(2, seqs, channels), fixed(*rows)],
        scratch_shapes=[pltpu.VMEM(rows, jnp.float32)] * 3,
        compiler_params=pltpu.CompilerParams(vmem_limit_bytes=48 << 20),
        cost_estimate=pl.CostEstimate(flops=1 << 20, bytes_accessed=1 << 16, transcendentals=0),
    )(flag, tokens, prev, vectors, mats)
    return outs[:3], outs[3], outs[4], outs[5]


def ffn_back_kernel(grad_ref, relu_ref, down_ref, up_ref, up_grad_ref, out_ref):
    wide = (((1,), (1,)), ((), ()))
    squared = lax.dot_general(grad_ref[...], down_ref[...], wide, preferred_element_type=jnp.float32)
    up_grad = (squared * (2.0 * relu_ref[...].astype(jnp.float32))).astype(jnp.bfloat16)
    up_grad_ref[...] = up_grad
    part = lax.dot_general(up_grad, up_ref[...], wide, preferred_element_type=jnp.float32)

    @pl.when(pl.program_id(0) == 0)
    def _():
        out_ref[...] = part

    @pl.when(pl.program_id(0) > 0)
    def _():
        out_ref[...] += part


def ffn_backward(grad, relu_up, down, up):
    rows, channels = grad.shape
    hidden = up.shape[1]
    block = 1024
    column = pl.BlockSpec((rows, block), lambda j: (0, j))
    return pl.pallas_call(
        ffn_back_kernel,
        grid=(hidden // block,),
        out_shape=[
            jax.ShapeDtypeStruct((rows, hidden), jnp.bfloat16),
            jax.ShapeDtypeStruct((rows, channels), jnp.float32),
        ],
        in_specs=[
            pl.BlockSpec((rows, channels), lambda j: (0, 0)),
            column,
            pl.BlockSpec((block, channels), lambda j: (j, 0)),
            pl.BlockSpec((channels, block), lambda j: (0, j)),
        ],
        out_specs=[column, pl.BlockSpec((rows, channels), lambda j: (0, 0))],
        compiler_params=pltpu.CompilerParams(vmem_limit_bytes=40 << 20),
        cost_estimate=pl.CostEstimate(
            flops=1 << 20, bytes_accessed=24 << 20, transcendentals=0
        ),
    )(grad, relu_up, down, up)


def in_grads_kernel(k_ref, v_ref, r_ref, gap_ref, mix_ref, w_ref, now_ref, next_ref, sum_ref):
    j = pl.program_id(0)
    grad = jnp.where(j == 0, k_ref[...], jnp.where(j == 1, v_ref[...], r_ref[...]))
    wide = (((1,), (1,)), ((), ()))
    part = lax.dot_general(grad, w_ref[0], wide, preferred_element_type=jnp.float32)
    mix = mix_ref[pl.ds(j, 1), :]
    now = part * mix
    sum_ref[pl.ds(j, 1), :] = jnp.sum(part * gap_ref[...], axis=0, keepdims=True)

    @pl.when(j == 0)
    def _():
        now_ref[...] = now
        next_ref[...] = part - now

    @pl.when(j > 0)
    def _():
        now_ref[...] += now
        next_ref[...] += part - now


def input_gradients(grads, gap, mixes, mats):
    rows, channels = gap.shape
    fixed = lambda *shape: pl.BlockSpec(shape, lambda j: (0,) * len(shape))
    return pl.pallas_call(
        in_grads_kernel,
        grid=(3,),
        out_shape=[jax.ShapeDtypeStruct(gap.shape, jnp.float32)] * 2
        + [jax.ShapeDtypeStruct((3, channels), jnp.float32)],
        in_specs=[fixed(rows, channels)] * 4
        + [fixed(3, channels), pl.BlockSpec((1, channels, channels), lambda j: (j, 0, 0))],
        out_specs=[fixed(rows, channels)] * 2 + [fixed(3, channels)],
        compiler_params=pltpu.CompilerParams(vmem_limit_bytes=40 << 20),
        cost_estimate=pl.CostEstimate(flops=1 << 20, bytes_accessed=8 << 20, transcendentals=0),
    )(*grads, gap, mixes, mats)


LANES = 256


def wkv_specs(seqs, span):
    field = pl.BlockSpec((seqs, span, LANES), lambda j: (0, 0, j))
    state = pl.BlockSpec((seqs, LANES), lambda j: (0, j))
    vector = pl.BlockSpec((1, LANES), lambda j: (0, j))
    return field, state, vector


def stacked_specs(seqs, span):
    shape = (None, seqs, span, LANES)
    return [pl.BlockSpec(shape, lambda j, n=n: (n, 0, 0, j)) for n in range(3)]


def wkv_forward(kvr, a0, b0, u, rate):
    shape = kvr.shape[1:]
    _, span, channels = shape
    seqs = shape[0]
    field, state, vector = wkv_specs(seqs, span)
    return pl.pallas_call(
        wkv_kernel,
        grid=(channels // LANES,),
        out_shape=[jax.ShapeDtypeStruct(shape, t) for t in (jnp.float32, jnp.float32, jnp.bfloat16)],
        in_specs=stacked_specs(seqs, span) + [state] * 2 + [vector] * 2,
        out_specs=[field] * 3,
        compiler_params=pltpu.CompilerParams(vmem_limit_bytes=32 << 20),
        cost_estimate=pl.CostEstimate(flops=1 << 20, bytes_accessed=1 << 16, transcendentals=0),
    )(kvr, kvr, kvr, a0, b0, u[None], rate[None])


def wkv_backward(kvr, a, b, grad, p0, q0, u, rate):
    seqs, span, channels = a.shape
    field, state, vector = wkv_specs(seqs, span)
    k_grad, v_grad, decay_grad, first_grad = pl.pallas_call(
        wkv_back_kernel,
        grid=(channels // LANES,),
        out_shape=[jax.ShapeDtypeStruct(a.shape, jnp.bfloat16)] * 2
        + [jax.ShapeDtypeStruct((1, channels), jnp.float32)] * 2,
        in_specs=stacked_specs(seqs, span) + [field] * 3 + [state] * 2 + [vector] * 2,
        out_specs=[field] * 2 + [vector] * 2,
        compiler_params=pltpu.CompilerParams(vmem_limit_bytes=32 << 20),
        cost_estimate=pl.CostEstimate(flops=1 << 20, bytes_accessed=1 << 16, transcendentals=0),
    )(kvr, kvr, kvr, a, b, grad, p0, q0, u[None], rate[None])
    return k_grad, v_grad, decay_grad[0], first_grad[0]


def matmul(form, left, right):
    return jnp.einsum(form, left, right, preferred_element_type=jnp.float32)


def shifted(block, axis, distance):
    count = lax.axis_size(axis)
    route = [(i - distance, i) for i in range(count) if 0 <= i - distance < count]
    return lax.ppermute(block, axis, route)


def previous_rows(field):
    came = shifted(field[:, -1, :], SEQ, 1)
    return jnp.concatenate([came[:, None, :], field[:, :-1, :]], axis=1)


def next_rows(field):
    came = shifted(field[:, 0, :], SEQ, -1)
    return jnp.concatenate([field[:, 1:, :], came[:, None, :]], axis=1)


def entering(factor, states, reverse):
    block = jnp.stack(states)
    low, high = in_order(block, spread(block, "core")[0])
    near, far = (high, low) if reverse else (low, high)
    chip = factor * near + far
    total, power = (jnp.zeros_like(block), jnp.ones_like(factor))
    for k in range(1, lax.axis_size("y")):
        total = total + power * shifted(chip, "y", -k if reverse else k)
        power = power * factor * factor
    core = lax.axis_index("core")
    total = jnp.where(core == (1 if reverse else 0), total, factor * total + near)
    return (total[0], total[1])


def in_order(own, other):
    core = lax.axis_index("core")
    return (jnp.where(core == 0, own, other), jnp.where(core == 0, other, own))


def own_half(x, own=True):
    half = x.shape[-1] // 2
    core = lax.axis_index("core")
    return jnp.where((core == 0) == own, x[..., :half], x[..., half:])


def after(x, deps):
    return lax.optimization_barrier((x, deps))[0] if jax.tree.leaves(deps) else x


def spread(block, axis):
    count = lax.axis_size(axis)
    return [
        lax.ppermute(block, axis, [(i, (i + k) % count) for i in range(count)])
        for k in range(1, count)
    ]


def cross(block, first, k):
    ys, cs, zs, xs = (lax.axis_size(axis) for axis in ALL)
    route = []
    for i in range(ys * cs * zs * xs):
        y, c, z, x = (i // (cs * zs * xs), i // (zs * xs) % cs, i // xs % zs, i % xs)
        if (c == 0) == first:
            x = (x + k) % xs
        else:
            y = (y + k) % ys
        route.append((i, ((y * cs + c) * zs + z) * xs + x))
    return lax.ppermute(block, ALL, route)


def beside_z(own):
    half = own.shape[1] // 2
    rows = lax.all_gather(own, "z", axis=0)
    return (rows[:, :, :half], rows[:, :, half:])


def beside_xy(pair, axes):
    return [[block] + spread(block, axis) for block, axis in zip(pair, axes)]


def other_core(parts):
    return [[spread(block, "core")[0] for block in part] for part in parts]


def assemble_kernel(entries, grid, at_ref, *refs):
    n_out = 1 + max(entry[2] for entry in entries)
    sources, outs, sems = (refs[: -n_out - 1], refs[-n_out - 1 : -1], refs[-1])
    ys, cs, zs, xs = grid
    y, c, x = (at_ref[j] for j in range(3))

    def back(at, k, count):
        return lax.rem(at - k + count, count)

    index = 0
    for dc in range(cs):
        for half, lead in enumerate((xs, ys)):
            for far in range(ys if half == 0 else xs):
                source = sources[index]
                index += 1

                def copy(k, _, source=source, dc=dc, half=half, far=far):
                    near, dz = (k // zs, lax.rem(k, zs))
                    dy, dx = (far, near) if half == 0 else (near, far)
                    block = back(y, dy, ys) * cs + back(c, dc, cs)
                    block = (block * zs + dz) * xs + back(x, dx, xs)
                    for first, rows, out, column, lead_at in entries:
                        width = source.shape[-1]
                        pltpu.make_async_copy(
                            source.at[near, dz, pl.ds(first, rows), :],
                            outs[out].at[lead_at, block, :, pl.ds(column + half * width, width)],
                            sems.at[out],
                        ).start()
                    return 0

                lax.fori_loop(0, lead * zs, copy, 0)
    for out in range(n_out):
        pltpu.make_async_copy(outs[out], outs[out], sems.at[out]).wait()


def assemble(mine, other, entries, shapes, grid):
    sources = [b for part in mine for b in part] + [b for part in other for b in part]
    at = jnp.stack([lax.axis_index(axis) for axis in ("y", "core", "x")]).astype(jnp.int32)
    count = grid[0] * grid[1] * grid[2] * grid[3]
    outs = pl.pallas_call(
        functools.partial(assemble_kernel, entries, grid),
        out_shape=[jax.ShapeDtypeStruct((n, count, *shape), jnp.bfloat16) for n, *shape in shapes],
        in_specs=[pl.BlockSpec(memory_space=pltpu.SMEM)]
        + [pl.BlockSpec(memory_space=pl.ANY)] * len(sources),
        out_specs=[pl.BlockSpec(memory_space=pltpu.VMEM)] * len(shapes),
        scratch_shapes=[pltpu.SemaphoreType.DMA((len(shapes),))],
        compiler_params=pltpu.CompilerParams(vmem_limit_bytes=40 << 20),
    )(at, *sources)
    return [out.reshape(out.shape[0], -1, out.shape[-1]) for out in outs]


class Partial:
    def __init__(self, parts, first, deps=()):
        self.parts, self.first = (parts, first)
        self.sent, self.came = ([], [])
        for k in range(1, lax.axis_size("x")):
            blocks = [after(self.take(p, k), deps) for p in parts]
            self.sent += blocks
            self.came.append([cross(block, first, k) for block in blocks])

    def take(self, p, k):
        count = lax.axis_size("x")
        x, y = (lax.rem(lax.axis_index(axis) + k, count) for axis in ("x", "y"))
        core = lax.axis_index("core")
        if self.first:
            by_x = lax.dynamic_index_in_dim(p, x, 3, keepdims=False).transpose(2, 1, 0, 3, 4)
            by_y = lax.dynamic_index_in_dim(p, y, 0, keepdims=False).transpose(1, 0, 2, 3, 4)
            return jnp.where(core == 0, by_x, by_y)
        return lax.dynamic_index_in_dim(p, jnp.where(core == 0, y, x), 2, keepdims=False)

    def finish(self, deps=()):
        totals = [self.take(p, 0).astype(jnp.float32) for p in self.parts]
        for blocks in after(self.came, deps):
            totals = [total + block.astype(jnp.float32) for total, block in zip(totals, blocks)]
        return [total.astype(jnp.bfloat16) for total in totals]


def stacked(parts, width):
    cut = [p[..., j : j + width] for p in parts for j in range(0, p.shape[-1], width)]
    return jnp.concatenate(cut, axis=2)


def over_z_direct(total):
    count, at = (lax.axis_size("z"), lax.axis_index("z"))
    block = lambda k: lax.dynamic_index_in_dim(total, lax.rem(at + k, count), 0, keepdims=False)
    out = block(0).astype(jnp.float32)
    for k in range(1, count):
        route = [(i, (i + k) % count) for i in range(count)]
        out = out + lax.ppermute(block(k), "z", route).astype(jnp.float32)
    return out.astype(jnp.bfloat16)


def over_z(total):
    zs, cores, rows, columns = total.shape
    flat = total.reshape(zs * cores * rows, columns)
    return lax.psum_scatter(flat, "z", scatter_dimension=0, tiled=True).reshape(cores, rows, columns)


def to_owner(total):
    core = lax.axis_index("core")
    came = spread(lax.dynamic_index_in_dim(total, 1 - core, 0, keepdims=False), "core")[0]
    return in_order(lax.dynamic_index_in_dim(total, core, 0, keepdims=False), came)


def per_device(
    tokens,
    lengths,
    cotangent,
    first_gain,
    first_bias,
    mix_key,
    mix_value,
    mix_recept,
    time_decay,
    time_first,
    key_weight,
    value_weight,
    recept_weight,
    output_weight,
    second_gain,
    second_bias,
    shift_key,
    shift_recept,
    up_weight,
    gate_weight,
    down_weight,
):
    grid = tuple(lax.axis_size(axis) for axis in ALL)
    count = grid[0] * grid[1] * grid[2] * grid[3]
    seq_count, piece_len, channels = tokens.shape
    hidden = up_weight.shape[1]
    mine = channels // count
    blocks = hidden // channels

    vectors = (
        first_gain,
        first_bias,
        mix_key,
        mix_value,
        mix_recept,
        time_decay,
        time_first,
        second_gain,
        second_bias,
        shift_key,
        shift_recept,
    )
    n_vec = len(vectors)
    packed = jnp.pad(jnp.stack(vectors), ((0, 16 - n_vec), (0, channels - mine)))
    pieces = (
        [key_weight, value_weight, recept_weight, packed],
        [output_weight] + [up_weight[:, j * channels : (j + 1) * channels] for j in range(blocks)],
        [gate_weight, down_weight],
    )
    places = (
        [(0, 0, 0), (0, 0, 1), (0, 0, 2), (1, 0, 0)],
        [(0, 0, 0)] + [(1, j * channels, 0) for j in range(blocks)],
        [(0, 0, 0), (1, 0, 0)],
    )
    chunks = [jnp.concatenate(piece) for piece in pieces]
    plans = []
    for piece, place in zip(pieces, places):
        first, entries, shapes = (0, [], {})
        for part, (out, column, lead) in zip(piece, place):
            entries.append((first, part.shape[0], out, column, lead))
            shapes[out] = (lead + 1, part.shape[0], column + channels)
            first += part.shape[0]
        plans.append((entries, [shapes[o] for o in sorted(shapes)]))
    stepwise = mine % 16 == 0

    def whole(at):
        gathered = lax.all_gather(chunks[at], ALL, axis=0)
        entries, shapes = plans[at]
        outs = []
        for out, (leads, _, columns) in enumerate(shapes):
            parts = [gathered[:, f : f + r] for f, r, o, _, _ in entries if o == out]
            if leads == 1:
                parts = [jnp.concatenate(parts, axis=-1)]
            outs.append(jnp.stack([p.reshape(-1, columns) for p in parts]))
        return outs

    if stepwise:
        half = channels // 2
        xy2 = beside_xy((chunks[2][:, :half], chunks[2][:, half:]), ("x", "y"))
        z0 = beside_z(chunks[0])
        z1 = beside_z(after(chunks[1], z0))
        z2 = [lax.all_gather(jnp.stack(part), "z", axis=1) for part in after(xy2, z0)]
        xy0 = beside_xy(after(z0, xy2), ("x", "y"))
        yx0 = beside_xy([jnp.stack(part) for part in xy0], ("y", "x"))
        xy1 = beside_xy(after(z1, yx0), ("x", "y"))
        first_mats, vecs = assemble(yx0, other_core(yx0), *plans[0], grid)
    else:
        first_mats, vecs = whole(0)
    vecs = vecs.reshape(count, 16, channels)[:, :n_vec, :mine]
    vecs = jnp.moveaxis(vecs, 1, 0).reshape(n_vec, channels).astype(jnp.float32)
    (
        norm_gain,
        norm_bias,
        key_mix,
        value_mix,
        recept_mix,
        decay_log,
        boost_log_scale,
        gain_two,
        bias_two,
        chan_key_mix,
        chan_recept_mix,
    ) = (vecs[j] for j in range(n_vec))
    seq_index = lax.axis_index(SEQ)
    positions = seq_index * piece_len + jnp.arange(piece_len, dtype=jnp.int32)
    live_mask = (positions[None, :] < lengths[:, None]).astype(jnp.float32)[:, :, None]
    field = tokens.astype(jnp.float32)
    normed_one, inverse_one = norm_stats(field)
    fading_rate_vector = jnp.exp(decay_log)
    place = jnp.arange(piece_len, dtype=jnp.float32)[:, None]
    piece_fall = jnp.exp(-piece_len * fading_rate_vector)
    rows = jnp.stack([norm_gain, norm_bias, key_mix, value_mix, recept_mix, fading_rate_vector])
    ins, kvr, local, gap_one = first_projections(
        (seq_index > 0).astype(jnp.int32)[None], tokens, shifted(tokens[:, -1, :], SEQ, 1), rows, first_mats
    )
    if stepwise:
        pair = [jnp.stack(part) for part in after(xy1, (ins, local))]
        local = after(local, pair)
        yx1 = beside_xy(pair, ("y", "x"))
        core1 = other_core([[part[0]] for part in yx1])
    key_in, value_in, recept_in = ins
    lookup_matrix_output, content_matrix_output, recept_proj = kvr
    local = (local[0], local[1])
    starting_accumulator, starting_normalizer = entering(piece_fall, local, False)
    if stepwise:
        starting_accumulator, starting_normalizer = after(
            (starting_accumulator, starting_normalizer), (yx1, core1, z2)
        )
    state_a, state_b, mixed_out = wkv_forward(
        kvr,
        starting_accumulator,
        starting_normalizer,
        boost_log_scale,
        fading_rate_vector,
    )
    if stepwise:
        yx2 = beside_xy(after(tuple(z2), yx1), ("y", "x"))
        rest1 = other_core([part[1:] for part in yx1])
        core1 = [one + rest for one, rest in zip(core1, rest1)]
        yx1 = after(yx1, (state_a, state_b))
        (output_mat,), (up_mat,) = assemble(yx1, core1, *plans[1], grid)
    else:
        (output_mat,), (up_mat,) = whole(1)
    branch = matmul("nlc,cd->nld", mixed_out, output_mat)
    residual = field + branch
    normed_two_raw, inverse_two = norm_stats(residual)
    normed_two = normed_two_raw * gain_two + bias_two
    before_two = previous_rows(normed_two)
    ffn_key = (normed_two * chan_key_mix + before_two * (1.0 - chan_key_mix)).astype(jnp.bfloat16)
    ffn_recept = (normed_two * chan_recept_mix + before_two * (1.0 - chan_recept_mix)).astype(
        jnp.bfloat16
    )
    flat_key = ffn_key.reshape(seq_count * piece_len, channels)
    relu_up = jax.nn.relu(jnp.dot(flat_key, up_mat, preferred_element_type=jnp.float32))
    squared, relu_up = (jnp.square(relu_up).astype(jnp.bfloat16), relu_up.astype(jnp.bfloat16))
    if stepwise:
        core2 = other_core([[part] for part in after(tuple(z2), (ffn_key, ffn_recept))])
        yx2 = after(yx2, (squared, relu_up, core2))
        rest2 = other_core([part[1:] for part in yx2])
        core2 = [one + rest for one, rest in zip(core2, rest2)]
        (gate_mat,), (down_mat,) = assemble(yx2, core2, *plans[2], grid)
    else:
        (gate_mat,), (down_mat,) = whole(2)
    squared = squared.reshape(seq_count, piece_len, hidden)
    down_proj = matmul("nlf,fd->nld", squared, down_mat)
    gate_value = jax.nn.sigmoid(matmul("nlc,cd->nld", ffn_recept, gate_mat))
    output = ((residual + gate_value * down_proj) * live_mask).astype(jnp.bfloat16)

    def outer(left, right):
        return jnp.einsum("nlc,nld->cd", left, right, preferred_element_type=jnp.float32)

    def to_core(left, right):
        send = outer(left, own_half(right, False)).astype(jnp.bfloat16)
        return send, spread(send, "core")[0]

    def both_cores(left, right, came):
        rows = outer(left, own_half(right)) + came.astype(jnp.float32)
        return rows.astype(jnp.bfloat16).reshape(*grid, -1, rows.shape[-1])

    seed = cotangent.astype(jnp.float32) * live_mask
    down_grad = (seed * gate_value).astype(jnp.bfloat16)
    gate_grad = (seed * down_proj * gate_value * (1.0 - gate_value)).astype(jnp.bfloat16)
    width = channels // 2
    down_send, down_came = to_core(squared, down_grad)
    gate_send, gate_came = to_core(ffn_recept, gate_grad)
    ffn_recept_grad = matmul("nld,cd->nlc", after(gate_grad, (down_send, gate_send)), gate_mat)
    late = (down_grad, gate_grad, down_came, gate_came)
    d_grad, g_grad, down_came, gate_came = after(late, ffn_recept_grad)
    way1 = Partial([both_cores(squared, d_grad, down_came), both_cores(ffn_recept, g_grad, gate_came)], True)
    flat = (seq_count * piece_len, -1)
    up_grad, ffn_key_grad = ffn_backward(
        after(down_grad, way1.sent).reshape(flat), relu_up, down_mat, up_mat
    )
    up_grad = up_grad.reshape(seq_count, piece_len, hidden)
    ffn_key_grad = ffn_key_grad.reshape(tokens.shape)
    up_send, up_came = to_core(ffn_key, up_grad)
    u_grad, up_came = after((up_grad, up_came), up_send)
    grad_up_part = both_cores(ffn_key, u_grad, up_came)
    normed_two_grad = (
        ffn_key_grad * chan_key_mix
        + ffn_recept_grad * chan_recept_mix
        + next_rows(ffn_key_grad * (1.0 - chan_key_mix) + ffn_recept_grad * (1.0 - chan_recept_mix))
    )
    gap_two = normed_two - before_two
    grad_chan_key = jnp.sum(ffn_key_grad * gap_two, axis=(0, 1))
    grad_chan_recept = jnp.sum(ffn_recept_grad * gap_two, axis=(0, 1))
    grad_gain_two = jnp.sum(normed_two_grad * normed_two_raw, axis=(0, 1))
    grad_bias_two = jnp.sum(normed_two_grad, axis=(0, 1))
    residual_grad = seed + norm_back(normed_two_grad * gain_two, normed_two_raw, inverse_two)
    branch_grad = residual_grad.astype(jnp.bfloat16)
    back1 = Partial(way1.finish(deps=(branch_grad,)), False)
    branch_grad = after(branch_grad, back1.sent)
    mixed_grad = matmul("nld,cd->nlc", branch_grad, output_mat)
    out_send, out_came = to_core(mixed_out, branch_grad)
    bonus = jnp.exp(boost_log_scale) * jnp.exp(lookup_matrix_output)
    over = 1.0 / (state_b + bonus)
    blended = (state_a + bonus * content_matrix_output) * over
    recept_sig = jax.nn.sigmoid(recept_proj)
    recept_grad = (mixed_grad * blended * recept_sig * (1.0 - recept_sig)).astype(jnp.bfloat16)
    alpha = mixed_grad * recept_sig * over * jnp.exp(-place * fading_rate_vector)
    local = (jnp.sum(alpha, axis=1), -jnp.sum(alpha * blended, axis=1))
    carry_p, carry_q = entering(piece_fall, local, True)
    z1 = over_z(stacked(back1.finish(), width))
    recept_send, recept_came = to_core(recept_in, recept_grad)
    g_out, g_recept, out_came, recept_came = after((branch_grad, recept_grad, out_came, recept_came), recept_send)
    part_out = both_cores(mixed_out, g_out, out_came)
    part_recept = both_cores(recept_in, g_recept, recept_came)
    way2 = Partial([grad_up_part, part_out, part_recept], True, deps=back1.came)
    carry_p, carry_q = after((carry_p, carry_q), way2.sent)
    key_grad, value_grad, grad_decay, boost_adjoint_term = wkv_backward(
        kvr,
        state_a,
        state_b,
        mixed_grad,
        carry_p,
        carry_q,
        boost_log_scale,
        fading_rate_vector,
    )
    key_send, key_came = to_core(key_in, key_grad)
    value_send, value_came = to_core(value_in, value_grad)
    late = (key_grad, value_grad, key_came, value_came)
    back2 = Partial(way2.finish(deps=(key_send, value_send)), False)
    k_grad, v_grad, key_came, value_came = after(late, back2.sent)
    part_key = both_cores(key_in, k_grad, key_came)
    part_value = both_cores(value_in, v_grad, value_came)
    way3 = Partial([part_key, part_value], True, deps=back2.came)
    z2 = over_z(stacked(back2.finish(deps=way3.sent), width))
    flat = (seq_count * piece_len, channels)
    grads = [g.reshape(flat) for g in after((k_grad, v_grad, recept_grad), (part_key, part_value))]
    mixes = jnp.stack([key_mix, value_mix, recept_mix])
    now_part, next_part, grad_mixes = input_gradients(grads, gap_one, mixes, first_mats)
    back3 = Partial(way3.finish(), False)
    now_part, next_part = after((now_part, next_part), way3.sent)
    normed_grad = now_part.reshape(tokens.shape) + next_rows(next_part.reshape(tokens.shape))
    grad_key_mix, grad_value_mix, grad_recept_mix = grad_mixes
    grad_gain_one = jnp.sum(normed_grad * normed_one, axis=(0, 1))
    grad_bias_one = jnp.sum(normed_grad, axis=(0, 1))
    tokens_grad = residual_grad + norm_back(normed_grad * norm_gain, normed_one, inverse_one)
    sums = jnp.concatenate(
        [
            grad_gain_one,
            grad_bias_one,
            grad_key_mix,
            grad_value_mix,
            grad_recept_mix,
            grad_decay,
            boost_adjoint_term,
            grad_gain_two,
            grad_bias_two,
            grad_chan_key,
            grad_chan_recept,
        ]
    )
    for axis in ("core", "x", "y", "z"):
        sums = sums + sum(spread(sums, axis))
    sums = lax.dynamic_slice_in_dim(sums.reshape(n_vec, channels), lax.axis_index(ALL) * mine, mine, 1)
    z3 = over_z_direct(stacked(back3.finish(), width))
    first, second, third = (to_owner(z) for z in (z1, z2, z3))

    def rows_of(pair, at, rows=mine, columns=1):
        cut = [h[at + j * rows : at + (j + 1) * rows] for h in pair for j in range(columns)]
        return jnp.concatenate(cut, axis=1).astype(jnp.float32)

    return (
        output,
        tokens_grad,
        *(sums[j] for j in range(7)),
        rows_of(third, 0),
        rows_of(third, mine),
        rows_of(second, (blocks + 1) * mine),
        rows_of(second, blocks * mine),
        *(sums[j] for j in range(7, n_vec)),
        rows_of(second, 0, columns=blocks),
        rows_of(first, hidden // count),
        rows_of(first, 0, hidden // count),
    )


def solution(mesh):
    seq, dp = (mesh.shape["seq"], mesh.shape["dp"])
    wide = len({device.coords[0] for device in mesh.devices.reshape(-1)})
    fine = jax.sharding.Mesh(mesh.devices.reshape(seq // 2, 2, dp // wide, wide), ALL)
    field, vector, matrix = (P(DP, SEQ, None), P(ALL), P(ALL, None))
    return jax.shard_map(
        per_device,
        mesh=fine,
        in_specs=(field, P(DP), field) + (vector,) * 7 + (matrix,) * 4 + (vector,) * 4 + (matrix,) * 3,
        out_specs=(field, field) + (vector,) * 7 + (matrix,) * 4 + (vector,) * 4 + (matrix,) * 3,
        check_vma=False,
    )
```

```python
import functools

import jax
import jax.numpy as jnp
from jax import lax
from jax.experimental import pallas as pl
from jax.experimental.pallas import tpu as pltpu
from jax.sharding import PartitionSpec as P

EPS = 1e-05

def norm_stats(field):
    center = field - jnp.mean(field, axis=-1, keepdims=True)
    inverse = lax.rsqrt(jnp.mean(center * center, axis=-1, keepdims=True) + EPS)
    return (center * inverse, inverse)


def norm_back(grad_normed, normalized, inverse):
    mean_grad = jnp.mean(grad_normed, axis=-1, keepdims=True)
    mean_proj = jnp.mean(grad_normed * normalized, axis=-1, keepdims=True)
    return inverse * (grad_normed - mean_grad - normalized * mean_proj)


SEQ = ("y", "core")
DP = ("z", "x")
ALL = ("y", "core", "z", "x")


def scan_tiles(rate, reverse):
    row = lax.broadcasted_iota(jnp.int32, (8, rate.shape[-1]), 0)
    steps = []
    for distance in (1, 2, 4):
        inside = row < 8 - distance if reverse else row >= distance
        steps.append((distance, jnp.where(inside, jnp.exp(-float(distance) * rate), 0.0)))
    return row, steps


def turn(x, distance, reverse):
    return pltpu.roll(x, 8 - distance if reverse else distance, 0)


def scan_rows(x, steps, reverse):
    for distance, factor in steps:
        x = x + factor * turn(x, distance, reverse)
    return x


def wkv_kernel(k_ref, v_ref, r_ref, a0_ref, b0_ref, u_ref, rate_ref, a_ref, b_ref, mixed_ref):
    seqs, span, lanes = k_ref.shape
    rate = rate_ref[...]
    boost = jnp.exp(u_ref[...])
    row, steps = scan_tiles(rate, False)
    falling = jnp.exp(-row.astype(jnp.float32) * rate)
    fall_all = jnp.exp(-8.0 * rate)
    first = row < 1
    pair = 16

    def body(i, carry):
        at = pl.ds(pl.multiple_of(i * pair, pair), pair)
        new = []
        for n in range(seqs):
            k16, v16, r16 = (ref[n, at, :] for ref in (k_ref, v_ref, r_ref))
            state = carry[2 * n : 2 * n + 2]
            tiles = []
            for g in range(2):
                k, v, r = (t[g * 8 : g * 8 + 8] for t in (k16, v16, r16))
                weight = jnp.exp(k)
                bonus = boost * weight
                sums = [scan_rows(t, steps, False) for t in (weight * v, weight)]
                a, b = (
                    falling * c + jnp.where(first, 0.0, turn(t, 1, False))
                    for c, t in zip(state, sums)
                )
                state = tuple(fall_all * c + t[7:8] for c, t in zip(state, sums))
                mixed = jax.nn.sigmoid(r) * ((a + bonus * v) / (b + bonus))
                tiles.append((a, b, mixed))
            a, b, mixed = (jnp.concatenate(t, axis=0) for t in zip(*tiles))
            a_ref[n, at, :] = a
            b_ref[n, at, :] = b
            mixed_ref[n, at, :] = mixed.astype(mixed_ref.dtype)
            new += state
        return tuple(new)

    start = []
    for n in range(seqs):
        start += [a0_ref[n : n + 1, :], b0_ref[n : n + 1, :]]
    lax.fori_loop(0, span // pair, body, tuple(start), unroll=2)


def wkv_back_kernel(
    k_ref, v_ref, r_ref, a_ref, b_ref, g_ref, p0_ref, q0_ref, u_ref, rate_ref,
    k_out, v_out, rate_out, first_out,
):
    seqs, span, lanes = k_ref.shape
    rate = rate_ref[...]
    boost = jnp.exp(u_ref[...])
    row, steps = scan_tiles(rate, True)
    falling = jnp.exp((row.astype(jnp.float32) - 7.0) * rate)
    fall_all = jnp.exp(-8.0 * rate)
    last = row > 6
    pair = 16
    count = span // pair

    def body(i, carry):
        at = pl.ds(pl.multiple_of((count - 1 - i) * pair, pair), pair)
        new = []
        rate_sum, first_sum = carry[-2:]
        for n in range(seqs):
            loaded = [ref[n, at, :] for ref in (k_ref, v_ref, r_ref, a_ref, b_ref, g_ref)]
            state = carry[2 * n : 2 * n + 2]
            tiles = []
            for g in (1, 0):
                k, v, r, a, b, grad = (t[g * 8 : g * 8 + 8] for t in loaded)
                weight = jnp.exp(k)
                bonus = boost * weight
                over = 1.0 / (b + bonus)
                wkv = (a + bonus * v) * over
                alpha = grad * jax.nn.sigmoid(r) * over
                sums = [scan_rows(t, steps, True) for t in (alpha, -alpha * wkv)]
                p, q = (
                    falling * c + jnp.where(last, 0.0, turn(t, 1, True))
                    for c, t in zip(state, sums)
                )
                state = tuple(fall_all * c + t[0:1] for c, t in zip(state, sums))
                share = alpha * bonus
                own = share * (v - wkv)
                tiles.append((own + weight * (p * v + q), share + weight * p))
                rate_sum = rate_sum + (a * p + b * q)
                first_sum = first_sum + own
            k_grad, v_grad = (jnp.concatenate(t, axis=0) for t in zip(*tiles[::-1]))
            k_out[n, at, :] = k_grad.astype(k_out.dtype)
            v_out[n, at, :] = v_grad.astype(v_out.dtype)
            new += state
        return tuple(new) + (rate_sum, first_sum)

    start = []
    for n in range(seqs):
        start += [p0_ref[n : n + 1, :], q0_ref[n : n + 1, :]]
    zero = jnp.zeros((8, lanes), jnp.float32)
    done = lax.fori_loop(0, count, body, tuple(start) + (zero, zero), unroll=2)
    rate_out[...] = -rate * jnp.exp(-rate) * jnp.sum(done[-2], axis=0, keepdims=True)
    first_out[...] = jnp.sum(done[-1], axis=0, keepdims=True)


def first_kernel(flag_ref, tok_ref, prev_ref, vec_ref, w_ref, x0_ref, x1_ref, x2_ref, y_ref, local_ref, gap_ref, normed, before, key):
    seqs, span, channels = tok_ref.shape
    j = pl.program_id(0)

    @pl.when(j == 0)
    def _():
        gain, bias = (vec_ref[0:1, :], vec_ref[1:2, :])
        for n in range(seqs):
            rows = pl.ds(n * span, span)
            field = norm_stats(tok_ref[n].astype(jnp.float32))[0] * gain + bias
            edge = norm_stats(prev_ref[n : n + 1, :].astype(jnp.float32))[0] * gain + bias
            edge = jnp.where(flag_ref[0] > 0, edge, 0.0)
            row = lax.broadcasted_iota(jnp.int32, field.shape, 0)
            normed[rows, :] = field
            earlier = jnp.where(row < 1, edge, pltpu.roll(field, 1, 0))
            before[rows, :] = earlier
            gap_ref[rows, :] = field - earlier

    mix = vec_ref[pl.ds(2 + j, 1), :]
    x = (normed[...] * mix + before[...] * (1.0 - mix)).astype(jnp.bfloat16)
    y = jnp.dot(x, w_ref[0], preferred_element_type=jnp.float32)
    y_ref[0] = y.reshape(seqs, span, channels)
    for k, ref in enumerate((x0_ref, x1_ref, x2_ref)):

        @pl.when(j == k)
        def _(ref=ref):
            ref[...] = x.reshape(seqs, span, channels)

    @pl.when(j == 0)
    def _():
        key[...] = y

    @pl.when(j == 1)
    def _():
        rate = vec_ref[5:6, :]
        place = lax.broadcasted_iota(jnp.int32, (span, channels), 0).astype(jnp.float32)
        fall = (place - (span - 1.0)) * rate
        for n in range(seqs):
            rows = slice(n * span, (n + 1) * span)
            weight = jnp.exp(key[rows, :] + fall)
            local_ref[0, n : n + 1, :] = jnp.sum(weight * y[rows], axis=0, keepdims=True)
            local_ref[1, n : n + 1, :] = jnp.sum(weight, axis=0, keepdims=True)


def first_projections(flag, tokens, prev, vectors, mats):
    seqs, span, channels = tokens.shape
    fixed = lambda *shape: pl.BlockSpec(shape, lambda j: (0,) * len(shape))
    rows = (seqs * span, channels)
    outs = pl.pallas_call(
        first_kernel,
        grid=(3,),
        out_shape=[jax.ShapeDtypeStruct(tokens.shape, jnp.bfloat16)] * 3
        + [jax.ShapeDtypeStruct((3, *tokens.shape), jnp.float32)]
        + [jax.ShapeDtypeStruct((2, seqs, channels), jnp.float32), jax.ShapeDtypeStruct(rows, jnp.float32)],
        in_specs=[
            pl.BlockSpec(memory_space=pltpu.SMEM),
            fixed(*tokens.shape),
            fixed(*prev.shape),
            fixed(*vectors.shape),
            pl.BlockSpec((1, channels, channels), lambda j: (j, 0, 0)),
        ],
        out_specs=[fixed(*tokens.shape)] * 3
        + [pl.BlockSpec((1, *tokens.shape), lambda j: (j, 0, 0, 0)), fixed(2, seqs, channels), fixed(*rows)],
        scratch_shapes=[pltpu.VMEM(rows, jnp.float32)] * 3,
        compiler_params=pltpu.CompilerParams(vmem_limit_bytes=48 << 20),
        cost_estimate=pl.CostEstimate(flops=1 << 20, bytes_accessed=1 << 16, transcendentals=0),
    )(flag, tokens, prev, vectors, mats)
    return outs[:3], outs[3], outs[4], outs[5]


def ffn_back_kernel(grad_ref, relu_ref, down_ref, up_ref, up_grad_ref, out_ref):
    wide = (((1,), (1,)), ((), ()))
    squared = lax.dot_general(grad_ref[...], down_ref[...], wide, preferred_element_type=jnp.float32)
    up_grad = (squared * (2.0 * relu_ref[...].astype(jnp.float32))).astype(jnp.bfloat16)
    up_grad_ref[...] = up_grad
    part = lax.dot_general(up_grad, up_ref[...], wide, preferred_element_type=jnp.float32)

    @pl.when(pl.program_id(0) == 0)
    def _():
        out_ref[...] = part

    @pl.when(pl.program_id(0) > 0)
    def _():
        out_ref[...] += part


def ffn_backward(grad, relu_up, down, up):
    rows, channels = grad.shape
    hidden = up.shape[1]
    block = 1024
    column = pl.BlockSpec((rows, block), lambda j: (0, j))
    return pl.pallas_call(
        ffn_back_kernel,
        grid=(hidden // block,),
        out_shape=[
            jax.ShapeDtypeStruct((rows, hidden), jnp.bfloat16),
            jax.ShapeDtypeStruct((rows, channels), jnp.float32),
        ],
        in_specs=[
            pl.BlockSpec((rows, channels), lambda j: (0, 0)),
            column,
            pl.BlockSpec((block, channels), lambda j: (j, 0)),
            pl.BlockSpec((channels, block), lambda j: (0, j)),
        ],
        out_specs=[column, pl.BlockSpec((rows, channels), lambda j: (0, 0))],
        compiler_params=pltpu.CompilerParams(vmem_limit_bytes=40 << 20),
        cost_estimate=pl.CostEstimate(
            flops=1 << 20, bytes_accessed=24 << 20, transcendentals=0
        ),
    )(grad, relu_up, down, up)


def in_grads_kernel(k_ref, v_ref, r_ref, gap_ref, mix_ref, w_ref, now_ref, next_ref, sum_ref):
    j = pl.program_id(0)
    grad = jnp.where(j == 0, k_ref[...], jnp.where(j == 1, v_ref[...], r_ref[...]))
    wide = (((1,), (1,)), ((), ()))
    part = lax.dot_general(grad, w_ref[0], wide, preferred_element_type=jnp.float32)
    mix = mix_ref[pl.ds(j, 1), :]
    now = part * mix
    sum_ref[pl.ds(j, 1), :] = jnp.sum(part * gap_ref[...], axis=0, keepdims=True)

    @pl.when(j == 0)
    def _():
        now_ref[...] = now
        next_ref[...] = part - now

    @pl.when(j > 0)
    def _():
        now_ref[...] += now
        next_ref[...] += part - now


def input_gradients(grads, gap, mixes, mats):
    rows, channels = gap.shape
    fixed = lambda *shape: pl.BlockSpec(shape, lambda j: (0,) * len(shape))
    return pl.pallas_call(
        in_grads_kernel,
        grid=(3,),
        out_shape=[jax.ShapeDtypeStruct(gap.shape, jnp.float32)] * 2
        + [jax.ShapeDtypeStruct((3, channels), jnp.float32)],
        in_specs=[fixed(rows, channels)] * 4
        + [fixed(3, channels), pl.BlockSpec((1, channels, channels), lambda j: (j, 0, 0))],
        out_specs=[fixed(rows, channels)] * 2 + [fixed(3, channels)],
        compiler_params=pltpu.CompilerParams(vmem_limit_bytes=40 << 20),
        cost_estimate=pl.CostEstimate(flops=1 << 20, bytes_accessed=8 << 20, transcendentals=0),
    )(*grads, gap, mixes, mats)


LANES = 256


def wkv_specs(seqs, span):
    field = pl.BlockSpec((seqs, span, LANES), lambda j: (0, 0, j))
    state = pl.BlockSpec((seqs, LANES), lambda j: (0, j))
    vector = pl.BlockSpec((1, LANES), lambda j: (0, j))
    return field, state, vector


def stacked_specs(seqs, span):
    shape = (None, seqs, span, LANES)
    return [pl.BlockSpec(shape, lambda j, n=n: (n, 0, 0, j)) for n in range(3)]


def wkv_forward(kvr, a0, b0, u, rate):
    shape = kvr.shape[1:]
    _, span, channels = shape
    seqs = shape[0]
    field, state, vector = wkv_specs(seqs, span)
    return pl.pallas_call(
        wkv_kernel,
        grid=(channels // LANES,),
        out_shape=[jax.ShapeDtypeStruct(shape, t) for t in (jnp.float32, jnp.float32, jnp.bfloat16)],
        in_specs=stacked_specs(seqs, span) + [state] * 2 + [vector] * 2,
        out_specs=[field] * 3,
        compiler_params=pltpu.CompilerParams(vmem_limit_bytes=32 << 20),
        cost_estimate=pl.CostEstimate(flops=1 << 20, bytes_accessed=1 << 16, transcendentals=0),
    )(kvr, kvr, kvr, a0, b0, u[None], rate[None])


def wkv_backward(kvr, a, b, grad, p0, q0, u, rate):
    seqs, span, channels = a.shape
    field, state, vector = wkv_specs(seqs, span)
    k_grad, v_grad, decay_grad, first_grad = pl.pallas_call(
        wkv_back_kernel,
        grid=(channels // LANES,),
        out_shape=[jax.ShapeDtypeStruct(a.shape, jnp.bfloat16)] * 2
        + [jax.ShapeDtypeStruct((1, channels), jnp.float32)] * 2,
        in_specs=stacked_specs(seqs, span) + [field] * 3 + [state] * 2 + [vector] * 2,
        out_specs=[field] * 2 + [vector] * 2,
        compiler_params=pltpu.CompilerParams(vmem_limit_bytes=32 << 20),
        cost_estimate=pl.CostEstimate(flops=1 << 20, bytes_accessed=1 << 16, transcendentals=0),
    )(kvr, kvr, kvr, a, b, grad, p0, q0, u[None], rate[None])
    return k_grad, v_grad, decay_grad[0], first_grad[0]


def matmul(form, left, right):
    return jnp.einsum(form, left, right, preferred_element_type=jnp.float32)


def shifted(block, axis, distance):
    count = lax.axis_size(axis)
    route = [(i - distance, i) for i in range(count) if 0 <= i - distance < count]
    return lax.ppermute(block, axis, route)


def previous_rows(field):
    came = shifted(field[:, -1, :], SEQ, 1)
    return jnp.concatenate([came[:, None, :], field[:, :-1, :]], axis=1)


def next_rows(field):
    came = shifted(field[:, 0, :], SEQ, -1)
    return jnp.concatenate([field[:, 1:, :], came[:, None, :]], axis=1)


def entering(factor, states, reverse):
    block = jnp.stack(states)
    low, high = in_order(block, spread(block, "core")[0])
    near, far = (high, low) if reverse else (low, high)
    chip = factor * near + far
    total, power = (jnp.zeros_like(block), jnp.ones_like(factor))
    for k in range(1, lax.axis_size("y")):
        total = total + power * shifted(chip, "y", -k if reverse else k)
        power = power * factor * factor
    core = lax.axis_index("core")
    total = jnp.where(core == (1 if reverse else 0), total, factor * total + near)
    return (total[0], total[1])


def in_order(own, other):
    core = lax.axis_index("core")
    return (jnp.where(core == 0, own, other), jnp.where(core == 0, other, own))


def own_half(x, own=True):
    half = x.shape[-1] // 2
    core = lax.axis_index("core")
    return jnp.where((core == 0) == own, x[..., :half], x[..., half:])


def after(x, deps):
    return lax.optimization_barrier((x, deps))[0] if jax.tree.leaves(deps) else x


def spread(block, axis):
    count = lax.axis_size(axis)
    return [
        lax.ppermute(block, axis, [(i, (i + k) % count) for i in range(count)])
        for k in range(1, count)
    ]


def cross(block, first, k):
    ys, cs, zs, xs = (lax.axis_size(axis) for axis in ALL)
    route = []
    for i in range(ys * cs * zs * xs):
        y, c, z, x = (i // (cs * zs * xs), i // (zs * xs) % cs, i // xs % zs, i % xs)
        if (c == 0) == first:
            x = (x + k) % xs
        else:
            y = (y + k) % ys
        route.append((i, ((y * cs + c) * zs + z) * xs + x))
    return lax.ppermute(block, ALL, route)


def beside_z(own):
    half = own.shape[1] // 2
    rows = lax.all_gather(own, "z", axis=0)
    return (rows[:, :, :half], rows[:, :, half:])


def beside_xy(pair, axes):
    return [[block] + spread(block, axis) for block, axis in zip(pair, axes)]


def other_core(parts):
    return [[spread(block, "core")[0] for block in part] for part in parts]


def assemble_kernel(entries, grid, at_ref, *refs):
    n_out = 1 + max(entry[2] for entry in entries)
    sources, outs, sems = (refs[: -n_out - 1], refs[-n_out - 1 : -1], refs[-1])
    ys, cs, zs, xs = grid
    y, c, x = (at_ref[j] for j in range(3))

    def back(at, k, count):
        return lax.rem(at - k + count, count)

    index = 0
    for dc in range(cs):
        for half, lead in enumerate((xs, ys)):
            for far in range(ys if half == 0 else xs):
                source = sources[index]
                index += 1

                def copy(k, _, source=source, dc=dc, half=half, far=far):
                    near, dz = (k // zs, lax.rem(k, zs))
                    dy, dx = (far, near) if half == 0 else (near, far)
                    block = back(y, dy, ys) * cs + back(c, dc, cs)
                    block = (block * zs + dz) * xs + back(x, dx, xs)
                    for first, rows, out, column, lead_at in entries:
                        width = source.shape[-1]
                        pltpu.make_async_copy(
                            source.at[near, dz, pl.ds(first, rows), :],
                            outs[out].at[lead_at, block, :, pl.ds(column + half * width, width)],
                            sems.at[out],
                        ).start()
                    return 0

                lax.fori_loop(0, lead * zs, copy, 0)
    for out in range(n_out):
        pltpu.make_async_copy(outs[out], outs[out], sems.at[out]).wait()


def assemble(mine, other, entries, shapes, grid):
    sources = [b for part in mine for b in part] + [b for part in other for b in part]
    at = jnp.stack([lax.axis_index(axis) for axis in ("y", "core", "x")]).astype(jnp.int32)
    count = grid[0] * grid[1] * grid[2] * grid[3]
    outs = pl.pallas_call(
        functools.partial(assemble_kernel, entries, grid),
        out_shape=[jax.ShapeDtypeStruct((n, count, *shape), jnp.bfloat16) for n, *shape in shapes],
        in_specs=[pl.BlockSpec(memory_space=pltpu.SMEM)]
        + [pl.BlockSpec(memory_space=pl.ANY)] * len(sources),
        out_specs=[pl.BlockSpec(memory_space=pltpu.VMEM)] * len(shapes),
        scratch_shapes=[pltpu.SemaphoreType.DMA((len(shapes),))],
        compiler_params=pltpu.CompilerParams(vmem_limit_bytes=40 << 20),
    )(at, *sources)
    return [out.reshape(out.shape[0], -1, out.shape[-1]) for out in outs]


class Partial:
    def __init__(self, parts, first, deps=()):
        self.parts, self.first = (parts, first)
        self.sent, self.came = ([], [])
        for k in range(1, lax.axis_size("x")):
            blocks = [after(self.take(p, k), deps) for p in parts]
            self.sent += blocks
            self.came.append([cross(block, first, k) for block in blocks])

    def take(self, p, k):
        count = lax.axis_size("x")
        x, y = (lax.rem(lax.axis_index(axis) + k, count) for axis in ("x", "y"))
        core = lax.axis_index("core")
        if self.first:
            by_x = lax.dynamic_index_in_dim(p, x, 3, keepdims=False).transpose(2, 1, 0, 3, 4)
            by_y = lax.dynamic_index_in_dim(p, y, 0, keepdims=False).transpose(1, 0, 2, 3, 4)
            return jnp.where(core == 0, by_x, by_y)
        return lax.dynamic_index_in_dim(p, jnp.where(core == 0, y, x), 2, keepdims=False)

    def finish(self, deps=()):
        totals = [self.take(p, 0).astype(jnp.float32) for p in self.parts]
        for blocks in after(self.came, deps):
            totals = [total + block.astype(jnp.float32) for total, block in zip(totals, blocks)]
        return [total.astype(jnp.bfloat16) for total in totals]


def stacked(parts, width):
    cut = [p[..., j : j + width] for p in parts for j in range(0, p.shape[-1], width)]
    return jnp.concatenate(cut, axis=2)


def over_z_direct(total):
    count, at = (lax.axis_size("z"), lax.axis_index("z"))
    block = lambda k: lax.dynamic_index_in_dim(total, lax.rem(at + k, count), 0, keepdims=False)
    out = block(0).astype(jnp.float32)
    for k in range(1, count):
        route = [(i, (i + k) % count) for i in range(count)]
        out = out + lax.ppermute(block(k), "z", route).astype(jnp.float32)
    return out.astype(jnp.bfloat16)


def over_z(total):
    zs, cores, rows, columns = total.shape
    flat = total.reshape(zs * cores * rows, columns)
    return lax.psum_scatter(flat, "z", scatter_dimension=0, tiled=True).reshape(cores, rows, columns)


def to_owner(total):
    core = lax.axis_index("core")
    came = spread(lax.dynamic_index_in_dim(total, 1 - core, 0, keepdims=False), "core")[0]
    return in_order(lax.dynamic_index_in_dim(total, core, 0, keepdims=False), came)


def per_device(
    tokens,
    lengths,
    cotangent,
    first_gain,
    first_bias,
    mix_key,
    mix_value,
    mix_recept,
    time_decay,
    time_first,
    key_weight,
    value_weight,
    recept_weight,
    output_weight,
    second_gain,
    second_bias,
    shift_key,
    shift_recept,
    up_weight,
    gate_weight,
    down_weight,
):
    grid = tuple(lax.axis_size(axis) for axis in ALL)
    count = grid[0] * grid[1] * grid[2] * grid[3]
    seq_count, piece_len, channels = tokens.shape
    hidden = up_weight.shape[1]
    mine = channels // count
    blocks = hidden // channels

    vectors = (
        first_gain,
        first_bias,
        mix_key,
        mix_value,
        mix_recept,
        time_decay,
        time_first,
        second_gain,
        second_bias,
        shift_key,
        shift_recept,
    )
    n_vec = len(vectors)
    packed = jnp.pad(jnp.stack(vectors), ((0, 16 - n_vec), (0, channels - mine)))
    pieces = (
        [key_weight, value_weight, recept_weight, packed],
        [output_weight] + [up_weight[:, j * channels : (j + 1) * channels] for j in range(blocks)],
        [gate_weight, down_weight],
    )
    places = (
        [(0, 0, 0), (0, 0, 1), (0, 0, 2), (1, 0, 0)],
        [(0, 0, 0)] + [(1, j * channels, 0) for j in range(blocks)],
        [(0, 0, 0), (1, 0, 0)],
    )
    chunks = [jnp.concatenate(piece) for piece in pieces]
    plans = []
    for piece, place in zip(pieces, places):
        first, entries, shapes = (0, [], {})
        for part, (out, column, lead) in zip(piece, place):
            entries.append((first, part.shape[0], out, column, lead))
            shapes[out] = (lead + 1, part.shape[0], column + channels)
            first += part.shape[0]
        plans.append((entries, [shapes[o] for o in sorted(shapes)]))
    stepwise = mine % 16 == 0

    def whole(at):
        gathered = lax.all_gather(chunks[at], ALL, axis=0)
        entries, shapes = plans[at]
        outs = []
        for out, (leads, _, columns) in enumerate(shapes):
            parts = [gathered[:, f : f + r] for f, r, o, _, _ in entries if o == out]
            if leads == 1:
                parts = [jnp.concatenate(parts, axis=-1)]
            outs.append(jnp.stack([p.reshape(-1, columns) for p in parts]))
        return outs

    if stepwise:
        half = channels // 2
        xy2 = beside_xy((chunks[2][:, :half], chunks[2][:, half:]), ("x", "y"))
        z0 = beside_z(chunks[0])
        z1 = beside_z(after(chunks[1], z0))
        z2 = [lax.all_gather(jnp.stack(part), "z", axis=1) for part in after(xy2, z0)]
        xy0 = beside_xy(after(z0, xy2), ("x", "y"))
        yx0 = beside_xy([jnp.stack(part) for part in xy0], ("y", "x"))
        xy1 = beside_xy(after(z1, yx0), ("x", "y"))
        first_mats, vecs = assemble(yx0, other_core(yx0), *plans[0], grid)
    else:
        first_mats, vecs = whole(0)
    vecs = vecs.reshape(count, 16, channels)[:, :n_vec, :mine]
    vecs = jnp.moveaxis(vecs, 1, 0).reshape(n_vec, channels).astype(jnp.float32)
    (
        norm_gain,
        norm_bias,
        key_mix,
        value_mix,
        recept_mix,
        decay_log,
        boost_log_scale,
        gain_two,
        bias_two,
        chan_key_mix,
        chan_recept_mix,
    ) = (vecs[j] for j in range(n_vec))
    seq_index = lax.axis_index(SEQ)
    positions = seq_index * piece_len + jnp.arange(piece_len, dtype=jnp.int32)
    live_mask = (positions[None, :] < lengths[:, None]).astype(jnp.float32)[:, :, None]
    field = tokens.astype(jnp.float32)
    normed_one, inverse_one = norm_stats(field)
    fading_rate_vector = jnp.exp(decay_log)
    place = jnp.arange(piece_len, dtype=jnp.float32)[:, None]
    piece_fall = jnp.exp(-piece_len * fading_rate_vector)
    rows = jnp.stack([norm_gain, norm_bias, key_mix, value_mix, recept_mix, fading_rate_vector])
    ins, kvr, local, gap_one = first_projections(
        (seq_index > 0).astype(jnp.int32)[None], tokens, shifted(tokens[:, -1, :], SEQ, 1), rows, first_mats
    )
    if stepwise:
        pair = [jnp.stack(part) for part in after(xy1, (ins, local))]
        local = after(local, pair)
        yx1 = beside_xy(pair, ("y", "x"))
        core1 = other_core([[part[0]] for part in yx1])
    key_in, value_in, recept_in = ins
    lookup_matrix_output, content_matrix_output, recept_proj = kvr
    local = (local[0], local[1])
    starting_accumulator, starting_normalizer = entering(piece_fall, local, False)
    if stepwise:
        starting_accumulator, starting_normalizer = after(
            (starting_accumulator, starting_normalizer), (yx1, core1, z2)
        )
    state_a, state_b, mixed_out = wkv_forward(
        kvr,
        starting_accumulator,
        starting_normalizer,
        boost_log_scale,
        fading_rate_vector,
    )
    if stepwise:
        yx2 = beside_xy(after(tuple(z2), yx1), ("y", "x"))
        rest1 = other_core([part[1:] for part in yx1])
        core1 = [one + rest for one, rest in zip(core1, rest1)]
        yx1 = after(yx1, (state_a, state_b))
        (output_mat,), (up_mat,) = assemble(yx1, core1, *plans[1], grid)
    else:
        (output_mat,), (up_mat,) = whole(1)
    branch = matmul("nlc,cd->nld", mixed_out, output_mat)
    residual = field + branch
    normed_two_raw, inverse_two = norm_stats(residual)
    normed_two = normed_two_raw * gain_two + bias_two
    if stepwise:
        normed_two = after(normed_two, yx2)
    before_two = previous_rows(normed_two)
    ffn_key = (normed_two * chan_key_mix + before_two * (1.0 - chan_key_mix)).astype(jnp.bfloat16)
    ffn_recept = (normed_two * chan_recept_mix + before_two * (1.0 - chan_recept_mix)).astype(
        jnp.bfloat16
    )
    flat_key = ffn_key.reshape(seq_count * piece_len, channels)
    relu_up = jax.nn.relu(jnp.dot(flat_key, up_mat, preferred_element_type=jnp.float32))
    squared, relu_up = (jnp.square(relu_up).astype(jnp.bfloat16), relu_up.astype(jnp.bfloat16))
    if stepwise:
        core2 = other_core([[part] for part in after(tuple(z2), (ffn_key, ffn_recept))])
        yx2 = after(yx2, (squared, relu_up, core2))
        rest2 = other_core([part[1:] for part in yx2])
        core2 = [one + rest for one, rest in zip(core2, rest2)]
        (gate_mat,), (down_mat,) = assemble(yx2, core2, *plans[2], grid)
    else:
        (gate_mat,), (down_mat,) = whole(2)
    squared = squared.reshape(seq_count, piece_len, hidden)
    down_proj = matmul("nlf,fd->nld", squared, down_mat)
    gate_value = jax.nn.sigmoid(matmul("nlc,cd->nld", ffn_recept, gate_mat))
    output = ((residual + gate_value * down_proj) * live_mask).astype(jnp.bfloat16)

    def outer(left, right):
        return jnp.einsum("nlc,nld->cd", left, right, preferred_element_type=jnp.float32)

    def to_core(left, right):
        send = outer(left, own_half(right, False)).astype(jnp.bfloat16)
        return send, spread(send, "core")[0]

    def both_cores(left, right, came):
        rows = outer(left, own_half(right)) + came.astype(jnp.float32)
        return rows.astype(jnp.bfloat16).reshape(*grid, -1, rows.shape[-1])

    seed = cotangent.astype(jnp.float32) * live_mask
    down_grad = (seed * gate_value).astype(jnp.bfloat16)
    gate_grad = (seed * down_proj * gate_value * (1.0 - gate_value)).astype(jnp.bfloat16)
    width = channels // 2
    down_send, down_came = to_core(squared, down_grad)
    gate_send, gate_came = to_core(ffn_recept, gate_grad)
    ffn_recept_grad = matmul("nld,cd->nlc", after(gate_grad, (down_send, gate_send)), gate_mat)
    late = (down_grad, gate_grad, down_came, gate_came)
    d_grad, g_grad, down_came, gate_came = after(late, ffn_recept_grad)
    way1 = Partial([both_cores(squared, d_grad, down_came), both_cores(ffn_recept, g_grad, gate_came)], True)
    flat = (seq_count * piece_len, -1)
    up_grad, ffn_key_grad = ffn_backward(
        after(down_grad, way1.sent).reshape(flat), relu_up, down_mat, up_mat
    )
    up_grad = up_grad.reshape(seq_count, piece_len, hidden)
    ffn_key_grad = ffn_key_grad.reshape(tokens.shape)
    up_send, up_came = to_core(ffn_key, up_grad)
    u_grad, up_came = after((up_grad, up_came), up_send)
    grad_up_part = both_cores(ffn_key, u_grad, up_came)
    normed_two_grad = (
        ffn_key_grad * chan_key_mix
        + ffn_recept_grad * chan_recept_mix
        + next_rows(ffn_key_grad * (1.0 - chan_key_mix) + ffn_recept_grad * (1.0 - chan_recept_mix))
    )
    gap_two = normed_two - before_two
    grad_chan_key = jnp.sum(ffn_key_grad * gap_two, axis=(0, 1))
    grad_chan_recept = jnp.sum(ffn_recept_grad * gap_two, axis=(0, 1))
    grad_gain_two = jnp.sum(normed_two_grad * normed_two_raw, axis=(0, 1))
    grad_bias_two = jnp.sum(normed_two_grad, axis=(0, 1))
    residual_grad = seed + norm_back(normed_two_grad * gain_two, normed_two_raw, inverse_two)
    branch_grad = residual_grad.astype(jnp.bfloat16)
    back1 = Partial(way1.finish(deps=(branch_grad,)), False)
    branch_grad = after(branch_grad, back1.sent)
    mixed_grad = matmul("nld,cd->nlc", branch_grad, output_mat)
    out_send, out_came = to_core(mixed_out, branch_grad)
    bonus = jnp.exp(boost_log_scale) * jnp.exp(lookup_matrix_output)
    over = 1.0 / (state_b + bonus)
    blended = (state_a + bonus * content_matrix_output) * over
    recept_sig = jax.nn.sigmoid(recept_proj)
    recept_grad = (mixed_grad * blended * recept_sig * (1.0 - recept_sig)).astype(jnp.bfloat16)
    alpha = mixed_grad * recept_sig * over * jnp.exp(-place * fading_rate_vector)
    local = (jnp.sum(alpha, axis=1), -jnp.sum(alpha * blended, axis=1))
    carry_p, carry_q = entering(piece_fall, local, True)
    z1 = over_z(stacked(back1.finish(), width))
    recept_send, recept_came = to_core(recept_in, recept_grad)
    g_out, g_recept, out_came, recept_came = after((branch_grad, recept_grad, out_came, recept_came), recept_send)
    part_out = both_cores(mixed_out, g_out, out_came)
    part_recept = both_cores(recept_in, g_recept, recept_came)
    way2 = Partial([grad_up_part, part_out, part_recept], True, deps=back1.came)
    carry_p, carry_q = after((carry_p, carry_q), way2.sent)
    key_grad, value_grad, grad_decay, boost_adjoint_term = wkv_backward(
        kvr,
        state_a,
        state_b,
        mixed_grad,
        carry_p,
        carry_q,
        boost_log_scale,
        fading_rate_vector,
    )
    key_send, key_came = to_core(key_in, key_grad)
    value_send, value_came = to_core(value_in, value_grad)
    late = (key_grad, value_grad, key_came, value_came)
    back2 = Partial(way2.finish(deps=(key_send, value_send)), False)
    k_grad, v_grad, key_came, value_came = after(late, back2.sent)
    part_key = both_cores(key_in, k_grad, key_came)
    part_value = both_cores(value_in, v_grad, value_came)
    way3 = Partial([part_key, part_value], True, deps=back2.came)
    z2 = over_z(stacked(back2.finish(deps=way3.sent), width))
    flat = (seq_count * piece_len, channels)
    grads = [g.reshape(flat) for g in after((k_grad, v_grad, recept_grad), (part_key, part_value))]
    mixes = jnp.stack([key_mix, value_mix, recept_mix])
    now_part, next_part, grad_mixes = input_gradients(grads, gap_one, mixes, first_mats)
    back3 = Partial(way3.finish(), False)
    now_part, next_part = after((now_part, next_part), way3.sent)
    normed_grad = now_part.reshape(tokens.shape) + next_rows(next_part.reshape(tokens.shape))
    grad_key_mix, grad_value_mix, grad_recept_mix = grad_mixes
    grad_gain_one = jnp.sum(normed_grad * normed_one, axis=(0, 1))
    grad_bias_one = jnp.sum(normed_grad, axis=(0, 1))
    tokens_grad = residual_grad + norm_back(normed_grad * norm_gain, normed_one, inverse_one)
    sums = jnp.concatenate(
        [
            grad_gain_one,
            grad_bias_one,
            grad_key_mix,
            grad_value_mix,
            grad_recept_mix,
            grad_decay,
            boost_adjoint_term,
            grad_gain_two,
            grad_bias_two,
            grad_chan_key,
            grad_chan_recept,
        ]
    )
    for axis in ("core", "x", "y", "z"):
        sums = sums + sum(spread(sums, axis))
    sums = lax.dynamic_slice_in_dim(sums.reshape(n_vec, channels), lax.axis_index(ALL) * mine, mine, 1)
    z3 = over_z_direct(stacked(back3.finish(), width))
    first, second, third = (to_owner(z) for z in (z1, z2, z3))

    def rows_of(pair, at, rows=mine, columns=1):
        cut = [h[at + j * rows : at + (j + 1) * rows] for h in pair for j in range(columns)]
        return jnp.concatenate(cut, axis=1).astype(jnp.float32)

    return (
        output,
        tokens_grad,
        *(sums[j] for j in range(7)),
        rows_of(third, 0),
        rows_of(third, mine),
        rows_of(second, (blocks + 1) * mine),
        rows_of(second, blocks * mine),
        *(sums[j] for j in range(7, n_vec)),
        rows_of(second, 0, columns=blocks),
        rows_of(first, hidden // count),
        rows_of(first, 0, hidden // count),
    )


def solution(mesh):
    seq, dp = (mesh.shape["seq"], mesh.shape["dp"])
    wide = len({device.coords[0] for device in mesh.devices.reshape(-1)})
    fine = jax.sharding.Mesh(mesh.devices.reshape(seq // 2, 2, dp // wide, wide), ALL)
    field, vector, matrix = (P(DP, SEQ, None), P(ALL), P(ALL, None))
    return jax.shard_map(
        per_device,
        mesh=fine,
        in_specs=(field, P(DP), field) + (vector,) * 7 + (matrix,) * 4 + (vector,) * 4 + (matrix,) * 3,
        out_specs=(field, field) + (vector,) * 7 + (matrix,) * 4 + (vector,) * 4 + (matrix,) * 3,
        check_vma=False,
    )
```

```python
import functools

import jax
import jax.numpy as jnp
from jax import lax
from jax.experimental import pallas as pl
from jax.experimental.pallas import tpu as pltpu
from jax.sharding import PartitionSpec as P

EPS = 1e-05

def norm_stats(field):
    center = field - jnp.mean(field, axis=-1, keepdims=True)
    inverse = lax.rsqrt(jnp.mean(center * center, axis=-1, keepdims=True) + EPS)
    return (center * inverse, inverse)


def norm_back(grad_normed, normalized, inverse):
    mean_grad = jnp.mean(grad_normed, axis=-1, keepdims=True)
    mean_proj = jnp.mean(grad_normed * normalized, axis=-1, keepdims=True)
    return inverse * (grad_normed - mean_grad - normalized * mean_proj)


SEQ = ("y", "core")
DP = ("z", "x")
ALL = ("y", "core", "z", "x")


def scan_tiles(rate, reverse):
    row = lax.broadcasted_iota(jnp.int32, (8, rate.shape[-1]), 0)
    steps = []
    for distance in (1, 2, 4):
        inside = row < 8 - distance if reverse else row >= distance
        steps.append((distance, jnp.where(inside, jnp.exp(-float(distance) * rate), 0.0)))
    return row, steps


def turn(x, distance, reverse):
    return pltpu.roll(x, 8 - distance if reverse else distance, 0)


def scan_rows(x, steps, reverse):
    for distance, factor in steps:
        x = x + factor * turn(x, distance, reverse)
    return x


def wkv_kernel(k_ref, v_ref, r_ref, a0_ref, b0_ref, u_ref, rate_ref, a_ref, b_ref, mixed_ref):
    seqs, span, lanes = k_ref.shape
    rate = rate_ref[...]
    boost = jnp.exp(u_ref[...])
    row, steps = scan_tiles(rate, False)
    falling = jnp.exp(-row.astype(jnp.float32) * rate)
    fall_all = jnp.exp(-8.0 * rate)
    first = row < 1
    pair = 16

    def body(i, carry):
        at = pl.ds(pl.multiple_of(i * pair, pair), pair)
        new = []
        for n in range(seqs):
            k16, v16, r16 = (ref[n, at, :] for ref in (k_ref, v_ref, r_ref))
            state = carry[2 * n : 2 * n + 2]
            tiles = []
            for g in range(2):
                k, v, r = (t[g * 8 : g * 8 + 8] for t in (k16, v16, r16))
                weight = jnp.exp(k)
                bonus = boost * weight
                sums = [scan_rows(t, steps, False) for t in (weight * v, weight)]
                a, b = (
                    falling * c + jnp.where(first, 0.0, turn(t, 1, False))
                    for c, t in zip(state, sums)
                )
                state = tuple(fall_all * c + t[7:8] for c, t in zip(state, sums))
                mixed = jax.nn.sigmoid(r) * ((a + bonus * v) / (b + bonus))
                tiles.append((a, b, mixed))
            a, b, mixed = (jnp.concatenate(t, axis=0) for t in zip(*tiles))
            a_ref[n, at, :] = a
            b_ref[n, at, :] = b
            mixed_ref[n, at, :] = mixed.astype(mixed_ref.dtype)
            new += state
        return tuple(new)

    start = []
    for n in range(seqs):
        start += [a0_ref[n : n + 1, :], b0_ref[n : n + 1, :]]
    lax.fori_loop(0, span // pair, body, tuple(start), unroll=2)


def wkv_back_kernel(
    k_ref, v_ref, r_ref, a_ref, b_ref, g_ref, p0_ref, q0_ref, u_ref, rate_ref,
    k_out, v_out, rate_out, first_out,
):
    seqs, span, lanes = k_ref.shape
    rate = rate_ref[...]
    boost = jnp.exp(u_ref[...])
    row, steps = scan_tiles(rate, True)
    falling = jnp.exp((row.astype(jnp.float32) - 7.0) * rate)
    fall_all = jnp.exp(-8.0 * rate)
    last = row > 6
    pair = 16
    count = span // pair

    def body(i, carry):
        at = pl.ds(pl.multiple_of((count - 1 - i) * pair, pair), pair)
        new = []
        rate_sum, first_sum = carry[-2:]
        for n in range(seqs):
            loaded = [ref[n, at, :] for ref in (k_ref, v_ref, r_ref, a_ref, b_ref, g_ref)]
            state = carry[2 * n : 2 * n + 2]
            tiles = []
            for g in (1, 0):
                k, v, r, a, b, grad = (t[g * 8 : g * 8 + 8] for t in loaded)
                weight = jnp.exp(k)
                bonus = boost * weight
                over = 1.0 / (b + bonus)
                wkv = (a + bonus * v) * over
                alpha = grad * jax.nn.sigmoid(r) * over
                sums = [scan_rows(t, steps, True) for t in (alpha, -alpha * wkv)]
                p, q = (
                    falling * c + jnp.where(last, 0.0, turn(t, 1, True))
                    for c, t in zip(state, sums)
                )
                state = tuple(fall_all * c + t[0:1] for c, t in zip(state, sums))
                share = alpha * bonus
                own = share * (v - wkv)
                tiles.append((own + weight * (p * v + q), share + weight * p))
                rate_sum = rate_sum + (a * p + b * q)
                first_sum = first_sum + own
            k_grad, v_grad = (jnp.concatenate(t, axis=0) for t in zip(*tiles[::-1]))
            k_out[n, at, :] = k_grad.astype(k_out.dtype)
            v_out[n, at, :] = v_grad.astype(v_out.dtype)
            new += state
        return tuple(new) + (rate_sum, first_sum)

    start = []
    for n in range(seqs):
        start += [p0_ref[n : n + 1, :], q0_ref[n : n + 1, :]]
    zero = jnp.zeros((8, lanes), jnp.float32)
    done = lax.fori_loop(0, count, body, tuple(start) + (zero, zero), unroll=2)
    rate_out[...] = -rate * jnp.exp(-rate) * jnp.sum(done[-2], axis=0, keepdims=True)
    first_out[...] = jnp.sum(done[-1], axis=0, keepdims=True)


def first_kernel(flag_ref, tok_ref, prev_ref, vec_ref, w_ref, x0_ref, x1_ref, x2_ref, y_ref, local_ref, gap_ref, normed, before, key):
    seqs, span, channels = tok_ref.shape
    j = pl.program_id(0)

    @pl.when(j == 0)
    def _():
        gain, bias = (vec_ref[0:1, :], vec_ref[1:2, :])
        for n in range(seqs):
            rows = pl.ds(n * span, span)
            field = norm_stats(tok_ref[n].astype(jnp.float32))[0] * gain + bias
            edge = norm_stats(prev_ref[n : n + 1, :].astype(jnp.float32))[0] * gain + bias
            edge = jnp.where(flag_ref[0] > 0, edge, 0.0)
            row = lax.broadcasted_iota(jnp.int32, field.shape, 0)
            normed[rows, :] = field
            earlier = jnp.where(row < 1, edge, pltpu.roll(field, 1, 0))
            before[rows, :] = earlier
            gap_ref[rows, :] = field - earlier

    mix = vec_ref[pl.ds(2 + j, 1), :]
    x = (normed[...] * mix + before[...] * (1.0 - mix)).astype(jnp.bfloat16)
    y = jnp.dot(x, w_ref[0], preferred_element_type=jnp.float32)
    y_ref[0] = y.reshape(seqs, span, channels)
    for k, ref in enumerate((x0_ref, x1_ref, x2_ref)):

        @pl.when(j == k)
        def _(ref=ref):
            ref[...] = x.reshape(seqs, span, channels)

    @pl.when(j == 0)
    def _():
        key[...] = y

    @pl.when(j == 1)
    def _():
        rate = vec_ref[5:6, :]
        place = lax.broadcasted_iota(jnp.int32, (span, channels), 0).astype(jnp.float32)
        fall = (place - (span - 1.0)) * rate
        for n in range(seqs):
            rows = slice(n * span, (n + 1) * span)
            weight = jnp.exp(key[rows, :] + fall)
            local_ref[0, n : n + 1, :] = jnp.sum(weight * y[rows], axis=0, keepdims=True)
            local_ref[1, n : n + 1, :] = jnp.sum(weight, axis=0, keepdims=True)


def first_projections(flag, tokens, prev, vectors, mats):
    seqs, span, channels = tokens.shape
    fixed = lambda *shape: pl.BlockSpec(shape, lambda j: (0,) * len(shape))
    rows = (seqs * span, channels)
    outs = pl.pallas_call(
        first_kernel,
        grid=(3,),
        out_shape=[jax.ShapeDtypeStruct(tokens.shape, jnp.bfloat16)] * 3
        + [jax.ShapeDtypeStruct((3, *tokens.shape), jnp.float32)]
        + [jax.ShapeDtypeStruct((2, seqs, channels), jnp.float32), jax.ShapeDtypeStruct(rows, jnp.float32)],
        in_specs=[
            pl.BlockSpec(memory_space=pltpu.SMEM),
            fixed(*tokens.shape),
            fixed(*prev.shape),
            fixed(*vectors.shape),
            pl.BlockSpec((1, channels, channels), lambda j: (j, 0, 0)),
        ],
        out_specs=[fixed(*tokens.shape)] * 3
        + [pl.BlockSpec((1, *tokens.shape), lambda j: (j, 0, 0, 0)), fixed(2, seqs, channels), fixed(*rows)],
        scratch_shapes=[pltpu.VMEM(rows, jnp.float32)] * 3,
        compiler_params=pltpu.CompilerParams(vmem_limit_bytes=48 << 20),
        cost_estimate=pl.CostEstimate(flops=1 << 20, bytes_accessed=1 << 16, transcendentals=0),
    )(flag, tokens, prev, vectors, mats)
    return outs[:3], outs[3], outs[4], outs[5]


def ffn_back_kernel(grad_ref, relu_ref, down_ref, up_ref, up_grad_ref, out_ref):
    wide = (((1,), (1,)), ((), ()))
    squared = lax.dot_general(grad_ref[...], down_ref[...], wide, preferred_element_type=jnp.float32)
    up_grad = (squared * (2.0 * relu_ref[...].astype(jnp.float32))).astype(jnp.bfloat16)
    up_grad_ref[...] = up_grad
    part = lax.dot_general(up_grad, up_ref[...], wide, preferred_element_type=jnp.float32)

    @pl.when(pl.program_id(0) == 0)
    def _():
        out_ref[...] = part

    @pl.when(pl.program_id(0) > 0)
    def _():
        out_ref[...] += part


def ffn_backward(grad, relu_up, down, up):
    rows, channels = grad.shape
    hidden = up.shape[1]
    block = 1024
    column = pl.BlockSpec((rows, block), lambda j: (0, j))
    return pl.pallas_call(
        ffn_back_kernel,
        grid=(hidden // block,),
        out_shape=[
            jax.ShapeDtypeStruct((rows, hidden), jnp.bfloat16),
            jax.ShapeDtypeStruct((rows, channels), jnp.float32),
        ],
        in_specs=[
            pl.BlockSpec((rows, channels), lambda j: (0, 0)),
            column,
            pl.BlockSpec((block, channels), lambda j: (j, 0)),
            pl.BlockSpec((channels, block), lambda j: (0, j)),
        ],
        out_specs=[column, pl.BlockSpec((rows, channels), lambda j: (0, 0))],
        compiler_params=pltpu.CompilerParams(vmem_limit_bytes=40 << 20),
        cost_estimate=pl.CostEstimate(
            flops=1 << 20, bytes_accessed=24 << 20, transcendentals=0
        ),
    )(grad, relu_up, down, up)


def in_grads_kernel(k_ref, v_ref, r_ref, gap_ref, mix_ref, w_ref, now_ref, next_ref, sum_ref):
    j = pl.program_id(0)
    grad = jnp.where(j == 0, k_ref[...], jnp.where(j == 1, v_ref[...], r_ref[...]))
    wide = (((1,), (1,)), ((), ()))
    part = lax.dot_general(grad, w_ref[0], wide, preferred_element_type=jnp.float32)
    mix = mix_ref[pl.ds(j, 1), :]
    now = part * mix
    sum_ref[pl.ds(j, 1), :] = jnp.sum(part * gap_ref[...], axis=0, keepdims=True)

    @pl.when(j == 0)
    def _():
        now_ref[...] = now
        next_ref[...] = part - now

    @pl.when(j > 0)
    def _():
        now_ref[...] += now
        next_ref[...] += part - now


def input_gradients(grads, gap, mixes, mats):
    rows, channels = gap.shape
    fixed = lambda *shape: pl.BlockSpec(shape, lambda j: (0,) * len(shape))
    return pl.pallas_call(
        in_grads_kernel,
        grid=(3,),
        out_shape=[jax.ShapeDtypeStruct(gap.shape, jnp.float32)] * 2
        + [jax.ShapeDtypeStruct((3, channels), jnp.float32)],
        in_specs=[fixed(rows, channels)] * 4
        + [fixed(3, channels), pl.BlockSpec((1, channels, channels), lambda j: (j, 0, 0))],
        out_specs=[fixed(rows, channels)] * 2 + [fixed(3, channels)],
        compiler_params=pltpu.CompilerParams(vmem_limit_bytes=40 << 20),
        cost_estimate=pl.CostEstimate(flops=1 << 20, bytes_accessed=8 << 20, transcendentals=0),
    )(*grads, gap, mixes, mats)


LANES = 256


def wkv_specs(seqs, span):
    field = pl.BlockSpec((seqs, span, LANES), lambda j: (0, 0, j))
    state = pl.BlockSpec((seqs, LANES), lambda j: (0, j))
    vector = pl.BlockSpec((1, LANES), lambda j: (0, j))
    return field, state, vector


def stacked_specs(seqs, span):
    shape = (None, seqs, span, LANES)
    return [pl.BlockSpec(shape, lambda j, n=n: (n, 0, 0, j)) for n in range(3)]


def wkv_forward(kvr, a0, b0, u, rate):
    shape = kvr.shape[1:]
    _, span, channels = shape
    seqs = shape[0]
    field, state, vector = wkv_specs(seqs, span)
    return pl.pallas_call(
        wkv_kernel,
        grid=(channels // LANES,),
        out_shape=[jax.ShapeDtypeStruct(shape, t) for t in (jnp.float32, jnp.float32, jnp.bfloat16)],
        in_specs=stacked_specs(seqs, span) + [state] * 2 + [vector] * 2,
        out_specs=[field] * 3,
        compiler_params=pltpu.CompilerParams(vmem_limit_bytes=32 << 20),
        cost_estimate=pl.CostEstimate(flops=1 << 20, bytes_accessed=1 << 16, transcendentals=0),
    )(kvr, kvr, kvr, a0, b0, u[None], rate[None])


def wkv_backward(kvr, a, b, grad, p0, q0, u, rate):
    seqs, span, channels = a.shape
    field, state, vector = wkv_specs(seqs, span)
    k_grad, v_grad, decay_grad, first_grad = pl.pallas_call(
        wkv_back_kernel,
        grid=(channels // LANES,),
        out_shape=[jax.ShapeDtypeStruct(a.shape, jnp.bfloat16)] * 2
        + [jax.ShapeDtypeStruct((1, channels), jnp.float32)] * 2,
        in_specs=stacked_specs(seqs, span) + [field] * 3 + [state] * 2 + [vector] * 2,
        out_specs=[field] * 2 + [vector] * 2,
        compiler_params=pltpu.CompilerParams(vmem_limit_bytes=32 << 20),
        cost_estimate=pl.CostEstimate(flops=1 << 20, bytes_accessed=1 << 16, transcendentals=0),
    )(kvr, kvr, kvr, a, b, grad, p0, q0, u[None], rate[None])
    return k_grad, v_grad, decay_grad[0], first_grad[0]


def matmul(form, left, right):
    return jnp.einsum(form, left, right, preferred_element_type=jnp.float32)


def shifted(block, axis, distance):
    count = lax.axis_size(axis)
    route = [(i - distance, i) for i in range(count) if 0 <= i - distance < count]
    return lax.ppermute(block, axis, route)


def previous_rows(field):
    came = shifted(field[:, -1, :], SEQ, 1)
    return jnp.concatenate([came[:, None, :], field[:, :-1, :]], axis=1)


def next_rows(field):
    came = shifted(field[:, 0, :], SEQ, -1)
    return jnp.concatenate([field[:, 1:, :], came[:, None, :]], axis=1)


def entering(factor, states, reverse):
    block = jnp.stack(states)
    low, high = in_order(block, spread(block, "core")[0])
    near, far = (high, low) if reverse else (low, high)
    chip = factor * near + far
    total, power = (jnp.zeros_like(block), jnp.ones_like(factor))
    for k in range(1, lax.axis_size("y")):
        total = total + power * shifted(chip, "y", -k if reverse else k)
        power = power * factor * factor
    core = lax.axis_index("core")
    total = jnp.where(core == (1 if reverse else 0), total, factor * total + near)
    return (total[0], total[1])


def in_order(own, other):
    core = lax.axis_index("core")
    return (jnp.where(core == 0, own, other), jnp.where(core == 0, other, own))


def own_half(x, own=True):
    half = x.shape[-1] // 2
    core = lax.axis_index("core")
    return jnp.where((core == 0) == own, x[..., :half], x[..., half:])


def after(x, deps):
    return lax.optimization_barrier((x, deps))[0] if jax.tree.leaves(deps) else x


def spread(block, axis):
    count = lax.axis_size(axis)
    return [
        lax.ppermute(block, axis, [(i, (i + k) % count) for i in range(count)])
        for k in range(1, count)
    ]


def cross(block, first, k):
    ys, cs, zs, xs = (lax.axis_size(axis) for axis in ALL)
    route = []
    for i in range(ys * cs * zs * xs):
        y, c, z, x = (i // (cs * zs * xs), i // (zs * xs) % cs, i // xs % zs, i % xs)
        if (c == 0) == first:
            x = (x + k) % xs
        else:
            y = (y + k) % ys
        route.append((i, ((y * cs + c) * zs + z) * xs + x))
    return lax.ppermute(block, ALL, route)


def beside_z(own):
    half = own.shape[1] // 2
    rows = lax.all_gather(own, "z", axis=0)
    return (rows[:, :, :half], rows[:, :, half:])


def beside_xy(pair, axes):
    return [[block] + spread(block, axis) for block, axis in zip(pair, axes)]


def other_core(parts):
    return [[spread(block, "core")[0] for block in part] for part in parts]


def assemble_kernel(entries, grid, at_ref, *refs):
    n_out = 1 + max(entry[2] for entry in entries)
    sources, outs, sems = (refs[: -n_out - 1], refs[-n_out - 1 : -1], refs[-1])
    ys, cs, zs, xs = grid
    y, c, x = (at_ref[j] for j in range(3))

    def back(at, k, count):
        return lax.rem(at - k + count, count)

    index = 0
    for dc in range(cs):
        for half, lead in enumerate((xs, ys)):
            for far in range(ys if half == 0 else xs):
                source = sources[index]
                index += 1

                def copy(k, _, source=source, dc=dc, half=half, far=far):
                    near, dz = (k // zs, lax.rem(k, zs))
                    dy, dx = (far, near) if half == 0 else (near, far)
                    block = back(y, dy, ys) * cs + back(c, dc, cs)
                    block = (block * zs + dz) * xs + back(x, dx, xs)
                    for first, rows, out, column, lead_at in entries:
                        width = source.shape[-1]
                        pltpu.make_async_copy(
                            source.at[near, dz, pl.ds(first, rows), :],
                            outs[out].at[lead_at, block, :, pl.ds(column + half * width, width)],
                            sems.at[out],
                        ).start()
                    return 0

                lax.fori_loop(0, lead * zs, copy, 0)
    for out in range(n_out):
        pltpu.make_async_copy(outs[out], outs[out], sems.at[out]).wait()


def assemble(mine, other, entries, shapes, grid):
    sources = [b for part in mine for b in part] + [b for part in other for b in part]
    at = jnp.stack([lax.axis_index(axis) for axis in ("y", "core", "x")]).astype(jnp.int32)
    count = grid[0] * grid[1] * grid[2] * grid[3]
    outs = pl.pallas_call(
        functools.partial(assemble_kernel, entries, grid),
        out_shape=[jax.ShapeDtypeStruct((n, count, *shape), jnp.bfloat16) for n, *shape in shapes],
        in_specs=[pl.BlockSpec(memory_space=pltpu.SMEM)]
        + [pl.BlockSpec(memory_space=pl.ANY)] * len(sources),
        out_specs=[pl.BlockSpec(memory_space=pltpu.VMEM)] * len(shapes),
        scratch_shapes=[pltpu.SemaphoreType.DMA((len(shapes),))],
        compiler_params=pltpu.CompilerParams(vmem_limit_bytes=40 << 20),
    )(at, *sources)
    return [out.reshape(out.shape[0], -1, out.shape[-1]) for out in outs]


class Partial:
    def __init__(self, parts, first, deps=()):
        self.parts, self.first = (parts, first)
        self.sent, self.came = ([], [])
        for k in range(1, lax.axis_size("x")):
            blocks = [after(self.take(p, k), deps) for p in parts]
            self.sent += blocks
            self.came.append([cross(block, first, k) for block in blocks])

    def take(self, p, k):
        count = lax.axis_size("x")
        x, y = (lax.rem(lax.axis_index(axis) + k, count) for axis in ("x", "y"))
        core = lax.axis_index("core")
        if self.first:
            by_x = lax.dynamic_index_in_dim(p, x, 3, keepdims=False).transpose(2, 1, 0, 3, 4)
            by_y = lax.dynamic_index_in_dim(p, y, 0, keepdims=False).transpose(1, 0, 2, 3, 4)
            return jnp.where(core == 0, by_x, by_y)
        return lax.dynamic_index_in_dim(p, jnp.where(core == 0, y, x), 2, keepdims=False)

    def finish(self, deps=()):
        totals = [self.take(p, 0).astype(jnp.float32) for p in self.parts]
        for blocks in after(self.came, deps):
            totals = [total + block.astype(jnp.float32) for total, block in zip(totals, blocks)]
        return [total.astype(jnp.bfloat16) for total in totals]


def stacked(parts, width):
    cut = [p[..., j : j + width] for p in parts for j in range(0, p.shape[-1], width)]
    return jnp.concatenate(cut, axis=2)


def over_z_direct(total):
    count, at = (lax.axis_size("z"), lax.axis_index("z"))
    block = lambda k: lax.dynamic_index_in_dim(total, lax.rem(at + k, count), 0, keepdims=False)
    out = block(0).astype(jnp.float32)
    for k in range(1, count):
        route = [(i, (i + k) % count) for i in range(count)]
        out = out + lax.ppermute(block(k), "z", route).astype(jnp.float32)
    return out.astype(jnp.bfloat16)


def over_z(total):
    zs, cores, rows, columns = total.shape
    flat = total.reshape(zs * cores * rows, columns)
    return lax.psum_scatter(flat, "z", scatter_dimension=0, tiled=True).reshape(cores, rows, columns)


def to_owner(total):
    core = lax.axis_index("core")
    came = spread(lax.dynamic_index_in_dim(total, 1 - core, 0, keepdims=False), "core")[0]
    return in_order(lax.dynamic_index_in_dim(total, core, 0, keepdims=False), came)


def per_device(
    tokens,
    lengths,
    cotangent,
    first_gain,
    first_bias,
    mix_key,
    mix_value,
    mix_recept,
    time_decay,
    time_first,
    key_weight,
    value_weight,
    recept_weight,
    output_weight,
    second_gain,
    second_bias,
    shift_key,
    shift_recept,
    up_weight,
    gate_weight,
    down_weight,
):
    grid = tuple(lax.axis_size(axis) for axis in ALL)
    count = grid[0] * grid[1] * grid[2] * grid[3]
    seq_count, piece_len, channels = tokens.shape
    hidden = up_weight.shape[1]
    mine = channels // count
    blocks = hidden // channels

    vectors = (
        first_gain,
        first_bias,
        mix_key,
        mix_value,
        mix_recept,
        time_decay,
        time_first,
        second_gain,
        second_bias,
        shift_key,
        shift_recept,
    )
    n_vec = len(vectors)
    packed = jnp.pad(jnp.stack(vectors), ((0, 16 - n_vec), (0, channels - mine)))
    pieces = (
        [key_weight, value_weight, recept_weight, packed],
        [output_weight] + [up_weight[:, j * channels : (j + 1) * channels] for j in range(blocks)],
        [gate_weight, down_weight],
    )
    places = (
        [(0, 0, 0), (0, 0, 1), (0, 0, 2), (1, 0, 0)],
        [(0, 0, 0)] + [(1, j * channels, 0) for j in range(blocks)],
        [(0, 0, 0), (1, 0, 0)],
    )
    chunks = [jnp.concatenate(piece) for piece in pieces]
    plans = []
    for piece, place in zip(pieces, places):
        first, entries, shapes = (0, [], {})
        for part, (out, column, lead) in zip(piece, place):
            entries.append((first, part.shape[0], out, column, lead))
            shapes[out] = (lead + 1, part.shape[0], column + channels)
            first += part.shape[0]
        plans.append((entries, [shapes[o] for o in sorted(shapes)]))
    stepwise = mine % 16 == 0

    def whole(at):
        gathered = lax.all_gather(chunks[at], ALL, axis=0)
        entries, shapes = plans[at]
        outs = []
        for out, (leads, _, columns) in enumerate(shapes):
            parts = [gathered[:, f : f + r] for f, r, o, _, _ in entries if o == out]
            if leads == 1:
                parts = [jnp.concatenate(parts, axis=-1)]
            outs.append(jnp.stack([p.reshape(-1, columns) for p in parts]))
        return outs

    if stepwise:
        half = channels // 2
        xy2 = beside_xy((chunks[2][:, :half], chunks[2][:, half:]), ("x", "y"))
        z0 = beside_z(chunks[0])
        z1 = beside_z(after(chunks[1], z0))
        z2 = [lax.all_gather(jnp.stack(part), "z", axis=1) for part in after(xy2, z0)]
        xy0 = beside_xy(after(z0, xy2), ("x", "y"))
        yx0 = beside_xy([jnp.stack(part) for part in xy0], ("y", "x"))
        xy1 = beside_xy(after(z1, yx0), ("x", "y"))
        first_mats, vecs = assemble(yx0, other_core(yx0), *plans[0], grid)
    else:
        first_mats, vecs = whole(0)
    vecs = vecs.reshape(count, 16, channels)[:, :n_vec, :mine]
    vecs = jnp.moveaxis(vecs, 1, 0).reshape(n_vec, channels).astype(jnp.float32)
    (
        norm_gain,
        norm_bias,
        key_mix,
        value_mix,
        recept_mix,
        decay_log,
        boost_log_scale,
        gain_two,
        bias_two,
        chan_key_mix,
        chan_recept_mix,
    ) = (vecs[j] for j in range(n_vec))
    seq_index = lax.axis_index(SEQ)
    positions = seq_index * piece_len + jnp.arange(piece_len, dtype=jnp.int32)
    live_mask = (positions[None, :] < lengths[:, None]).astype(jnp.float32)[:, :, None]
    field = tokens.astype(jnp.float32)
    normed_one, inverse_one = norm_stats(field)
    fading_rate_vector = jnp.exp(decay_log)
    place = jnp.arange(piece_len, dtype=jnp.float32)[:, None]
    piece_fall = jnp.exp(-piece_len * fading_rate_vector)
    rows = jnp.stack([norm_gain, norm_bias, key_mix, value_mix, recept_mix, fading_rate_vector])
    ins, kvr, local, gap_one = first_projections(
        (seq_index > 0).astype(jnp.int32)[None], tokens, shifted(tokens[:, -1, :], SEQ, 1), rows, first_mats
    )
    if stepwise:
        pair = [jnp.stack(part) for part in after(xy1, (ins, local))]
        local = after(local, pair)
        yx1 = beside_xy(pair, ("y", "x"))
        core1 = other_core([[part[0]] for part in yx1])
    key_in, value_in, recept_in = ins
    lookup_matrix_output, content_matrix_output, recept_proj = kvr
    local = (local[0], local[1])
    starting_accumulator, starting_normalizer = entering(piece_fall, local, False)
    if stepwise:
        starting_accumulator, starting_normalizer = after(
            (starting_accumulator, starting_normalizer), (yx1, core1, z2)
        )
    state_a, state_b, mixed_out = wkv_forward(
        kvr,
        starting_accumulator,
        starting_normalizer,
        boost_log_scale,
        fading_rate_vector,
    )
    if stepwise:
        yx2 = beside_xy(after(tuple(z2), yx1), ("y", "x"))
        rest1 = other_core([part[1:] for part in yx1])
        core1 = [one + rest for one, rest in zip(core1, rest1)]
        yx1 = after(yx1, (state_a, state_b))
        (output_mat,), (up_mat,) = assemble(yx1, core1, *plans[1], grid)
    else:
        (output_mat,), (up_mat,) = whole(1)
    branch = matmul("nlc,cd->nld", mixed_out, output_mat)
    residual = field + branch
    normed_two_raw, inverse_two = norm_stats(residual)
    normed_two = normed_two_raw * gain_two + bias_two
    if stepwise:
        normed_two = after(normed_two, yx2)
    before_two = previous_rows(normed_two)
    ffn_key = (normed_two * chan_key_mix + before_two * (1.0 - chan_key_mix)).astype(jnp.bfloat16)
    ffn_recept = (normed_two * chan_recept_mix + before_two * (1.0 - chan_recept_mix)).astype(
        jnp.bfloat16
    )
    flat_key = ffn_key.reshape(seq_count * piece_len, channels)
    relu_up = jax.nn.relu(jnp.dot(flat_key, up_mat, preferred_element_type=jnp.float32))
    squared, relu_up = (jnp.square(relu_up).astype(jnp.bfloat16), relu_up.astype(jnp.bfloat16))
    if stepwise:
        core2 = other_core([[part] for part in after(tuple(z2), (ffn_key, ffn_recept))])
        yx2 = after(yx2, (ffn_key, ffn_recept))
        rest2 = other_core([part[1:] for part in yx2])
        core2 = [one + rest for one, rest in zip(core2, rest2)]
        (gate_mat,), (down_mat,) = assemble(yx2, core2, *plans[2], grid)
    else:
        (gate_mat,), (down_mat,) = whole(2)
    squared = squared.reshape(seq_count, piece_len, hidden)
    down_proj = matmul("nlf,fd->nld", squared, down_mat)
    gate_value = jax.nn.sigmoid(matmul("nlc,cd->nld", ffn_recept, gate_mat))
    output = ((residual + gate_value * down_proj) * live_mask).astype(jnp.bfloat16)

    def outer(left, right):
        return jnp.einsum("nlc,nld->cd", left, right, preferred_element_type=jnp.float32)

    def to_core(left, right):
        send = outer(left, own_half(right, False)).astype(jnp.bfloat16)
        return send, spread(send, "core")[0]

    def both_cores(left, right, came):
        rows = outer(left, own_half(right)) + came.astype(jnp.float32)
        return rows.astype(jnp.bfloat16).reshape(*grid, -1, rows.shape[-1])

    seed = cotangent.astype(jnp.float32) * live_mask
    down_grad = (seed * gate_value).astype(jnp.bfloat16)
    gate_grad = (seed * down_proj * gate_value * (1.0 - gate_value)).astype(jnp.bfloat16)
    width = channels // 2
    down_send, down_came = to_core(squared, down_grad)
    gate_send, gate_came = to_core(ffn_recept, gate_grad)
    ffn_recept_grad = matmul("nld,cd->nlc", after(gate_grad, (down_send, gate_send)), gate_mat)
    late = (down_grad, gate_grad, down_came, gate_came)
    d_grad, g_grad, down_came, gate_came = after(late, ffn_recept_grad)
    way1 = Partial([both_cores(squared, d_grad, down_came), both_cores(ffn_recept, g_grad, gate_came)], True)
    flat = (seq_count * piece_len, -1)
    up_grad, ffn_key_grad = ffn_backward(
        after(down_grad, way1.sent).reshape(flat), relu_up, down_mat, up_mat
    )
    up_grad = up_grad.reshape(seq_count, piece_len, hidden)
    ffn_key_grad = ffn_key_grad.reshape(tokens.shape)
    up_send, up_came = to_core(ffn_key, up_grad)
    u_grad, up_came = after((up_grad, up_came), up_send)
    grad_up_part = both_cores(ffn_key, u_grad, up_came)
    normed_two_grad = (
        ffn_key_grad * chan_key_mix
        + ffn_recept_grad * chan_recept_mix
        + next_rows(ffn_key_grad * (1.0 - chan_key_mix) + ffn_recept_grad * (1.0 - chan_recept_mix))
    )
    gap_two = normed_two - before_two
    grad_chan_key = jnp.sum(ffn_key_grad * gap_two, axis=(0, 1))
    grad_chan_recept = jnp.sum(ffn_recept_grad * gap_two, axis=(0, 1))
    grad_gain_two = jnp.sum(normed_two_grad * normed_two_raw, axis=(0, 1))
    grad_bias_two = jnp.sum(normed_two_grad, axis=(0, 1))
    residual_grad = seed + norm_back(normed_two_grad * gain_two, normed_two_raw, inverse_two)
    branch_grad = residual_grad.astype(jnp.bfloat16)
    back1 = Partial(way1.finish(deps=(branch_grad,)), False)
    branch_grad = after(branch_grad, back1.sent)
    mixed_grad = matmul("nld,cd->nlc", branch_grad, output_mat)
    out_send, out_came = to_core(mixed_out, branch_grad)
    bonus = jnp.exp(boost_log_scale) * jnp.exp(lookup_matrix_output)
    over = 1.0 / (state_b + bonus)
    blended = (state_a + bonus * content_matrix_output) * over
    recept_sig = jax.nn.sigmoid(recept_proj)
    recept_grad = (mixed_grad * blended * recept_sig * (1.0 - recept_sig)).astype(jnp.bfloat16)
    alpha = mixed_grad * recept_sig * over * jnp.exp(-place * fading_rate_vector)
    local = (jnp.sum(alpha, axis=1), -jnp.sum(alpha * blended, axis=1))
    carry_p, carry_q = entering(piece_fall, local, True)
    z1 = over_z(stacked(back1.finish(), width))
    recept_send, recept_came = to_core(recept_in, recept_grad)
    g_out, g_recept, out_came, recept_came = after((branch_grad, recept_grad, out_came, recept_came), recept_send)
    part_out = both_cores(mixed_out, g_out, out_came)
    part_recept = both_cores(recept_in, g_recept, recept_came)
    way2 = Partial([grad_up_part, part_out, part_recept], True, deps=back1.came)
    carry_p, carry_q = after((carry_p, carry_q), way2.sent)
    key_grad, value_grad, grad_decay, boost_adjoint_term = wkv_backward(
        kvr,
        state_a,
        state_b,
        mixed_grad,
        carry_p,
        carry_q,
        boost_log_scale,
        fading_rate_vector,
    )
    key_send, key_came = to_core(key_in, key_grad)
    value_send, value_came = to_core(value_in, value_grad)
    late = (key_grad, value_grad, key_came, value_came)
    back2 = Partial(way2.finish(deps=(key_send, value_send)), False)
    k_grad, v_grad, key_came, value_came = after(late, back2.sent)
    part_key = both_cores(key_in, k_grad, key_came)
    part_value = both_cores(value_in, v_grad, value_came)
    way3 = Partial([part_key, part_value], True, deps=back2.came)
    z2 = over_z(stacked(back2.finish(deps=way3.sent), width))
    flat = (seq_count * piece_len, channels)
    grads = [g.reshape(flat) for g in after((k_grad, v_grad, recept_grad), (part_key, part_value))]
    mixes = jnp.stack([key_mix, value_mix, recept_mix])
    now_part, next_part, grad_mixes = input_gradients(grads, gap_one, mixes, first_mats)
    back3 = Partial(way3.finish(), False)
    now_part, next_part = after((now_part, next_part), way3.sent)
    normed_grad = now_part.reshape(tokens.shape) + next_rows(next_part.reshape(tokens.shape))
    grad_key_mix, grad_value_mix, grad_recept_mix = grad_mixes
    grad_gain_one = jnp.sum(normed_grad * normed_one, axis=(0, 1))
    grad_bias_one = jnp.sum(normed_grad, axis=(0, 1))
    tokens_grad = residual_grad + norm_back(normed_grad * norm_gain, normed_one, inverse_one)
    sums = jnp.concatenate(
        [
            grad_gain_one,
            grad_bias_one,
            grad_key_mix,
            grad_value_mix,
            grad_recept_mix,
            grad_decay,
            boost_adjoint_term,
            grad_gain_two,
            grad_bias_two,
            grad_chan_key,
            grad_chan_recept,
        ]
    )
    for axis in ("core", "x", "y", "z"):
        sums = sums + sum(spread(sums, axis))
    sums = lax.dynamic_slice_in_dim(sums.reshape(n_vec, channels), lax.axis_index(ALL) * mine, mine, 1)
    z3 = over_z_direct(stacked(back3.finish(), width))
    first, second, third = (to_owner(z) for z in (z1, z2, z3))

    def rows_of(pair, at, rows=mine, columns=1):
        cut = [h[at + j * rows : at + (j + 1) * rows] for h in pair for j in range(columns)]
        return jnp.concatenate(cut, axis=1).astype(jnp.float32)

    return (
        output,
        tokens_grad,
        *(sums[j] for j in range(7)),
        rows_of(third, 0),
        rows_of(third, mine),
        rows_of(second, (blocks + 1) * mine),
        rows_of(second, blocks * mine),
        *(sums[j] for j in range(7, n_vec)),
        rows_of(second, 0, columns=blocks),
        rows_of(first, hidden // count),
        rows_of(first, 0, hidden // count),
    )


def solution(mesh):
    seq, dp = (mesh.shape["seq"], mesh.shape["dp"])
    wide = len({device.coords[0] for device in mesh.devices.reshape(-1)})
    fine = jax.sharding.Mesh(mesh.devices.reshape(seq // 2, 2, dp // wide, wide), ALL)
    field, vector, matrix = (P(DP, SEQ, None), P(ALL), P(ALL, None))
    return jax.shard_map(
        per_device,
        mesh=fine,
        in_specs=(field, P(DP), field) + (vector,) * 7 + (matrix,) * 4 + (vector,) * 4 + (matrix,) * 3,
        out_specs=(field, field) + (vector,) * 7 + (matrix,) * 4 + (vector,) * 4 + (matrix,) * 3,
        check_vma=False,
    )
```
